32 devices in a mesh: ctx: 8 (over z, y), head: 4 (over x, core).
Axes of the slice: x: 2, y: 2, z: 4, core: 2. Of those that a mesh axis runs over, the one named last changes fastest.
Arguments:
- hidden: bfloat16 [2, 2048, 2048], P(None, 'ctx'), may hold values from -6 to 6
- positions: int32 [2, 2048], replicated, may hold values from 0 to 2047, as said below
- norm_attention: bfloat16 [2048], P('ctx'), may hold values from 0.099609375 to 1.8984375
- w_query: bfloat16 [2048, 2048], P('ctx', 'head'), may hold values from -0.125 to 0.125
- w_key: bfloat16 [2048, 512], P('ctx', 'head'), may hold values from -0.125 to 0.125
- w_value: bfloat16 [2048, 512], P('ctx', 'head'), may hold values from -0.125 to 0.125
- w_out: bfloat16 [2048, 2048], P('head', 'ctx'), may hold values from -2 to 2
- norm_feed: bfloat16 [2048], P('ctx'), may hold values from 0.099609375 to 1.8984375
- w_gate: bfloat16 [2048, 8192], P('ctx', 'head'), may hold values from -0.125 to 0.125
- w_up: bfloat16 [2048, 8192], P('ctx', 'head'), may hold values from -0.125 to 0.125
- w_down: bfloat16 [8192, 2048], P('head', 'ctx'), may hold values from -0.0625 to 0.0625
- cotangent: bfloat16 [2, 2048, 2048], P(None, 'ctx'), may hold values from -6 to 6
Outputs:
- output: bfloat16 [2, 2048, 2048], P(None, 'ctx')
- grad_input: float32 [2, 2048, 2048], P(None, 'ctx')
- grad_norm_attention: float32 [2048], P('ctx')
- grad_query: float32 [2048, 2048], P('ctx', 'head')
- grad_key: float32 [2048, 512], P('ctx', 'head')
- grad_value: float32 [2048, 512], P('ctx', 'head')
- grad_out: float32 [2048, 2048], P('head', 'ctx')
- grad_norm_feed: float32 [2048], P('ctx')
- grad_gate: float32 [2048, 8192], P('ctx', 'head')
- grad_up: float32 [2048, 8192], P('ctx', 'head')
- grad_down: float32 [8192, 2048], P('head', 'ctx')
The draws below stay inside these ranges and needn't reach their ends.
Inputs may be any that keep to these rules, and one draw needn't show every extreme that they name: In each sequence the positions are a permutation of 0 to 2047; every aligned run of 128 stored rows holds consecutive positions in increasing order.
All inputs are finite; a program needn't handle non-finite values.
Results may differ from the reference program's by a relative error of at most 0.025.
Values may be sent and summed in bfloat16 or wider, within the bound.
No kernel may reach another device: no remote copies, remote signals or barrier semaphores. Data moves between devices by JAX's collectives and lax.ppermute only.
A program may use at most 192 MiB of HBM per device.

```python
import math
import jax
import jax.numpy as jnp
from jax import lax

D = 2048
HQ = 32
HK = 8
HD = 64
FF = 8192
SEQS = 2
HALF = 128
SEQ_LEN = 2048
BLOCKS = 16


def draw_positions(key, part):
    key = jax.random.fold_in(key, 11)
    seq_keys = jax.random.split(key, SEQS)
    orders = jax.vmap(lambda one_key: jax.random.permutation(one_key, BLOCKS))(seq_keys)
    slot_index = jnp.arange(SEQ_LEN, dtype=jnp.int32) // HALF
    offset = jnp.arange(SEQ_LEN, dtype=jnp.int32) % HALF
    return (orders[:, slot_index] * HALF + offset[None, :]).astype(jnp.int32)


def levels(key, dims, cuts, least, top_value):
    def one(axis_at, shards_of):
        heights = jax.random.uniform(jax.random.fold_in(jax.random.fold_in(key, 6), axis_at), (shards_of,), jnp.float32, least / len(cuts), top_value / len(cuts))
        return jnp.repeat(jnp.exp(heights), dims[axis_at] // shards_of).reshape((-1,) + (1,) * (len(dims) - axis_at - 1))

    gain = one(*cuts[0])
    for cut in cuts[1:]:
        gain = gain * one(*cut)
    return gain


def bell_draw(rng, shape, scale, limit, cuts=(), kind=jnp.bfloat16):
    gain = levels(rng, shape, cuts, -0.22, 0.18) if cuts else 1.0
    values = jax.random.normal(rng, shape, jnp.float32) * scale * gain
    return jnp.minimum(jnp.maximum(values, -limit), limit).astype(kind)


def setup_inputs(seed: int = 0) -> dict:
    key_list = jax.random.split(jax.random.key(seed), 13)
    hidden = bell_draw(key_list[0], (SEQS, SEQ_LEN, D), 1.0, 6.0, ((1, 8),))
    positions = draw_positions(jax.random.fold_in(key_list[12], 71), 0)
    norm_attention = jnp.clip(1.0 + 0.18 * jax.random.normal(key_list[2], (D,), jnp.float32), 0.099609375, 1.8984375).astype(jnp.bfloat16)
    w_query = bell_draw(key_list[3], (D, HQ * HD), D ** -0.5, 0.125, ((0, 8), (1, 4)))
    w_key = bell_draw(key_list[4], (D, HK * HD), D ** -0.5, 0.125, ((0, 8), (1, 4)))
    w_value = bell_draw(key_list[5], (D, HK * HD), D ** -0.5, 0.125, ((0, 8), (1, 4)))
    w_out = bell_draw(key_list[6], (HQ * HD, D), (max(1, HQ * HD * 8 // SEQ_LEN)) ** -0.5, 2.0, ((0, 4), (1, 8)))
    norm_feed = jnp.clip(1.0 + 0.18 * jax.random.normal(key_list[7], (D,), jnp.float32), 0.099609375, 1.8984375).astype(jnp.bfloat16)
    w_gate = bell_draw(key_list[8], (D, FF), D ** -0.5, 0.125, ((0, 8), (1, 4)))
    w_up = bell_draw(key_list[9], (D, FF), D ** -0.5, 0.125, ((0, 8), (1, 4)))
    w_down = bell_draw(key_list[10], (FF, D), FF ** -0.5, 0.0625, ((0, 4), (1, 8)))
    cotangent = bell_draw(key_list[11], (SEQS, SEQ_LEN, D), 1.0, 6.0, ((1, 8),))
    return dict(hidden=hidden, positions=positions, norm_attention=norm_attention, w_query=w_query, w_key=w_key, w_value=w_value, w_out=w_out, norm_feed=norm_feed, w_gate=w_gate, w_up=w_up, w_down=w_down, cotangent=cotangent)


EPSILON = 1e-05
ROPE_BASE = 500000.0
HIGHEST = lax.Precision.HIGHEST
NEGATIVE = -1e+30

@jax.custom_vjp
def low(v):
    return lax.optimization_barrier(v.astype(jnp.bfloat16)).astype(jnp.float32)

@jax.custom_vjp
def low_back(v):
    return v

def low_keep(v):
    return (low(v), None)

def low_pass(kept, grad):
    return (grad,)

def back_keep(v):
    return (v, None)

def back_low(kept, grad):
    return (low(grad),)
low.defvjp(low_keep, low_pass)
low_back.defvjp(back_keep, back_low)

def rotation(place_rows, head_dim):
    half_dim = head_dim // 2
    frequency = jnp.exp(jnp.arange(half_dim, dtype=jnp.float32) * (-2.0 * math.log(ROPE_BASE) / head_dim))
    angles = place_rows.astype(jnp.float32)[..., None] * frequency
    return (jnp.cos(angles), jnp.sin(angles))

def rotate(values, cos_part, sin_part):
    half_dim = values.shape[-1] // 2
    first_half = values[..., :half_dim]
    second_half = values[..., half_dim:]
    return jnp.concatenate([first_half * cos_part - second_half * sin_part, second_half * cos_part + first_half * sin_part], axis=-1)

def rms_norm(values, gain_vec):
    return values * lax.rsqrt(lax.optimization_barrier(jnp.mean(values * values, axis=-1, keepdims=True)) + EPSILON) * gain_vec

def matmul(left_side, right_side):
    return jnp.dot(left_side, right_side, precision=HIGHEST, preferred_element_type=jnp.float32)

def layer_one(tokens, position, weights):
    norm_attention, w_query, w_key, w_value, w_out, norm_feed, w_gate, w_up, w_down = weights
    length = tokens.shape[0]
    group_size = HQ // HK
    score_scale = HD ** (-0.5)
    normed = low(rms_norm(tokens, norm_attention))
    cos_part, sin_part = rotation(position, HD)
    cos_heads = cos_part[:, None, :]
    sin_heads = sin_part[:, None, :]
    queries = low_back(matmul(normed, w_query)).reshape(length, HQ, HD)
    queries = low(rotate(queries, cos_heads, sin_heads)).reshape(length, HK, group_size, HD)
    key_rows = low_back(matmul(normed, w_key)).reshape(length, HK, HD)
    key_rows = low(rotate(key_rows, cos_heads, sin_heads))
    value_rows = low(low_back(matmul(normed, w_value))).reshape(length, HK, HD)
    block_rows = math.gcd(length, 256)

    def attend_block(block_args):
        query_block, place_block = block_args
        scores = jnp.einsum('bkgd,lkd->kgbl', query_block, key_rows, precision=HIGHEST) * score_scale
        scores = low_back(scores)
        allowed = position[None, None, None, :] <= place_block[None, None, :, None]
        masked = jnp.where(allowed, scores, NEGATIVE)
        row_peak = lax.optimization_barrier(jnp.max(masked, axis=-1, keepdims=True))
        shifted = jnp.where(allowed, jnp.exp(masked - row_peak), 0.0)
        softmax_out = low(shifted / lax.optimization_barrier(jnp.sum(shifted, axis=-1, keepdims=True)))
        return jnp.einsum('kgbl,lkd->bkgd', softmax_out, value_rows, precision=HIGHEST)
    attended = lax.map(jax.checkpoint(attend_block), (queries.reshape(length // block_rows, block_rows, HK, group_size, HD), position.reshape(length // block_rows, block_rows)))
    attended = low(low_back(attended.reshape(length, HQ * HD)))
    mid_stream = tokens + low_back(matmul(attended, w_out))
    normed_two = low(rms_norm(mid_stream, norm_feed))
    gate_pre = low_back(matmul(normed_two, w_gate))
    up_pre = low_back(matmul(normed_two, w_up))
    activated = low(gate_pre * jax.nn.sigmoid(gate_pre) * up_pre)
    return mid_stream + low_back(matmul(activated, w_down))

def forward(tokens, position, weights):

    def seq_step(carry_in, inputs):
        return (carry_in, layer_one(inputs[0], inputs[1], weights))
    unused, outputs = lax.scan(seq_step, jnp.zeros((), jnp.float32), (tokens, position))
    return outputs

def reference(hidden, positions, norm_attention, w_query, w_key, w_value, w_out, norm_feed, w_gate, w_up, w_down, cotangent):
    weights = tuple((weight.astype(jnp.float32) for weight in (norm_attention, w_query, w_key, w_value, w_out, norm_feed, w_gate, w_up, w_down)))

    def forward_all(tokens_in, *weight_list):
        return forward(tokens_in, positions, weight_list)
    output, pullback = jax.vjp(forward_all, hidden.astype(jnp.float32), *weights)
    gradients = pullback(cotangent.astype(jnp.float32))
    return (output.astype(jnp.bfloat16), gradients[0], gradients[1], gradients[2], gradients[3], gradients[4], gradients[5], gradients[6], gradients[7], gradients[8], gradients[9])
```

```python
import functools
import math

import jax
import jax.numpy as jnp
from jax import lax
from jax.experimental import pallas as pl
from jax.experimental.pallas import tpu as pltpu
from jax.sharding import PartitionSpec as P

HQ = 32
HK = 8
HD = 64
GROUP = HQ // HK
RUN = 128

EPSILON = 1e-05
ROPE_BASE = 500000.0
NEGATIVE = -1e30
LOG2E = math.log2(math.e)
SCALE = HD ** (-0.5)
BF = jnp.bfloat16
F32 = jnp.float32

NN = (((1,), (0,)), ((), ()))
NT = (((1,), (1,)), ((), ()))
TN = (((0,), (0,)), ((), ()))


def mm(a, b, dims=NN):
    return lax.dot_general(a, b, dims, preferred_element_type=F32)


def ring_order(n):
    return list(range(0, n, 2)) + list(range(1, n, 2))[::-1]


def ring_pairs(n, step):
    order = ring_order(n)
    return [(order[p], order[(p + step) % n]) for p in range(n)]


def ring_gather(right, left, n):
    rights, lefts = [right], [left]
    for unused in range(n - 1):
        right = lax.ppermute(right, "ctx", ring_pairs(n, 1))
        left = lax.ppermute(left, "ctx", ring_pairs(n, -1))
        rights.append(right)
        lefts.append(left)
    return rights, lefts


def ring_scatter(rights, lefts, n):
    right, left = rights[1 % n], lefts[1 % n]
    for s in list(range(2, n)) + [0]:
        right = lax.ppermute(right, "ctx", ring_pairs(n, 1))
        left = lax.ppermute(left, "ctx", ring_pairs(n, -1))
        right = (right.astype(F32) + rights[s].astype(F32)).astype(BF)
        left = (left.astype(F32) + lefts[s].astype(F32)).astype(BF)
    return right, left


def other_core(value):
    return lax.ppermute(value, "head", [(h, h ^ 1) for h in range(4)])


def other_x(value):
    return lax.ppermute(value, "head", [(h, h ^ 2) for h in range(4)])


def head_scatter(partial, seq, core):
    half = partial.shape[1] // 2
    mine = lax.dynamic_slice_in_dim(partial, core * half, half, 1)
    theirs = lax.dynamic_slice_in_dim(partial, (1 - core) * half, half, 1)
    summed = mine.astype(F32) + other_core(theirs).astype(F32)
    keep = lax.dynamic_slice_in_dim(summed, seq, 1, 0)[0]
    send = lax.dynamic_slice_in_dim(summed, 1 - seq, 1, 0)[0].astype(BF)
    return keep + other_x(send).astype(F32)


def head_gather(own, seq, core):
    far = other_x(own)
    pair = jnp.where(seq == 0, jnp.stack([own, far]), jnp.stack([far, own]))
    near = other_core(pair)
    return jnp.where(
        core == 0, jnp.concatenate([pair, near], 1), jnp.concatenate([near, pair], 1)
    )


def swap_halves(v):
    lane = lax.broadcasted_iota(jnp.int32, v.shape, 1) % HD
    return jnp.where(lane < HD // 2, pltpu.roll(v, 2 * HD - HD // 2, 1), pltpu.roll(v, HD // 2, 1))


def qkv_kernel(x_ref, w_ref, cos_ref, sin_ref, n_ref, q_ref, kv_ref):
    x = x_ref[0].astype(F32)
    inverse = lax.rsqrt(jnp.mean(x * x, axis=-1, keepdims=True) + EPSILON)
    unit = (x * inverse).astype(BF)
    n_ref[0] = unit
    y = mm(unit, w_ref[...])
    cos, sin = cos_ref[0], sin_ref[0]
    q_width, k_width = q_ref.shape[2], kv_ref.shape[2] // 2
    for j in range(0, q_width, 2 * HD):
        v = y[:, j : j + 2 * HD]
        q_ref[0, :, j : j + 2 * HD] = (v * cos + swap_halves(v) * sin).astype(BF)
    for j in range(0, k_width, 2 * HD):
        v = y[:, q_width + j : q_width + j + 2 * HD]
        kv_ref[0, :, j : j + 2 * HD] = (v * cos + swap_halves(v) * sin).astype(BF)
    kv_ref[0, :, k_width:] = y[:, q_width + k_width :].astype(BF)


def qkv_call(hidden, weight, cos, sin, q_width, kv_width):
    sequences, rows, width = hidden.shape
    block = RUN
    grid = (sequences, rows // block)
    spec = lambda w: pl.BlockSpec((1, block, w), lambda s, r: (s, r, 0))
    return pl.pallas_call(
        qkv_kernel,
        grid=grid,
        in_specs=[
            spec(width),
            pl.BlockSpec(weight.shape, lambda s, r: (0, 0)),
            spec(2 * HD),
            spec(2 * HD),
        ],
        out_specs=[spec(width), spec(q_width), spec(kv_width)],
        out_shape=[
            jax.ShapeDtypeStruct((sequences, rows, width), BF),
            jax.ShapeDtypeStruct((sequences, rows, q_width), BF),
            jax.ShapeDtypeStruct((sequences, rows, kv_width), BF),
        ],
        compiler_params=pltpu.CompilerParams(vmem_limit_bytes=40 * 1024 * 1024),
        cost_estimate=pl.CostEstimate(
            flops=2 * sequences * rows * width * weight.shape[1],
            bytes_accessed=weight.size * 2 + hidden.size * 4,
            transcendentals=0,
        ),
        name="norm_qkv",
    )(hidden, weight, cos, sin)


def half_mask(v, which):
    lane = lax.broadcasted_iota(jnp.int32, v.shape, 1)
    keep = (lane < HD) if which == 0 else (lane >= HD)
    return jnp.where(keep, v, jnp.zeros_like(v))


def stack_heads(block):
    return jnp.concatenate(
        [block[:, g * 2 * HD : (g + 1) * 2 * HD] for g in range(GROUP)], axis=0
    )


def causal_mask(shape):
    key = lax.broadcasted_iota(jnp.int32, shape, 0)
    query = lax.broadcasted_iota(jnp.int32, shape, 1) % RUN
    return key <= query


def attend_kernel(sq_ref, sk_ref, q_ref, kv_ref, o_ref, lse_ref, s_ref, m_ref, l_ref, acc_ref):
    seq, run = pl.program_id(0), pl.program_id(1)
    start = sq_ref[seq, run]
    runs = kv_ref.shape[1]
    columns = GROUP * RUN
    queries = stack_heads(q_ref[0])
    q_pair = [half_mask(queries, k) for k in range(2)]
    m_ref[...] = jnp.full_like(m_ref, NEGATIVE)
    l_ref[...] = jnp.zeros_like(l_ref)
    acc_ref[...] = jnp.zeros_like(acc_ref)

    def score_step(i, carry):
        key_start = sk_ref[seq, i]

        def scores(masked):
            keys = kv_ref[0, i, :, : 2 * HD]
            for k in range(2):
                s = mm(keys, q_pair[k], NT) * (SCALE * LOG2E)
                if masked:
                    s = jnp.where(causal_mask(s.shape), s, NEGATIVE)
                s_ref[k, pl.ds(pl.multiple_of(i * RUN, RUN), RUN), :] = s
                m_ref[k] = jnp.maximum(m_ref[k], jnp.max(s.reshape(-1, 8, columns), axis=0))

        @pl.when(key_start < start)
        def _():
            scores(False)

        @pl.when(key_start == start)
        def _():
            scores(True)

        return carry

    lax.fori_loop(0, runs, score_step, 0)
    peaks = [jnp.max(m_ref[k], axis=0, keepdims=True) for k in range(2)]

    def value_step(i, carry):
        @pl.when(sk_ref[seq, i] <= start)
        def _():
            values = kv_ref[0, i, :, 2 * HD :]
            for k in range(2):
                p = jnp.exp2(s_ref[k, pl.ds(pl.multiple_of(i * RUN, RUN), RUN), :] - peaks[k])
                l_ref[k] += jnp.sum(p.reshape(-1, 8, columns), axis=0)
                acc_ref[k] += mm(values, p.astype(BF), TN)

        return carry

    lax.fori_loop(0, runs, value_step, 0)
    rows = []
    for k in range(2):
        total = jnp.sum(l_ref[k], axis=0, keepdims=True)
        lse_ref[0, 0, k : k + 1, :] = peaks[k] + jnp.log2(total)
        rows.append(acc_ref[k, k * HD : (k + 1) * HD, :] / total)
    both = jnp.concatenate(rows, axis=0)
    for g in range(GROUP):
        o_ref[0, :, g * 2 * HD : (g + 1) * 2 * HD] = both[:, g * RUN : (g + 1) * RUN].T


def attend_call(starts_q, starts_k, query, kv):
    sequences, rows, width = query.shape
    runs = kv.shape[1]
    columns = GROUP * RUN
    smem = pl.BlockSpec(memory_space=pltpu.SMEM)
    row_spec = pl.BlockSpec((1, RUN, width), lambda s, r: (s, r, 0))
    return pl.pallas_call(
        attend_kernel,
        grid=(sequences, rows // RUN),
        in_specs=[
            smem,
            smem,
            row_spec,
            pl.BlockSpec((1,) + kv.shape[1:], lambda s, r: (s, 0, 0, 0)),
        ],
        out_specs=[row_spec, pl.BlockSpec((1, 1, 2, columns), lambda s, r: (s, r, 0, 0))],
        out_shape=[
            jax.ShapeDtypeStruct((sequences, rows, width), F32),
            jax.ShapeDtypeStruct((sequences, rows // RUN, 2, columns), F32),
        ],
        scratch_shapes=[
            pltpu.VMEM((2, runs * RUN, columns), F32),
            pltpu.VMEM((2, 8, columns), F32),
            pltpu.VMEM((2, 8, columns), F32),
            pltpu.VMEM((2, 2 * HD, columns), F32),
        ],
        compiler_params=pltpu.CompilerParams(vmem_limit_bytes=56 * 1024 * 1024),
        cost_estimate=pl.CostEstimate(
            flops=4 * sequences * rows * runs * RUN * width,
            bytes_accessed=kv.size * 2 + query.size * 6,
            transcendentals=sequences * rows * runs * RUN * 4,
        ),
        name="attend",
    )(starts_q, starts_k, query, kv)


def attend_back_kernel(
    sq_ref, sk_ref, q_ref, do_ref, o_ref, lse_ref, kv_ref, cos_ref, sin_ref, dq_ref, dkv_ref, sum_ref, acc_ref
):
    seq, run = pl.program_id(0), pl.program_id(1)
    start = sq_ref[seq, run]
    runs = kv_ref.shape[1]
    queries = stack_heads(q_ref[0])
    upstream = stack_heads(do_ref[0])
    attended = stack_heads(o_ref[0])
    q_pair = [half_mask(queries, k) for k in range(2)]
    u_pair = [half_mask(upstream, k) for k in range(2)]
    product = upstream.astype(F32) * attended
    deltas = [
        lax.dot_general(
            half_mask(jnp.ones((8, 2 * HD), F32), k),
            product,
            NT,
            precision=lax.Precision.HIGHEST,
            preferred_element_type=F32,
        )[:1]
        for k in range(2)
    ]
    lses = [lse_ref[0, 0, k : k + 1, :] for k in range(2)]
    acc_ref[...] = jnp.zeros_like(acc_ref)

    @pl.when(run == 0)
    def _():
        sum_ref[...] = jnp.zeros_like(sum_ref)

    def step(i, carry):
        key_start = sk_ref[seq, i]

        def work(masked):
            keys = kv_ref[0, i, :, : 2 * HD]
            values = kv_ref[0, i, :, 2 * HD :]
            for k in range(2):
                s = mm(keys, q_pair[k], NT) * (SCALE * LOG2E)
                if masked:
                    s = jnp.where(causal_mask(s.shape), s, NEGATIVE)
                p = jnp.exp2(s - lses[k])
                dp = mm(values, u_pair[k], NT)
                ds = (p * (dp - deltas[k])).astype(BF)
                sum_ref[i, :, : 2 * HD] += mm(ds, q_pair[k])
                sum_ref[i, :, 2 * HD :] += mm(p.astype(BF), u_pair[k])
                acc_ref[k] += mm(keys, ds, TN)

        @pl.when(key_start < start)
        def _():
            work(False)

        @pl.when(key_start == start)
        def _():
            work(True)

        return carry

    lax.fori_loop(0, runs, step, 0)
    both = jnp.concatenate([acc_ref[k, k * HD : (k + 1) * HD, :] for k in range(2)], axis=0)
    cos, sin = cos_ref[0], sin_ref[0]
    for g in range(GROUP):
        v = both[:, g * RUN : (g + 1) * RUN].T * SCALE
        dq_ref[0, :, g * 2 * HD : (g + 1) * 2 * HD] = (v * cos - swap_halves(v) * sin).astype(BF)

    @pl.when(run == pl.num_programs(1) - 1)
    def _():
        dkv_ref[0, :, :, : 2 * HD] = (sum_ref[:, :, : 2 * HD] * SCALE).astype(BF)
        dkv_ref[0, :, :, 2 * HD :] = sum_ref[:, :, 2 * HD :].astype(BF)


def attend_back_call(starts_q, starts_k, query, upstream, attended, lse, kv, cos, sin):
    sequences, rows, width = query.shape
    runs = kv.shape[1]
    columns = GROUP * RUN
    smem = pl.BlockSpec(memory_space=pltpu.SMEM)
    row_spec = pl.BlockSpec((1, RUN, width), lambda s, r: (s, r, 0))
    table_spec = pl.BlockSpec((1, RUN, 2 * HD), lambda s, r: (s, r, 0))
    kv_spec = pl.BlockSpec((1,) + kv.shape[1:], lambda s, r: (s, 0, 0, 0))
    return pl.pallas_call(
        attend_back_kernel,
        grid=(sequences, rows // RUN),
        in_specs=[
            smem,
            smem,
            row_spec,
            row_spec,
            row_spec,
            pl.BlockSpec((1, 1, 2, columns), lambda s, r: (s, r, 0, 0)),
            kv_spec,
            table_spec,
            table_spec,
        ],
        out_specs=[row_spec, kv_spec],
        out_shape=[
            jax.ShapeDtypeStruct((sequences, rows, width), BF),
            jax.ShapeDtypeStruct(kv.shape, BF),
        ],
        scratch_shapes=[
            pltpu.VMEM((runs, RUN, 4 * HD), F32),
            pltpu.VMEM((2, 2 * HD, columns), F32),
        ],
        compiler_params=pltpu.CompilerParams(vmem_limit_bytes=56 * 1024 * 1024),
        cost_estimate=pl.CostEstimate(
            flops=10 * sequences * rows * runs * RUN * width,
            bytes_accessed=kv.size * 4 + query.size * 10,
            transcendentals=sequences * rows * runs * RUN * 4,
        ),
        name="attend_back",
    )(starts_q, starts_k, query, upstream, attended, lse, kv, cos, sin)


def rotation_tables(place_rows):
    half = HD // 2
    frequency = jnp.exp(jnp.arange(half, dtype=F32) * (-2.0 * math.log(ROPE_BASE) / HD))
    angles = place_rows.astype(F32)[..., None] * frequency
    cos, sin = jnp.cos(angles), jnp.sin(angles)
    return (
        jnp.concatenate([cos, cos, cos, cos], axis=-1),
        jnp.concatenate([-sin, sin, -sin, sin], axis=-1),
    )


def pair_heads(w):
    return w.reshape(w.shape[0], 2, GROUP, HD).swapaxes(1, 2).reshape(w.shape[0], -1)


def unpair_heads(w):
    return w.reshape(w.shape[0], GROUP, 2, HD).swapaxes(1, 2).reshape(w.shape[0], -1)


def local(
    hidden,
    positions,
    norm_attention,
    w_query,
    w_key,
    w_value,
    w_out,
    norm_feed,
    w_gate,
    w_up,
    w_down,
    cotangent,
    *,
    n,
):
    sequences, rows, width = hidden.shape
    half = rows // 2
    quarter = half // 2
    place, head = lax.axis_index("ctx"), lax.axis_index("head")
    seq, core = head // 2, head % 2
    order = jnp.array(ring_order(n), jnp.int32)
    ring_place = jnp.where(place % 2 == 0, place // 2, n - 1 - place // 2)
    steps = jnp.arange(n, dtype=jnp.int32)
    right_from = order[(ring_place - steps) % n]
    left_from = order[(ring_place + steps) % n]

    gain_a = norm_attention.astype(F32)[:, None]
    gain_f = norm_feed.astype(F32)[:, None]
    own_qkv = jnp.concatenate([pair_heads(w_query), w_key, w_value], axis=1)
    q_width, k_width = w_query.shape[1], w_key.shape[1]
    qkv_weight = lax.all_gather(
        (own_qkv.astype(F32) * gain_a).astype(BF), "ctx", axis=0, tiled=True
    )
    out_weight_t = lax.all_gather(pair_heads(w_out.T), "ctx", axis=0, tiled=True)

    def spread(w):
        cut = w.reshape(w.shape[0], n, -1).swapaxes(0, 1)
        got = lax.all_to_all(cut, "ctx", 0, 0, tiled=True)
        own = got.reshape(width, -1)
        far = other_x(own)
        pair = jnp.concatenate([own, far], axis=1)
        return jnp.concatenate([pair, other_core(pair)], axis=1)

    gate_weight = spread((w_gate.astype(F32) * gain_f).astype(BF))
    up_weight = spread((w_up.astype(F32) * gain_f).astype(BF))
    down_weight_t = spread(w_down.T)
    units = gate_weight.shape[1]

    def own_rows(array):
        return lax.dynamic_slice(array, (seq, core * half, 0), (1, half, width))[0]

    own_cotangent = own_rows(cotangent)
    cot_all = lax.all_gather(own_cotangent, "ctx", axis=0)
    cot_rows = jnp.concatenate(
        [lax.dynamic_index_in_dim(cot_all, right_from[s], 0, False)[:quarter] for s in range(n)]
        + [lax.dynamic_index_in_dim(cot_all, left_from[s], 0, False)[quarter:] for s in range(n)],
        axis=0,
    )

    own_positions = lax.dynamic_slice_in_dim(positions, place * rows, rows, 1)
    cos, sin = rotation_tables(own_positions)
    starts = positions[:, ::RUN] // RUN
    starts_q = own_positions[:, ::RUN] // RUN
    starts_k = jnp.take(starts, jnp.concatenate([right_from * 2, left_from * 2 + 1]), axis=1)
    unit_a, query, key_value = qkv_call(
        hidden, qkv_weight, cos, sin, q_width, 2 * k_width
    )
    rights, lefts = ring_gather(key_value[:, :RUN], key_value[:, RUN:], n)
    kv = jnp.stack(rights + lefts, axis=1)
    attended_full, lse = attend_call(starts_q, starts_k, query, kv)
    attended = attended_full.astype(BF).reshape(sequences * rows, q_width)
    out_partial = mm(attended, out_weight_t, NT).astype(BF).reshape(sequences, rows, width)
    own_hidden = own_rows(hidden).astype(F32)
    x1 = own_hidden + head_scatter(out_partial, seq, core)

    inverse_f = lax.rsqrt(jnp.mean(x1 * x1, axis=-1, keepdims=True) + EPSILON)
    unit_f = x1 * inverse_f
    unit_low = unit_f.astype(BF)
    rights, lefts = ring_gather(unit_low[:quarter], unit_low[quarter:], n)
    feed_rows = jnp.concatenate(rights + lefts, axis=0)
    gate = mm(feed_rows, gate_weight)
    up = mm(feed_rows, up_weight)
    dact = mm(cot_rows, down_weight_t)
    sigma = jax.nn.sigmoid(gate)
    silu = gate * sigma
    act = (silu * up).astype(BF)
    dgate = (dact * up * sigma * (1.0 + gate * (1.0 - sigma))).astype(BF)
    dup = (dact * silu).astype(BF)
    e_partial = (mm(dgate, gate_weight, NT) + mm(dup, up_weight, NT)).astype(BF)
    e_pieces = [e_partial[j * quarter : (j + 1) * quarter] for j in range(2 * n)]
    e_right, e_left = ring_scatter(e_pieces[:n], e_pieces[n:], n)
    e_feed = jnp.concatenate([e_right, e_left], axis=0).astype(F32)
    mid_grad = own_cotangent.astype(F32) + inverse_f * (
        e_feed - unit_f * jnp.mean(e_feed * unit_f, axis=-1, keepdims=True)
    )
    mid_low = head_gather(mid_grad.astype(BF), seq, core).reshape(sequences * rows, width)

    ring_of = jnp.arange(n, dtype=jnp.int32)
    ring_of = jnp.where(ring_of % 2 == 0, ring_of // 2, n - 1 - ring_of // 2)
    right_step = (ring_place - ring_of) % n
    left_step = (ring_of - ring_place) % n + n
    act_rows = jnp.concatenate(
        [
            lax.dynamic_slice_in_dim(act, step[t] * quarter, quarter, 0)
            for t in range(n)
            for step in (right_step, left_step)
        ],
        axis=0,
    )
    down_sum = lax.psum_scatter(
        mm(act_rows, down_weight_t, NT).astype(BF), "ctx", scatter_dimension=0, tiled=True
    )
    x2 = x1 + down_sum.astype(F32)
    output = head_gather(x2.astype(BF), seq, core)

    def collect(left_rows, right_rows):
        grad = mm(left_rows, right_rows, TN).astype(BF)
        pieces = [grad[:, j * units // 4 : (j + 1) * units // 4] for j in range(4)]
        kept = jnp.concatenate([pieces[0], pieces[1]], axis=1)
        sent = jnp.concatenate([pieces[2], pieces[3]], axis=1)
        near = kept.astype(F32) + other_core(sent).astype(F32)
        total = near[:, : units // 4] + other_x(near[:, units // 4 :].astype(BF)).astype(F32)
        cut = total.astype(BF).reshape(n, width // n, -1)
        got = lax.all_to_all(cut, "ctx", 0, 0, tiled=True)
        return got.swapaxes(0, 1).reshape(width // n, -1).astype(F32)

    gate_grad = collect(feed_rows, dgate)
    up_grad = collect(feed_rows, dup)
    down_grad = collect(cot_rows, act).T
    feed_sums = jnp.sum(
        gate_grad * w_gate.astype(F32) + up_grad * w_up.astype(F32), axis=1, keepdims=True
    )

    attended_grad = mm(mid_low, out_weight_t).astype(BF).reshape(sequences, rows, q_width)
    dquery, dkv = attend_back_call(
        starts_q, starts_k, query, attended_grad, attended_full, lse, kv, cos, sin
    )
    dkv_right, dkv_left = ring_scatter(
        [dkv[:, j] for j in range(n)], [dkv[:, n + j] for j in range(n)], n
    )
    dkv_own = jnp.concatenate([dkv_right, dkv_left], axis=1).astype(F32)
    dkey_rot = dkv_own[:, :, :k_width]
    swapped = jnp.concatenate(
        [
            dkey_rot[:, :, HD // 2 : HD],
            dkey_rot[:, :, : HD // 2],
            dkey_rot[:, :, HD + HD // 2 :],
            dkey_rot[:, :, HD : HD + HD // 2],
        ],
        axis=-1,
    )
    dkey = dkey_rot * cos - swapped * sin
    dqkv = jnp.concatenate(
        [dquery, dkey.astype(BF), dkv_own[:, :, k_width:].astype(BF)], axis=2
    ).reshape(sequences * rows, -1)
    unit_rows = unit_a.reshape(sequences * rows, width)

    def scatter(left_rows, right_rows):
        return lax.psum_scatter(
            mm(left_rows, right_rows, TN).astype(BF), "ctx", scatter_dimension=0, tiled=True
        ).astype(F32)

    out_grad = unpair_heads(scatter(mid_low, attended)).T
    query_sum = scatter(unit_rows, dquery.reshape(sequences * rows, -1))
    kv_sum = scatter(unit_rows, dqkv[:, q_width:])
    own_weight = own_qkv.astype(F32)
    attention_sums = jnp.sum(
        query_sum * own_weight[:, :q_width], axis=1, keepdims=True
    ) + jnp.sum(kv_sum * own_weight[:, q_width:], axis=1, keepdims=True)
    query_grad = unpair_heads(query_sum) * gain_a
    kv_grad = kv_sum * gain_a

    e_out = mm(dqkv, qkv_weight, NT).astype(BF).reshape(sequences, rows, width)
    e_in = head_scatter(e_out, seq, core)
    inverse_a = lax.rsqrt(jnp.mean(own_hidden * own_hidden, axis=-1, keepdims=True) + EPSILON)
    unit_own = own_hidden * inverse_a
    input_grad = mid_grad + inverse_a * (
        e_in - unit_own * jnp.mean(e_in * unit_own, axis=-1, keepdims=True)
    )
    input_grad = head_gather(input_grad.astype(BF), seq, core).astype(F32)

    sums = jnp.concatenate([attention_sums, feed_sums], axis=1).T
    sums = sums + other_core(sums)
    sums = sums + other_x(sums)

    return (
        output,
        input_grad,
        sums[0],
        query_grad,
        kv_grad[:, :k_width],
        kv_grad[:, k_width:],
        out_grad,
        sums[1],
        gate_grad * gain_f,
        up_grad * gain_f,
        down_grad,
    )


def solution(mesh):
    return jax.shard_map(
        functools.partial(local, n=mesh.shape["ctx"]),
        mesh=mesh,
        in_specs=(
            P(None, "ctx", None),
            P(),
            P("ctx"),
            P("ctx", "head"),
            P("ctx", "head"),
            P("ctx", "head"),
            P("head", "ctx"),
            P("ctx"),
            P("ctx", "head"),
            P("ctx", "head"),
            P("head", "ctx"),
            P(None, "ctx", None),
        ),
        out_specs=(
            P(None, "ctx", None),
            P(None, "ctx", None),
            P("ctx"),
            P("ctx", "head"),
            P("ctx", "head"),
            P("ctx", "head"),
            P("head", "ctx"),
            P("ctx"),
            P("ctx", "head"),
            P("ctx", "head"),
            P("head", "ctx"),
        ),
        check_vma=False,
    )
```

```python
import functools
import math

import jax
import jax.numpy as jnp
from jax import lax
from jax.experimental import pallas as pl
from jax.experimental.pallas import tpu as pltpu
from jax.sharding import PartitionSpec as P

HQ = 32
HK = 8
HD = 64
GROUP = HQ // HK
RUN = 128

EPSILON = 1e-05
ROPE_BASE = 500000.0
NEGATIVE = -1e30
LOG2E = math.log2(math.e)
SCALE = HD ** (-0.5)
BF = jnp.bfloat16
F32 = jnp.float32

NN = (((1,), (0,)), ((), ()))
NT = (((1,), (1,)), ((), ()))
TN = (((0,), (0,)), ((), ()))


def mm(a, b, dims=NN):
    return lax.dot_general(a, b, dims, preferred_element_type=F32)


def ring_order(n):
    return list(range(0, n, 2)) + list(range(1, n, 2))[::-1]


def ring_step(value, n):
    order = ring_order(n)
    pairs = []
    for p in range(n):
        for h in range(4):
            step = 1 if h % 2 == 0 else -1
            pairs.append((order[p] * 4 + h, order[(p + step) % n] * 4 + h))
    return lax.ppermute(value, ("ctx", "head"), pairs)


def in_turn(value, other):
    return value if other is None else lax.optimization_barrier((value, other))[0]


class Side:
    def __init__(self, hooks):
        self.hooks, self.due = hooks or {}, {}

    def before(self, step, value):
        return in_turn(value, self.due.pop(step, None))

    def after(self, step, token):
        if step in self.hooks:
            self.due[step + 2] = self.hooks[step](token)


def ring_gather(chains, n, hooks=None, pieces=None):
    chains, side, last = list(chains), Side(hooks), None
    pieces = [] if pieces is None else pieces
    pieces.append(tuple(chains))
    for step in range(n - 1):
        chains[0] = side.before(step, chains[0])
        for j in range(len(chains)):
            last = chains[j] = in_turn(ring_step(chains[j], n), last)
        pieces.append(tuple(chains))
        side.after(step, last)
    return pieces


def ring_scatter(pieces, n, hooks=None):
    totals, side, last = list(pieces[1 % n]), Side(hooks), None
    for step, s in enumerate(list(range(2, n)) + [0]):
        totals[0] = side.before(step, totals[0])
        for j in range(len(totals)):
            got = in_turn(ring_step(totals[j], n), last)
            last = totals[j] = (got.astype(F32) + pieces[s][j].astype(F32)).astype(BF)
        side.after(step, last)
    return jnp.concatenate(totals, axis=0)


def cut_chains(piece, n):
    count = 2 if n <= 8 else 1
    size = piece.shape[0] // count
    return tuple(piece[j * size : (j + 1) * size] for j in range(count))


def fold(weight, rows):
    count = rows // weight.shape[0]
    size = weight.shape[1] // count
    return jnp.concatenate([weight[:, j * size : (j + 1) * size] for j in range(count)], axis=0)


def unfold(folded, rows):
    count = folded.shape[0] // rows
    return jnp.concatenate([folded[j * rows : (j + 1) * rows] for j in range(count)], axis=1)


def other_core(value):
    return lax.ppermute(value, "head", [(h, h ^ 1) for h in range(4)])


def other_x(value):
    return lax.ppermute(value, "head", [(h, h ^ 2) for h in range(4)])


def head_scatter(partial, seq, core):
    half = partial.shape[1] // 2
    mine = lax.dynamic_slice_in_dim(partial, core * half, half, 1)
    theirs = lax.dynamic_slice_in_dim(partial, (1 - core) * half, half, 1)
    summed = mine.astype(F32) + other_core(theirs).astype(F32)
    keep = lax.dynamic_slice_in_dim(summed, seq, 1, 0)[0]
    send = lax.dynamic_slice_in_dim(summed, 1 - seq, 1, 0)[0].astype(BF)
    return keep + other_x(send).astype(F32)


def head_gather(own, seq, core):
    far = other_x(own)
    pair = jnp.where(seq == 0, jnp.stack([own, far]), jnp.stack([far, own]))
    near = other_core(pair)
    return jnp.where(
        core == 0, jnp.concatenate([pair, near], 1), jnp.concatenate([near, pair], 1)
    )


def swap_halves(v):
    lane = lax.broadcasted_iota(jnp.int32, v.shape, 1) % HD
    return jnp.where(lane < HD // 2, pltpu.roll(v, 2 * HD - HD // 2, 1), pltpu.roll(v, HD // 2, 1))


def rotated(v, cos, sin):
    return v * cos + swap_halves(v) * sin


def qkv_kernel(x_ref, w_ref, cos_ref, sin_ref, n_ref, kv_ref, q_ref):
    x = x_ref[0].astype(F32)
    inverse = lax.rsqrt(jnp.mean(x * x, axis=-1, keepdims=True) + EPSILON)
    unit = (x * inverse).astype(BF)
    n_ref[0] = unit
    y = mm(unit, w_ref[...])
    cos, sin = cos_ref[0], sin_ref[0]
    width = kv_ref.shape[2] // 2
    for j in range(0, width, 2 * HD):
        kv_ref[0, :, j : j + 2 * HD] = rotated(y[:, j : j + 2 * HD], cos, sin).astype(BF)
    kv_ref[0, :, width:] = y[:, width : 2 * width].astype(BF)
    for j in range(0, q_ref.shape[2], 2 * HD):
        at = 2 * width + j
        q_ref[0, :, j : j + 2 * HD] = rotated(y[:, at : at + 2 * HD], cos, sin).astype(BF)


def qkv_call(hidden, weight, cos, sin, q_width, kv_width):
    sequences, rows, width = hidden.shape
    spec = lambda w: pl.BlockSpec((1, RUN, w), lambda s, r: (s, r, 0))
    widths = (width, kv_width, q_width)
    return pl.pallas_call(
        qkv_kernel,
        grid=(sequences, rows // RUN),
        in_specs=[
            spec(width),
            pl.BlockSpec(weight.shape, lambda s, r: (0, 0)),
            spec(2 * HD),
            spec(2 * HD),
        ],
        out_specs=[spec(w) for w in widths],
        out_shape=[jax.ShapeDtypeStruct((sequences, rows, w), BF) for w in widths],
        compiler_params=pltpu.CompilerParams(vmem_limit_bytes=40 * 1024 * 1024),
        cost_estimate=pl.CostEstimate(
            flops=2 * sequences * rows * width * weight.shape[1],
            bytes_accessed=weight.size * 2 + hidden.size * 4,
            transcendentals=0,
        ),
        name="norm_qkv",
    )(hidden, weight, cos, sin)


def half_mask(v, which):
    lane = lax.broadcasted_iota(jnp.int32, v.shape, 1)
    keep = (lane < HD) if which == 0 else (lane >= HD)
    return jnp.where(keep, v, jnp.zeros_like(v))


def stack_heads(block):
    return jnp.concatenate(
        [block[:, g * 2 * HD : (g + 1) * 2 * HD] for g in range(GROUP)], axis=0
    )


def causal_mask(shape):
    key = lax.broadcasted_iota(jnp.int32, shape, 0)
    query = lax.broadcasted_iota(jnp.int32, shape, 1) % RUN
    return key <= query


def attend_kernel(sq_ref, sk_ref, q_ref, kv_ref, o_ref, lse_ref, s_ref, m_ref, l_ref, acc_ref):
    seq, run = pl.program_id(0), pl.program_id(1)
    start = sq_ref[seq, run]
    runs = kv_ref.shape[1]
    columns = GROUP * RUN
    queries = stack_heads(q_ref[0])
    q_pair = [half_mask(queries, k) for k in range(2)]
    m_ref[...] = jnp.full_like(m_ref, NEGATIVE)
    l_ref[...] = jnp.zeros_like(l_ref)
    acc_ref[...] = jnp.zeros_like(acc_ref)

    def score_step(i, carry):
        key_start = sk_ref[seq, i]

        def scores(masked):
            keys = kv_ref[0, i, :, : 2 * HD]
            for k in range(2):
                s = mm(keys, q_pair[k], NT) * (SCALE * LOG2E)
                if masked:
                    s = jnp.where(causal_mask(s.shape), s, NEGATIVE)
                s_ref[k, pl.ds(pl.multiple_of(i * RUN, RUN), RUN), :] = s
                m_ref[k] = jnp.maximum(m_ref[k], jnp.max(s.reshape(-1, 8, columns), axis=0))

        @pl.when(key_start < start)
        def _():
            scores(False)

        @pl.when(key_start == start)
        def _():
            scores(True)

        return carry

    lax.fori_loop(0, runs, score_step, 0)
    peaks = [jnp.max(m_ref[k], axis=0, keepdims=True) for k in range(2)]

    def value_step(i, carry):
        @pl.when(sk_ref[seq, i] <= start)
        def _():
            values = kv_ref[0, i, :, 2 * HD :]
            for k in range(2):
                p = jnp.exp2(s_ref[k, pl.ds(pl.multiple_of(i * RUN, RUN), RUN), :] - peaks[k])
                l_ref[k] += jnp.sum(p.reshape(-1, 8, columns), axis=0)
                acc_ref[k] += mm(values, p.astype(BF), TN)

        return carry

    lax.fori_loop(0, runs, value_step, 0)
    rows = []
    for k in range(2):
        total = jnp.sum(l_ref[k], axis=0, keepdims=True)
        lse_ref[0, 0, k : k + 1, :] = peaks[k] + jnp.log2(total)
        rows.append(acc_ref[k, k * HD : (k + 1) * HD, :] / total)
    both = jnp.concatenate(rows, axis=0)
    for g in range(GROUP):
        o_ref[0, :, g * 2 * HD : (g + 1) * 2 * HD] = both[:, g * RUN : (g + 1) * RUN].T


def attend_call(starts_q, starts_k, query, kv):
    sequences, rows, width = query.shape
    runs = kv.shape[1]
    columns = GROUP * RUN
    smem = pl.BlockSpec(memory_space=pltpu.SMEM)
    row_spec = pl.BlockSpec((1, RUN, width), lambda s, r: (s, r, 0))
    return pl.pallas_call(
        attend_kernel,
        grid=(sequences, rows // RUN),
        in_specs=[
            smem,
            smem,
            row_spec,
            pl.BlockSpec((1,) + kv.shape[1:], lambda s, r: (s, 0, 0, 0)),
        ],
        out_specs=[row_spec, pl.BlockSpec((1, 1, 2, columns), lambda s, r: (s, r, 0, 0))],
        out_shape=[
            jax.ShapeDtypeStruct((sequences, rows, width), F32),
            jax.ShapeDtypeStruct((sequences, rows // RUN, 2, columns), F32),
        ],
        scratch_shapes=[
            pltpu.VMEM((2, runs * RUN, columns), F32),
            pltpu.VMEM((2, 8, columns), F32),
            pltpu.VMEM((2, 8, columns), F32),
            pltpu.VMEM((2, 2 * HD, columns), F32),
        ],
        compiler_params=pltpu.CompilerParams(vmem_limit_bytes=56 * 1024 * 1024),
        cost_estimate=pl.CostEstimate(
            flops=50 * sequences * rows * runs * RUN * width,
            bytes_accessed=kv.size * 2 + query.size * 6,
            transcendentals=sequences * rows * runs * RUN * 4,
        ),
        name="attend",
    )(starts_q, starts_k, query, kv)


def attend_back_kernel(
    sq_ref, sk_ref, q_ref, do_ref, o_ref, lse_ref, kv_ref, cos_ref, sin_ref, dq_ref, dkv_ref, sum_ref, acc_ref
):
    seq, run = pl.program_id(0), pl.program_id(1)
    start = sq_ref[seq, run]
    runs = kv_ref.shape[1]
    queries = stack_heads(q_ref[0])
    upstream = stack_heads(do_ref[0])
    attended = stack_heads(o_ref[0])
    q_pair = [half_mask(queries, k) for k in range(2)]
    u_pair = [half_mask(upstream, k) for k in range(2)]
    product = upstream.astype(F32) * attended
    deltas = [
        lax.dot_general(
            half_mask(jnp.ones((8, 2 * HD), F32), k),
            product,
            NT,
            precision=lax.Precision.HIGHEST,
            preferred_element_type=F32,
        )[:1]
        for k in range(2)
    ]
    lses = [lse_ref[0, 0, k : k + 1, :] for k in range(2)]
    acc_ref[...] = jnp.zeros_like(acc_ref)

    @pl.when(run == 0)
    def _():
        sum_ref[...] = jnp.zeros_like(sum_ref)

    def step(i, carry):
        key_start = sk_ref[seq, i]

        def work(masked):
            keys = kv_ref[0, i, :, : 2 * HD]
            values = kv_ref[0, i, :, 2 * HD :]
            for k in range(2):
                s = mm(keys, q_pair[k], NT) * (SCALE * LOG2E)
                if masked:
                    s = jnp.where(causal_mask(s.shape), s, NEGATIVE)
                p = jnp.exp2(s - lses[k])
                dp = mm(values, u_pair[k], NT)
                ds = (p * (dp - deltas[k])).astype(BF)
                sum_ref[i, :, : 2 * HD] += mm(ds, q_pair[k])
                sum_ref[i, :, 2 * HD :] += mm(p.astype(BF), u_pair[k])
                acc_ref[k] += mm(keys, ds, TN)

        @pl.when(key_start < start)
        def _():
            work(False)

        @pl.when(key_start == start)
        def _():
            work(True)

        return carry

    lax.fori_loop(0, runs, step, 0)
    both = jnp.concatenate([acc_ref[k, k * HD : (k + 1) * HD, :] for k in range(2)], axis=0)
    cos, sin = cos_ref[0], sin_ref[0]
    for g in range(GROUP):
        v = both[:, g * RUN : (g + 1) * RUN].T * SCALE
        dq_ref[0, :, g * 2 * HD : (g + 1) * 2 * HD] = (v * cos - swap_halves(v) * sin).astype(BF)

    @pl.when(run == pl.num_programs(1) - 1)
    def _():
        dkv_ref[0, :, :, : 2 * HD] = (sum_ref[:, :, : 2 * HD] * SCALE).astype(BF)
        dkv_ref[0, :, :, 2 * HD :] = sum_ref[:, :, 2 * HD :].astype(BF)


def attend_back_call(starts_q, starts_k, query, upstream, attended, lse, kv, cos, sin):
    sequences, rows, width = query.shape
    runs = kv.shape[1]
    columns = GROUP * RUN
    smem = pl.BlockSpec(memory_space=pltpu.SMEM)
    row_spec = pl.BlockSpec((1, RUN, width), lambda s, r: (s, r, 0))
    table_spec = pl.BlockSpec((1, RUN, 2 * HD), lambda s, r: (s, r, 0))
    kv_spec = pl.BlockSpec((1,) + kv.shape[1:], lambda s, r: (s, 0, 0, 0))
    return pl.pallas_call(
        attend_back_kernel,
        grid=(sequences, rows // RUN),
        in_specs=[
            smem,
            smem,
            row_spec,
            row_spec,
            row_spec,
            pl.BlockSpec((1, 1, 2, columns), lambda s, r: (s, r, 0, 0)),
            kv_spec,
            table_spec,
            table_spec,
        ],
        out_specs=[row_spec, kv_spec],
        out_shape=[
            jax.ShapeDtypeStruct((sequences, rows, width), BF),
            jax.ShapeDtypeStruct(kv.shape, BF),
        ],
        scratch_shapes=[
            pltpu.VMEM((runs, RUN, 4 * HD), F32),
            pltpu.VMEM((2, 2 * HD, columns), F32),
        ],
        compiler_params=pltpu.CompilerParams(vmem_limit_bytes=56 * 1024 * 1024),
        cost_estimate=pl.CostEstimate(
            flops=80 * sequences * rows * runs * RUN * width,
            bytes_accessed=kv.size * 4 + query.size * 10,
            transcendentals=sequences * rows * runs * RUN * 4,
        ),
        name="attend_back",
    )(starts_q, starts_k, query, upstream, attended, lse, kv, cos, sin)


def feed_kernel(count, *refs):
    pieces, refs = refs[:count], refs[count:]
    gate0, gate1, up0, up1, down0, down1, *refs = refs
    outs, refs = refs[:count], refs[count:]
    dgate_ref, dup_ref, act_ref, h_ref, c_ref, e_ref, x_ref = refs
    step = pl.program_id(0)
    width = h_ref.shape[1]
    rows = pieces[0].shape[0]

    @pl.when(step == 0)
    def _():
        for at, piece in enumerate(pieces):
            h_ref[at * rows : (at + 1) * rows] = piece[:, :width]
            c_ref[at * rows : (at + 1) * rows] = piece[:, width:]
        e_ref[...] = jnp.zeros_like(e_ref)
        x_ref[...] = jnp.zeros_like(x_ref)

    def work(w_gate, w_up, w_down):
        gate = mm(h_ref[...], w_gate[...])
        up = mm(h_ref[...], w_up[...])
        dact = mm(c_ref[...], w_down[...])
        sigma = 1.0 / (1.0 + jnp.exp(-gate))
        silu = gate * sigma
        act = (silu * up).astype(BF)
        dgate = (dact * up * sigma * (1.0 + gate * (1.0 - sigma))).astype(BF)
        dup = (dact * silu).astype(BF)
        act_ref[...] = act
        dgate_ref[...] = dgate
        dup_ref[...] = dup
        e_ref[...] += mm(dgate, w_gate[...], NT) + mm(dup, w_up[...], NT)
        x_ref[...] += mm(act, w_down[...], NT)

    @pl.when(step < pl.num_programs(0) // 2)
    def _():
        work(gate0, up0, down0)

    @pl.when(step >= pl.num_programs(0) // 2)
    def _():
        work(gate1, up1, down1)

    @pl.when(step == pl.num_programs(0) - 1)
    def _():
        for at, out in enumerate(outs):
            out[:, :width] = e_ref[at * rows : (at + 1) * rows].astype(BF)
            out[:, width:] = x_ref[at * rows : (at + 1) * rows].astype(BF)


def feed_call(pieces, weights):
    count = len(pieces)
    rows, double = pieces[0].shape
    width = double // 2
    chunk = weights[0].shape[1]
    units = 2 * chunk
    weight_spec = pl.BlockSpec((width, chunk), lambda u: (0, 0))
    whole = pl.BlockSpec((rows, double), lambda u: (0, 0))
    slab = pl.BlockSpec((count * rows, chunk), lambda u: (0, u))
    return pl.pallas_call(
        functools.partial(feed_kernel, count),
        grid=(2,),
        in_specs=[whole] * count + [weight_spec] * 6,
        out_specs=[whole] * count + [slab, slab, slab],
        out_shape=[jax.ShapeDtypeStruct((rows, double), BF)] * count
        + [jax.ShapeDtypeStruct((count * rows, units), BF)] * 3,
        scratch_shapes=[
            pltpu.VMEM((count * rows, width), BF),
            pltpu.VMEM((count * rows, width), BF),
            pltpu.VMEM((count * rows, width), F32),
            pltpu.VMEM((count * rows, width), F32),
        ],
        compiler_params=pltpu.CompilerParams(vmem_limit_bytes=56 * 1024 * 1024),
        cost_estimate=pl.CostEstimate(
            flops=12 * count * rows * width * units,
            bytes_accessed=6 * width * units + 12 * count * rows * width,
            transcendentals=0,
        ),
        name="feed",
    )(*pieces, *weights)


def reorder_kernel(index_ref, x_ref, o_ref):
    for t in range(o_ref.shape[0]):
        o_ref[t] = x_ref[index_ref[t]]


def reorder_call(index, blocks):
    return pl.pallas_call(
        reorder_kernel,
        in_specs=[
            pl.BlockSpec(memory_space=pltpu.SMEM),
            pl.BlockSpec(memory_space=pltpu.VMEM),
        ],
        out_specs=pl.BlockSpec(memory_space=pltpu.VMEM),
        out_shape=jax.ShapeDtypeStruct(blocks.shape, blocks.dtype),
        compiler_params=pltpu.CompilerParams(vmem_limit_bytes=32 * 1024 * 1024),
        name="reorder",
    )(index, blocks)


def ctx_order_kernel(index_ref, *refs):
    *pieces, o_ref = refs
    count = len(pieces) // o_ref.shape[0]
    rows = pieces[0].shape[0]
    for at, piece in enumerate(pieces):
        to = index_ref[at // count]
        part = at % count
        o_ref[to, part * rows : (part + 1) * rows, :] = piece[...]


def ctx_order_call(ring_from, pieces):
    n, count = len(pieces), len(pieces[0])
    rows, width = pieces[0][0].shape
    vmem = pl.BlockSpec(memory_space=pltpu.VMEM)
    return pl.pallas_call(
        ctx_order_kernel,
        in_specs=[pl.BlockSpec(memory_space=pltpu.SMEM)] + [vmem] * (n * count),
        out_specs=vmem,
        out_shape=jax.ShapeDtypeStruct((n, count * rows, width), BF),
        compiler_params=pltpu.CompilerParams(vmem_limit_bytes=32 * 1024 * 1024),
        name="ctx_order",
    )(ring_from, *[part for piece in pieces for part in piece])


def unpack_kernel(index_ref, *refs):
    *pieces, kv_ref, w_ref = refs
    sequences = kv_ref.shape[0]
    wide = kv_ref.shape[3]
    n, weight_rows, weight_width = w_ref.shape
    count = len(pieces) // n
    rows = pieces[0].shape[0]
    folds = count * rows // weight_rows
    size = weight_width // folds
    lines = min(rows, weight_rows)
    for at, piece in enumerate(pieces):
        for j in range(sequences):
            for r in range(rows // RUN):
                kv_ref[j, at * rows // RUN + r] = piece[
                    r * RUN : (r + 1) * RUN, j * wide : (j + 1) * wide
                ]
        for line in range(0, rows, lines):
            fold_at, row_at = divmod((at % count) * rows + line, weight_rows)
            w_ref[
                index_ref[at // count], row_at : row_at + lines, fold_at * size : (fold_at + 1) * size
            ] = piece[line : line + lines, sequences * wide :]


def unpack_call(ring_from, pieces, sequences, wide, weight_rows, weight_width):
    n, count = len(pieces), len(pieces[0])
    rows = pieces[0][0].shape[0]
    vmem = pl.BlockSpec(memory_space=pltpu.VMEM)
    return pl.pallas_call(
        unpack_kernel,
        in_specs=[pl.BlockSpec(memory_space=pltpu.SMEM)] + [vmem] * (n * count),
        out_specs=[vmem, vmem],
        out_shape=[
            jax.ShapeDtypeStruct((sequences, n * count * rows // RUN, RUN, wide), BF),
            jax.ShapeDtypeStruct((n, weight_rows, weight_width), BF),
        ],
        compiler_params=pltpu.CompilerParams(vmem_limit_bytes=48 * 1024 * 1024),
        name="unpack",
    )(ring_from, *[part for piece in pieces for part in piece])


def pack_kernel(index_ref, dkv_ref, w_ref, o_ref):
    sequences, n, rows, wide = dkv_ref.shape
    weight_rows, weight_width = w_ref.shape[1:]
    folds = rows // weight_rows
    size = weight_width // folds
    for s in range(n):
        for j in range(sequences):
            o_ref[s, :, j * wide : (j + 1) * wide] = dkv_ref[j, s]
        for j in range(folds):
            o_ref[s, j * weight_rows : (j + 1) * weight_rows, sequences * wide :] = w_ref[
                index_ref[s], :, j * size : (j + 1) * size
            ]


def pack_call(index, dkv, weight):
    sequences, n, rows, wide = dkv.shape
    extra = weight.shape[1] * weight.shape[2] // rows
    vmem = pl.BlockSpec(memory_space=pltpu.VMEM)
    return pl.pallas_call(
        pack_kernel,
        in_specs=[pl.BlockSpec(memory_space=pltpu.SMEM), vmem, vmem],
        out_specs=vmem,
        out_shape=jax.ShapeDtypeStruct((n, rows, sequences * wide + extra), BF),
        compiler_params=pltpu.CompilerParams(vmem_limit_bytes=48 * 1024 * 1024),
        name="pack",
    )(index, dkv, weight)


def finish_kernel(got_ref, w_ref, gain_ref, grad_ref, sum_ref):
    n, rows, chunk = got_ref.shape
    sums = jnp.zeros((rows, 1), F32)
    for t in range(n):
        grad = got_ref[t].astype(F32)
        grad_ref[:, t * chunk : (t + 1) * chunk] = grad * gain_ref[...]
        weight = w_ref[:, t * chunk : (t + 1) * chunk].astype(F32)
        sums += jnp.sum(grad * weight, axis=1, keepdims=True)
    sum_ref[...] = sums


def finish_call(got, weight, gain):
    n, rows, chunk = got.shape
    vmem = pl.BlockSpec(memory_space=pltpu.VMEM)
    return pl.pallas_call(
        finish_kernel,
        in_specs=[vmem] * 3,
        out_specs=[vmem] * 2,
        out_shape=[
            jax.ShapeDtypeStruct((rows, n * chunk), F32),
            jax.ShapeDtypeStruct((rows, 1), F32),
        ],
        compiler_params=pltpu.CompilerParams(vmem_limit_bytes=32 * 1024 * 1024),
        name="finish",
    )(got, weight, gain)


def finish_down_kernel(got_ref, grad_ref):
    n, rows, chunk = got_ref.shape
    for t in range(n):
        grad_ref[t * chunk : (t + 1) * chunk, :] = got_ref[t].astype(F32).T


def finish_down_call(got):
    n, rows, chunk = got.shape
    vmem = pl.BlockSpec(memory_space=pltpu.VMEM)
    return pl.pallas_call(
        finish_down_kernel,
        in_specs=[vmem],
        out_specs=vmem,
        out_shape=jax.ShapeDtypeStruct((n * chunk, rows), F32),
        compiler_params=pltpu.CompilerParams(vmem_limit_bytes=32 * 1024 * 1024),
        name="finish_down",
    )(got)


def rotation_tables(place_rows):
    half = HD // 2
    frequency = jnp.exp(jnp.arange(half, dtype=F32) * (-2.0 * math.log(ROPE_BASE) / HD))
    angles = place_rows.astype(F32)[..., None] * frequency
    cos, sin = jnp.cos(angles), jnp.sin(angles)
    return (
        jnp.concatenate([cos, cos, cos, cos], axis=-1),
        jnp.concatenate([-sin, sin, -sin, sin], axis=-1),
    )


def pair_heads(w):
    return w.reshape(w.shape[0], 2, GROUP, HD).swapaxes(1, 2).reshape(w.shape[0], -1)


def unpair_heads(w):
    return w.reshape(w.shape[0], GROUP, 2, HD).swapaxes(1, 2).reshape(w.shape[0], -1)


def local(
    hidden,
    positions,
    norm_attention,
    w_query,
    w_key,
    w_value,
    w_out,
    norm_feed,
    w_gate,
    w_up,
    w_down,
    cotangent,
    *,
    n,
):
    sequences, rows, width = hidden.shape
    half = rows // 2
    place, head = lax.axis_index("ctx"), lax.axis_index("head")
    seq, core = head // 2, head % 2
    order = jnp.array(ring_order(n), jnp.int32)
    ring_place = jnp.where(place % 2 == 0, place // 2, n - 1 - place // 2)
    step_sign = 1 - 2 * core
    ring_from = order[(ring_place - step_sign * jnp.arange(n, dtype=jnp.int32)) % n]

    gain_a = norm_attention.astype(F32)[:, None]
    gain_f = norm_feed.astype(F32)[:, None]
    q_width, k_width = w_query.shape[1], w_key.shape[1]
    own_qkv = jnp.concatenate([w_key, w_value, pair_heads(w_query)], axis=1)
    qkv_pieces = ring_gather(cut_chains((own_qkv.astype(F32) * gain_a).astype(BF), n), n)
    qkv_weight = ctx_order_call(ring_from, qkv_pieces).reshape(width, -1)

    def own_rows(array):
        return lax.dynamic_slice(array, (seq, core * half, 0), (1, half, width))[0]

    own_cotangent = own_rows(cotangent)

    def cut_units(w):
        return w.reshape(w.shape[0], n, -1).swapaxes(0, 1)

    def exchange(cut):
        return lax.all_to_all(cut, "ctx", 0, 0, tiled=True)

    def beside(own, far, token):
        return jnp.concatenate([in_turn(own, token), far], axis=1)

    gate_got = exchange(cut_units((w_gate.astype(F32) * gain_f).astype(BF)))
    qkv_weight, gate_got = lax.optimization_barrier((qkv_weight, gate_got))

    own_positions = lax.dynamic_slice_in_dim(positions, place * rows, rows, 1)
    cos, sin = rotation_tables(own_positions)
    starts = positions[:, ::RUN] // RUN
    starts_q = own_positions[:, ::RUN] // RUN
    key_runs = jnp.stack([ring_from * 2, ring_from * 2 + 1], axis=1).reshape(-1)
    starts_k = jnp.take(starts, key_runs, axis=1)
    unit_a, key_value, query = qkv_call(hidden, qkv_weight, cos, sin, q_width, 2 * k_width)
    pair_width = key_value.shape[2]
    gate_own = gate_got.reshape(width, -1)
    gate_far = other_x(gate_own)
    side = {}

    def gate_work(token):
        side["gate_pair"] = beside(gate_own, gate_far, token)
        side["gate_near"] = other_core(side["gate_pair"])
        return side["gate_pair"], side["gate_near"]

    pieces = ring_gather(
        cut_chains(
            jnp.concatenate([key_value[0], key_value[1], fold(pair_heads(w_out.T), rows)], axis=1), n
        ),
        n,
        {min(3, n - 3): gate_work},
    )
    kv, out_weight_t = unpack_call(
        ring_from, pieces, sequences, pair_width, width // n, q_width
    )
    out_weight_t = out_weight_t.reshape(width, q_width)
    kv, sent_up, sent_down = lax.optimization_barrier((kv, w_up, w_down))
    feed_sent = jnp.stack(
        [cut_units((sent_up.astype(F32) * gain_f).astype(BF)), cut_units(sent_down.T)], axis=1
    )
    feed_got = exchange(feed_sent)
    attended_full, lse = attend_call(starts_q, starts_k, query, kv)

    attended = attended_full.astype(BF).reshape(sequences * rows, q_width)
    out_partial = mm(attended, out_weight_t, NT).astype(BF).reshape(sequences, rows, width)
    own_hidden = own_rows(hidden).astype(F32)
    x1 = own_hidden + head_scatter(out_partial, seq, core)
    x1, feed_got = lax.optimization_barrier((x1, feed_got))

    inverse_f = lax.rsqrt(jnp.mean(x1 * x1, axis=-1, keepdims=True) + EPSILON)
    unit_f = x1 * inverse_f
    unit_low = unit_f.astype(BF)
    up_own, down_own = feed_got[:, 0].reshape(width, -1), feed_got[:, 1].reshape(width, -1)
    up_far, down_far = other_x(up_own), other_x(down_own)
    units = 4 * up_own.shape[1]
    arrived, feeds = [], []
    group = max(2, n // 8)

    def feed_work(token):
        j = group * len(feeds)
        parts = [part for piece in arrived[j : j + group] for part in piece]
        parts[0] = in_turn(parts[0], token)
        weights = [side[name + end] for name in ("gate", "up", "down") for end in ("_pair", "_near")]
        feeds.append(feed_call(parts, weights))
        return feeds[-1]

    def up_work(token):
        side["up_pair"] = beside(up_own, up_far, token)
        side["up_near"] = other_core(side["up_pair"])
        return side["up_pair"]

    def down_work(token):
        side["down_pair"] = beside(down_own, down_far, token)
        side["down_near"] = other_core(side["down_pair"])
        return feed_work(token)

    chains = cut_chains(jnp.concatenate([unit_low, own_cotangent], axis=1), n)
    ring_gather(
        chains, n, {n - 6: up_work, n - 5: down_work, n - 4: feed_work, n - 3: feed_work}, arrived
    )
    while len(feeds) < n // group:
        feed_work(None)
    partial, dgate, dup, act = [], [], [], []
    count = len(chains)
    for *outs, dgate_slab, dup_slab, act_slab in feeds:
        partial += [tuple(outs[j : j + count]) for j in range(0, len(outs), count)]
        dgate.append(dgate_slab)
        dup.append(dup_slab)
        act.append(act_slab)
    pieces = arrived
    parts = [part for piece in pieces for part in piece]
    feed_rows = jnp.concatenate([part[:, :width] for part in parts], axis=0)
    cot_rows = jnp.concatenate([part[:, width:] for part in parts], axis=0)
    dgate, dup, act = [jnp.concatenate(total, axis=0) for total in (dgate, dup, act)]

    def quarters(grad, at):
        size = units // 4
        return [grad[:, at + j * size : at + (j + 1) * size] for j in range(4)]

    def sum_cores(pieces):
        kept = jnp.concatenate([pieces[0], pieces[1]], axis=1)
        sent = jnp.concatenate([pieces[2], pieces[3]], axis=1)
        return (kept.astype(F32) + other_core(sent).astype(F32)).astype(BF)

    grads, near = [], []

    def grad_work(token):
        j = len(grads)
        rows_at, slab = ((feed_rows, dgate), (feed_rows, dup), (cot_rows, act))[j]
        grads.append(mm(rows_at, in_turn(slab, token), TN).astype(BF))
        return grads[-1]

    def near_work(token):
        near.append(sum_cores(quarters(in_turn(grads[len(near)], token), 0)))
        return near[-1]

    sums_own = ring_scatter(
        partial,
        n,
        {
            0: grad_work,
            1: lambda token: (grad_work(token), near_work(token)),
            2: lambda token: (grad_work(token), near_work(token)),
            3: near_work,
        },
    ).astype(F32)
    far = [other_x(w[:, units // 4 :]) for w in near[:2]]

    def sum_x(near, far, token):
        total = in_turn(near[:, : units // 4], token).astype(F32) + far.astype(F32)
        return total.astype(BF).reshape(n, width // n, -1)

    near_x = jnp.stack([sum_x(w, f, sums_own) for w, f in zip(near, far)], axis=1)
    e_feed, down_sum = sums_own[:, :width], sums_own[:, width:]
    mid_grad = own_cotangent.astype(F32) + inverse_f * (
        e_feed - unit_f * jnp.mean(e_feed * unit_f, axis=-1, keepdims=True)
    )
    delivered = exchange(near_x)
    mid_low = head_gather(mid_grad.astype(BF), seq, core).reshape(sequences * rows, width)

    unit_rows = unit_a.reshape(sequences * rows, width)
    attended_grad = mm(mid_low, out_weight_t).astype(BF).reshape(sequences, rows, q_width)
    out_grad_t = mm(mid_low, attended, TN).astype(BF)
    attended_grad, out_grad_t = lax.optimization_barrier((attended_grad, out_grad_t))
    down_far = other_x(in_turn(near[2][:, units // 4 :], attended_grad))
    dquery, dkv = attend_back_call(
        starts_q, starts_k, query, attended_grad, attended_full, lse, kv, cos, sin
    )
    dquery = dquery.reshape(sequences * rows, -1)
    dquery, dkv, delivered, down_sum = lax.optimization_barrier(
        (dquery, dkv, delivered, down_sum)
    )
    down_total = sum_x(near[2], down_far, dquery)
    down_delivered = exchange(down_total)
    dkv = dkv.reshape(sequences, n, 2 * RUN, pair_width)
    dkv_width = sequences * pair_width
    x2 = x1 + down_sum
    packed = pack_call(ring_from, dkv, out_grad_t.reshape(n, width // n, q_width))

    def gate_finish(token):
        side["gate"] = finish_call(in_turn(delivered[:, 0], token), w_gate, gain_f)
        return side["gate"]

    def up_finish(token):
        side["up"] = finish_call(in_turn(delivered[:, 1], token), w_up, gain_f)
        return side["up"]

    def output_work(token):
        side["output"] = head_gather(in_turn(x2, token).astype(BF), seq, core)
        return side["output"]

    ring_sum = ring_scatter(
        [cut_chains(packed[s], n) for s in range(n)],
        n,
        {0: output_work, 2: gate_finish, 3: up_finish},
    )
    output = side["output"]
    (gate_grad, gate_sums), (up_grad, up_sums) = side["gate"], side["up"]
    dkv_own = jnp.stack(
        [ring_sum[:, j * pair_width : (j + 1) * pair_width] for j in range(sequences)]
    ).astype(F32)
    out_sum = unfold(ring_sum[:, dkv_width:], width // n)
    dkey_rot = dkv_own[:, :, :k_width]
    swapped = jnp.concatenate(
        [
            dkey_rot[:, :, HD // 2 : HD],
            dkey_rot[:, :, : HD // 2],
            dkey_rot[:, :, HD + HD // 2 :],
            dkey_rot[:, :, HD : HD + HD // 2],
        ],
        axis=-1,
    )
    dkey = dkey_rot * cos - swapped * sin
    dkv_low = jnp.concatenate(
        [dkey.astype(BF), dkv_own[:, :, k_width:].astype(BF)], axis=2
    ).reshape(sequences * rows, -1)

    dqkv = jnp.concatenate([dkv_low, dquery], axis=1)
    e_out = mm(dqkv, qkv_weight, NT).astype(BF)
    qkv_grad = mm(unit_rows, dqkv, TN).astype(BF).reshape(n, width // n, -1)
    qkv_ring = reorder_call(ring_from, qkv_grad)

    def down_finish(token):
        side["down"] = finish_down_call(in_turn(down_delivered, token))
        return side["down"]

    def out_finish(token):
        side["out"] = unpair_heads(in_turn(out_sum, token).astype(F32)).T
        return side["out"]

    qkv_sum = ring_scatter(
        [cut_chains(qkv_ring[s], n) for s in range(n)], n, {1: out_finish, 3: down_finish}
    ).astype(F32)
    out_grad, down_grad = side["out"], side["down"]
    e_in = head_scatter(e_out.reshape(sequences, rows, width), seq, core)
    inverse_a = lax.rsqrt(jnp.mean(own_hidden * own_hidden, axis=-1, keepdims=True) + EPSILON)
    unit_own = own_hidden * inverse_a
    input_grad = mid_grad + inverse_a * (
        e_in - unit_own * jnp.mean(e_in * unit_own, axis=-1, keepdims=True)
    )
    input_grad = head_gather(input_grad.astype(BF), seq, core).astype(F32)

    feed_sums = gate_sums + up_sums
    attention_sums = jnp.sum(qkv_sum * own_qkv.astype(F32), axis=1, keepdims=True)
    qkv_sum = qkv_sum * gain_a
    kv_grad, query_grad = qkv_sum[:, : 2 * k_width], unpair_heads(qkv_sum[:, 2 * k_width :])
    sums = jnp.concatenate([attention_sums, feed_sums], axis=1).T
    sums = sums + other_core(sums)
    sums = sums + other_x(sums)

    return (
        output,
        input_grad,
        sums[0],
        query_grad,
        kv_grad[:, :k_width],
        kv_grad[:, k_width:],
        out_grad,
        sums[1],
        gate_grad,
        up_grad,
        down_grad,
    )


def solution(mesh):
    return jax.shard_map(
        functools.partial(local, n=mesh.shape["ctx"]),
        mesh=mesh,
        in_specs=(
            P(None, "ctx", None),
            P(),
            P("ctx"),
            P("ctx", "head"),
            P("ctx", "head"),
            P("ctx", "head"),
            P("head", "ctx"),
            P("ctx"),
            P("ctx", "head"),
            P("ctx", "head"),
            P("head", "ctx"),
            P(None, "ctx", None),
        ),
        out_specs=(
            P(None, "ctx", None),
            P(None, "ctx", None),
            P("ctx"),
            P("ctx", "head"),
            P("ctx", "head"),
            P("ctx", "head"),
            P("head", "ctx"),
            P("ctx"),
            P("ctx", "head"),
            P("ctx", "head"),
            P("head", "ctx"),
        ),
        check_vma=False,
    )
```

```python
import functools
import math

import jax
import jax.numpy as jnp
from jax import lax
from jax.experimental import pallas as pl
from jax.experimental.pallas import tpu as pltpu
from jax.sharding import PartitionSpec as P

HQ = 32
HK = 8
HD = 64
GROUP = HQ // HK
RUN = 128

EPSILON = 1e-05
ROPE_BASE = 500000.0
NEGATIVE = -1e30
LOG2E = math.log2(math.e)
SCALE = HD ** (-0.5)
BF = jnp.bfloat16
F32 = jnp.float32

NN = (((1,), (0,)), ((), ()))
NT = (((1,), (1,)), ((), ()))
TN = (((0,), (0,)), ((), ()))


def mm(a, b, dims=NN):
    return lax.dot_general(a, b, dims, preferred_element_type=F32)


def ring_order(n):
    return list(range(0, n, 2)) + list(range(1, n, 2))[::-1]


def ring_step(value, n):
    order = ring_order(n)
    pairs = []
    for p in range(n):
        for h in range(4):
            step = 1 if h % 2 == 0 else -1
            pairs.append((order[p] * 4 + h, order[(p + step) % n] * 4 + h))
    return lax.ppermute(value, ("ctx", "head"), pairs)


def in_turn(value, other):
    return value if other is None else lax.optimization_barrier((value, other))[0]


class Side:
    def __init__(self, hooks):
        self.hooks, self.due = hooks or {}, None

    def arrived(self, got, last):
        due, self.due = self.due, None
        return in_turn(got, last if due is None else (last, due))

    def after(self, step, token):
        if step in self.hooks:
            self.due = self.hooks[step](token)


def ring_gather(chains, n, hooks=None, pieces=None):
    chains, side, last = list(chains), Side(hooks), None
    pieces = [] if pieces is None else pieces
    pieces.append(tuple(chains))
    for step in range(n - 1):
        for j in range(len(chains)):
            got = ring_step(chains[j], n)
            final = j == len(chains) - 1
            last = chains[j] = side.arrived(got, last) if final else in_turn(got, last)
        pieces.append(tuple(chains))
        side.after(step, last)
    return pieces


def ring_scatter(pieces, n, hooks=None, due=None):
    totals, side, last = list(pieces[1 % n]), Side(hooks), None
    side.due = due
    for step, s in enumerate(list(range(2, n)) + [0]):
        for j in range(len(totals)):
            got = ring_step(totals[j], n)
            final = j == len(totals) - 1
            got = side.arrived(got, last) if final else in_turn(got, last)
            last = totals[j] = (got.astype(F32) + pieces[s][j].astype(F32)).astype(BF)
        side.after(step, last)
    return totals


def cut_chains(piece, n):
    count = 2 if n <= 8 else 1
    size = piece.shape[0] // count
    return tuple(piece[j * size : (j + 1) * size] for j in range(count))


def other_core(value):
    return lax.ppermute(value, "head", [(h, h ^ 1) for h in range(4)])


def other_x(value):
    return lax.ppermute(value, "head", [(h, h ^ 2) for h in range(4)])


def part(array, seq, core):
    half = array.shape[1] // 2
    return lax.dynamic_slice(array, (seq, core * half, 0), (1, half, array.shape[2]))[0]


def head_parts(own):
    far = other_x(own)
    near = other_core(jnp.concatenate([own, far], axis=0))
    return own, far, near[: own.shape[0]], near[own.shape[0] :]


def placed(parts, seq, core):
    own, far, near, both = parts
    by_core = lambda a, b: (jnp.where(core == 0, a, b), jnp.where(core == 0, b, a))
    mine, other = by_core(own, near), by_core(far, both)
    first = [jnp.where(seq == 0, a, b) for a, b in zip(mine, other)]
    second = [jnp.where(seq == 0, b, a) for a, b in zip(mine, other)]
    return jnp.stack([jnp.concatenate(first, axis=0), jnp.concatenate(second, axis=0)])


def swap_halves(v):
    lane = lax.broadcasted_iota(jnp.int32, v.shape, 1) % HD
    return jnp.where(lane < HD // 2, pltpu.roll(v, 2 * HD - HD // 2, 1), pltpu.roll(v, HD // 2, 1))


def rotated(v, cos, sin):
    return v * cos + swap_halves(v) * sin


def qkv_kernel(count, index_ref, unit_ref, cos_ref, sin_ref, *refs):
    *pieces, kv_ref, q_ref, w_ref = refs
    lines = pieces[0].shape[0]

    @pl.when(pl.program_id(0) == 0)
    def _():
        for at, piece in enumerate(pieces):
            line = (index_ref[at // count] * count + at % count) * lines
            w_ref[pl.ds(pl.multiple_of(line, lines), lines), :] = piece[...]

    y = mm(unit_ref[0], w_ref[...])
    cos, sin = cos_ref[0], sin_ref[0]
    width = kv_ref.shape[2] // 2
    for j in range(0, width, 2 * HD):
        kv_ref[0, :, j : j + 2 * HD] = rotated(y[:, j : j + 2 * HD], cos, sin).astype(BF)
    kv_ref[0, :, width:] = y[:, width : 2 * width].astype(BF)
    for j in range(0, q_ref.shape[2], 2 * HD):
        at = 2 * width + j
        q_ref[0, :, j : j + 2 * HD] = rotated(y[:, at : at + 2 * HD], cos, sin).astype(BF)


def qkv_call(ring_from, unit, pieces, cos, sin, q_width, kv_width):
    sequences, rows, width = unit.shape
    count = len(pieces[0])
    parts = [part for piece in pieces for part in piece]
    spec = lambda w: pl.BlockSpec((1, rows, w), lambda s: (s, 0, 0))
    whole = lambda shape: pl.BlockSpec(shape, lambda s: (0, 0))
    weight = (width, kv_width + q_width)
    return pl.pallas_call(
        functools.partial(qkv_kernel, count),
        grid=(sequences,),
        in_specs=[
            pl.BlockSpec(memory_space=pltpu.SMEM),
            spec(width),
            spec(2 * HD),
            spec(2 * HD),
        ]
        + [whole(part.shape) for part in parts],
        out_specs=[spec(kv_width), spec(q_width), whole(weight)],
        out_shape=[
            jax.ShapeDtypeStruct((sequences, rows, kv_width), BF),
            jax.ShapeDtypeStruct((sequences, rows, q_width), BF),
            jax.ShapeDtypeStruct(weight, BF),
        ],
        compiler_params=pltpu.CompilerParams(vmem_limit_bytes=60 * 1024 * 1024),
        cost_estimate=pl.CostEstimate(
            flops=2 * sequences * rows * width * weight[1],
            bytes_accessed=weight[0] * weight[1] * 4 + unit.size * 4,
            transcendentals=0,
        ),
        name="qkv",
    )(ring_from, unit, cos, sin, *parts)


def half_mask(v, which):
    lane = lax.broadcasted_iota(jnp.int32, v.shape, 1)
    keep = (lane < HD) if which == 0 else (lane >= HD)
    return jnp.where(keep, v, jnp.zeros_like(v))


def stack_heads(block):
    return jnp.concatenate(
        [block[:, g * 2 * HD : (g + 1) * 2 * HD] for g in range(GROUP)], axis=0
    )


def causal_mask(shape):
    key = lax.broadcasted_iota(jnp.int32, shape, 0)
    query = lax.broadcasted_iota(jnp.int32, shape, 1) % RUN
    return key <= query


def load_runs(pieces, kv_ref):
    rows = pieces[0].shape[0]
    for at, piece in enumerate(pieces):
        for r in range(rows // RUN):
            kv_ref[at * rows // RUN + r] = piece[r * RUN : (r + 1) * RUN]


def attend_kernel(n, sq_ref, sk_ref, q_ref, *refs):
    pieces, refs = refs[:n], refs[n:]
    o_ref, low_ref, lse_ref, kv_ref, s_ref, m_ref, l_ref, acc_ref = refs
    seq, run = pl.program_id(0), pl.program_id(1)
    start = sq_ref[seq, run]

    @pl.when(run == 0)
    def _():
        load_runs(pieces, kv_ref)

    runs = kv_ref.shape[0]
    columns = GROUP * RUN
    queries = stack_heads(q_ref[0])
    q_pair = [half_mask(queries, k) for k in range(2)]
    m_ref[...] = jnp.full_like(m_ref, NEGATIVE)
    l_ref[...] = jnp.zeros_like(l_ref)
    acc_ref[...] = jnp.zeros_like(acc_ref)

    def score_step(i, carry):
        key_start = sk_ref[seq, i]

        def scores(masked):
            keys = kv_ref[i, :, : 2 * HD]
            for k in range(2):
                s = mm(keys, q_pair[k], NT) * (SCALE * LOG2E)
                if masked:
                    s = jnp.where(causal_mask(s.shape), s, NEGATIVE)
                s_ref[k, pl.ds(pl.multiple_of(i * RUN, RUN), RUN), :] = s
                m_ref[k] = jnp.maximum(m_ref[k], jnp.max(s.reshape(-1, 8, columns), axis=0))

        @pl.when(key_start < start)
        def _():
            scores(False)

        @pl.when(key_start == start)
        def _():
            scores(True)

        return carry

    lax.fori_loop(0, runs, score_step, 0)
    peaks = [jnp.max(m_ref[k], axis=0, keepdims=True) for k in range(2)]

    def value_step(i, carry):
        @pl.when(sk_ref[seq, i] <= start)
        def _():
            values = kv_ref[i, :, 2 * HD :]
            for k in range(2):
                p = jnp.exp2(s_ref[k, pl.ds(pl.multiple_of(i * RUN, RUN), RUN), :] - peaks[k])
                l_ref[k] += jnp.sum(p.reshape(-1, 8, columns), axis=0)
                acc_ref[k] += mm(values, p.astype(BF), TN)

        return carry

    lax.fori_loop(0, runs, value_step, 0)
    rows = []
    for k in range(2):
        total = jnp.sum(l_ref[k], axis=0, keepdims=True)
        lse_ref[0, 0, k : k + 1, :] = peaks[k] + jnp.log2(total)
        rows.append(acc_ref[k, k * HD : (k + 1) * HD, :] / total)
    both = jnp.concatenate(rows, axis=0)
    for g in range(GROUP):
        out = both[:, g * RUN : (g + 1) * RUN].T
        o_ref[0, :, g * 2 * HD : (g + 1) * 2 * HD] = out
        low_ref[0, :, g * 2 * HD : (g + 1) * 2 * HD] = out.astype(BF)


def attend_call(starts_q, starts_k, query, pieces):
    sequences, rows, width = query.shape
    n, piece_rows, kv_width = len(pieces), pieces[0].shape[0], pieces[0].shape[1] // sequences
    runs = n * piece_rows // RUN
    columns = GROUP * RUN
    smem = pl.BlockSpec(memory_space=pltpu.SMEM)
    row_spec = pl.BlockSpec((1, RUN, width), lambda s, r: (s, r, 0))
    return pl.pallas_call(
        functools.partial(attend_kernel, n),
        grid=(sequences, rows // RUN),
        in_specs=[
            smem,
            smem,
            row_spec,
        ]
        + [pl.BlockSpec((piece_rows, kv_width), lambda s, r: (0, s))] * n,
        out_specs=[row_spec, row_spec, pl.BlockSpec((1, 1, 2, columns), lambda s, r: (s, r, 0, 0))],
        out_shape=[
            jax.ShapeDtypeStruct((sequences, rows, width), F32),
            jax.ShapeDtypeStruct((sequences, rows, width), BF),
            jax.ShapeDtypeStruct((sequences, rows // RUN, 2, columns), F32),
        ],
        scratch_shapes=[
            pltpu.VMEM((runs, RUN, kv_width), BF),
            pltpu.VMEM((2, runs * RUN, columns), F32),
            pltpu.VMEM((2, 8, columns), F32),
            pltpu.VMEM((2, 8, columns), F32),
            pltpu.VMEM((2, 2 * HD, columns), F32),
        ],
        compiler_params=pltpu.CompilerParams(vmem_limit_bytes=56 * 1024 * 1024),
        cost_estimate=pl.CostEstimate(
            flops=50 * sequences * rows * runs * RUN * width,
            bytes_accessed=n * pieces[0].size * 2 + query.size * 6,
            transcendentals=sequences * rows * runs * RUN * 4,
        ),
        name="attend",
    )(starts_q, starts_k, query, *pieces)


def attend_back_kernel(n, sq_ref, sk_ref, q_ref, do_ref, o_ref, lse_ref, cos_ref, sin_ref, *refs):
    pieces, refs = refs[:n], refs[n:]
    dq_ref, dkv_ref, kv_ref, sum_ref, acc_ref = refs
    seq, run = pl.program_id(0), pl.program_id(1)
    start = sq_ref[seq, run]
    runs = kv_ref.shape[0]
    queries = stack_heads(q_ref[0])
    upstream = stack_heads(do_ref[0])
    attended = stack_heads(o_ref[0])
    q_pair = [half_mask(queries, k) for k in range(2)]
    u_pair = [half_mask(upstream, k) for k in range(2)]
    product = upstream.astype(F32) * attended
    deltas = [
        lax.dot_general(
            half_mask(jnp.ones((8, 2 * HD), F32), k),
            product,
            NT,
            precision=lax.Precision.HIGHEST,
            preferred_element_type=F32,
        )[:1]
        for k in range(2)
    ]
    lses = [lse_ref[0, 0, k : k + 1, :] for k in range(2)]
    acc_ref[...] = jnp.zeros_like(acc_ref)

    @pl.when(run == 0)
    def _():
        load_runs(pieces, kv_ref)
        sum_ref[...] = jnp.zeros_like(sum_ref)

    def step(i, carry):
        key_start = sk_ref[seq, i]

        def work(masked):
            keys = kv_ref[i, :, : 2 * HD]
            values = kv_ref[i, :, 2 * HD :]
            for k in range(2):
                s = mm(keys, q_pair[k], NT) * (SCALE * LOG2E)
                if masked:
                    s = jnp.where(causal_mask(s.shape), s, NEGATIVE)
                p = jnp.exp2(s - lses[k])
                dp = mm(values, u_pair[k], NT)
                ds = (p * (dp - deltas[k])).astype(BF)
                sum_ref[i, :, : 2 * HD] += mm(ds, q_pair[k])
                sum_ref[i, :, 2 * HD :] += mm(p.astype(BF), u_pair[k])
                acc_ref[k] += mm(keys, ds, TN)

        @pl.when(key_start < start)
        def _():
            work(False)

        @pl.when(key_start == start)
        def _():
            work(True)

        return carry

    lax.fori_loop(0, runs, step, 0)
    both = jnp.concatenate([acc_ref[k, k * HD : (k + 1) * HD, :] for k in range(2)], axis=0)
    cos, sin = cos_ref[0], sin_ref[0]
    for g in range(GROUP):
        v = both[:, g * RUN : (g + 1) * RUN].T * SCALE
        dq_ref[0, :, g * 2 * HD : (g + 1) * 2 * HD] = (v * cos - swap_halves(v) * sin).astype(BF)

    @pl.when(run == pl.num_programs(1) - 1)
    def _():
        dkv_ref[:, :, : 2 * HD] = (sum_ref[:, :, : 2 * HD] * SCALE).astype(BF)
        dkv_ref[:, :, 2 * HD :] = sum_ref[:, :, 2 * HD :].astype(BF)


def attend_back_call(starts_q, starts_k, query, upstream, attended, lse, pieces, cos, sin):
    sequences, rows, width = query.shape
    n, piece_rows, kv_width = len(pieces), pieces[0].shape[0], pieces[0].shape[1] // sequences
    runs = n * piece_rows // RUN
    columns = GROUP * RUN
    smem = pl.BlockSpec(memory_space=pltpu.SMEM)
    row_spec = pl.BlockSpec((1, RUN, width), lambda s, r: (s, r, 0))
    table_spec = pl.BlockSpec((1, RUN, 2 * HD), lambda s, r: (s, r, 0))
    kv_spec = pl.BlockSpec((runs, RUN, kv_width), lambda s, r: (0, 0, s))
    return pl.pallas_call(
        functools.partial(attend_back_kernel, n),
        grid=(sequences, rows // RUN),
        in_specs=[
            smem,
            smem,
            row_spec,
            row_spec,
            row_spec,
            pl.BlockSpec((1, 1, 2, columns), lambda s, r: (s, r, 0, 0)),
            table_spec,
            table_spec,
        ]
        + [pl.BlockSpec((piece_rows, kv_width), lambda s, r: (0, s))] * n,
        out_specs=[row_spec, kv_spec],
        out_shape=[
            jax.ShapeDtypeStruct((sequences, rows, width), BF),
            jax.ShapeDtypeStruct((runs, RUN, sequences * kv_width), BF),
        ],
        scratch_shapes=[
            pltpu.VMEM((runs, RUN, kv_width), BF),
            pltpu.VMEM((runs, RUN, 4 * HD), F32),
            pltpu.VMEM((2, 2 * HD, columns), F32),
        ],
        compiler_params=pltpu.CompilerParams(vmem_limit_bytes=56 * 1024 * 1024),
        cost_estimate=pl.CostEstimate(
            flops=80 * sequences * rows * runs * RUN * width,
            bytes_accessed=n * pieces[0].size * 4 + query.size * 10,
            transcendentals=sequences * rows * runs * RUN * 4,
        ),
        name="attend_back",
    )(starts_q, starts_k, query, upstream, attended, lse, cos, sin, *pieces)


def ctx_order_kernel(index_ref, *refs):
    *pieces, o_ref = refs
    count = len(pieces) // o_ref.shape[0]
    rows = pieces[0].shape[0]
    for at, piece in enumerate(pieces):
        line = at % count * rows
        o_ref[index_ref[at // count], line : line + rows, :] = piece[...]


def ctx_order_call(ring_from, pieces):
    n, count = len(pieces), len(pieces[0])
    rows, width = pieces[0][0].shape
    return pl.pallas_call(
        ctx_order_kernel,
        grid=(1,),
        in_specs=[pl.BlockSpec(memory_space=pltpu.SMEM)]
        + [pl.BlockSpec((rows, width), lambda i: (0, 0))] * (n * count),
        out_specs=pl.BlockSpec((n, count * rows, width), lambda i: (0, 0, 0)),
        out_shape=jax.ShapeDtypeStruct((n, count * rows, width), BF),
        compiler_params=pltpu.CompilerParams(vmem_limit_bytes=20 * 1024 * 1024),
        name="ctx_order",
    )(ring_from, *[piece for chains in pieces for piece in chains])


def ring_order_kernel(index_ref, x_ref, o_ref):
    for s in range(o_ref.shape[0]):
        o_ref[s] = x_ref[index_ref[s]]


def ring_order_call(ring_from, blocks):
    return pl.pallas_call(
        ring_order_kernel,
        in_specs=[
            pl.BlockSpec(memory_space=pltpu.SMEM),
            pl.BlockSpec(memory_space=pltpu.VMEM),
        ],
        out_specs=pl.BlockSpec(memory_space=pltpu.VMEM),
        out_shape=jax.ShapeDtypeStruct(blocks.shape, blocks.dtype),
        compiler_params=pltpu.CompilerParams(vmem_limit_bytes=12 * 1024 * 1024),
        name="ring_order",
    )(ring_from, blocks)


def gather_rows_kernel(*refs):
    *pieces, o_ref = refs
    rows = pieces[0].shape[0]
    for at, piece in enumerate(pieces):
        o_ref[at * rows : (at + 1) * rows] = piece[...]


def gather_rows_call(pieces):
    rows, width = pieces[0].shape
    shape = (len(pieces) * rows, width)
    return pl.pallas_call(
        gather_rows_kernel,
        grid=(1,),
        in_specs=[pl.BlockSpec((rows, width), lambda i: (0, 0))] * len(pieces),
        out_specs=pl.BlockSpec(shape, lambda i: (0, 0)),
        out_shape=jax.ShapeDtypeStruct(shape, BF),
        compiler_params=pltpu.CompilerParams(vmem_limit_bytes=16 * 1024 * 1024),
        name="gather_rows",
    )(*pieces)


def finish_kernel(got_ref, w_ref, gain_ref, grad_ref, sum_ref):
    n, rows, chunk = got_ref.shape
    sums = jnp.zeros((rows, 1), F32)
    for t in range(n):
        grad = got_ref[t].astype(F32)
        grad_ref[:, t * chunk : (t + 1) * chunk] = grad * gain_ref[...]
        weight = w_ref[:, t * chunk : (t + 1) * chunk].astype(F32)
        sums += jnp.sum(grad * weight, axis=1, keepdims=True)
    sum_ref[...] = sums


def finish_call(got, weight, gain):
    n, rows, chunk = got.shape
    vmem = pl.BlockSpec(memory_space=pltpu.VMEM)
    return pl.pallas_call(
        finish_kernel,
        in_specs=[vmem] * 3,
        out_specs=[vmem] * 2,
        out_shape=[
            jax.ShapeDtypeStruct((rows, n * chunk), F32),
            jax.ShapeDtypeStruct((rows, 1), F32),
        ],
        compiler_params=pltpu.CompilerParams(vmem_limit_bytes=16 * 1024 * 1024),
        name="finish",
    )(got, weight, gain)


def finish_down_kernel(got_ref, grad_ref):
    n, rows, chunk = got_ref.shape
    for t in range(n):
        grad_ref[t * chunk : (t + 1) * chunk, :] = got_ref[t].astype(F32).T


def finish_down_call(got):
    n, rows, chunk = got.shape
    vmem = pl.BlockSpec(memory_space=pltpu.VMEM)
    return pl.pallas_call(
        finish_down_kernel,
        in_specs=[vmem],
        out_specs=vmem,
        out_shape=jax.ShapeDtypeStruct((n * chunk, rows), F32),
        compiler_params=pltpu.CompilerParams(vmem_limit_bytes=16 * 1024 * 1024),
        name="finish_down",
    )(got)


def rotation_tables(place_rows):
    half = HD // 2
    frequency = jnp.exp(jnp.arange(half, dtype=F32) * (-2.0 * math.log(ROPE_BASE) / HD))
    angles = place_rows.astype(F32)[..., None] * frequency
    cos, sin = jnp.cos(angles), jnp.sin(angles)
    return (
        jnp.concatenate([cos, cos, cos, cos], axis=-1),
        jnp.concatenate([-sin, sin, -sin, sin], axis=-1),
    )


def pair_heads(w):
    return w.reshape(w.shape[0], 2, GROUP, HD).swapaxes(1, 2).reshape(w.shape[0], -1)


def unpair_heads(w):
    return w.reshape(w.shape[0], GROUP, 2, HD).swapaxes(1, 2).reshape(w.shape[0], -1)


def local(
    hidden,
    positions,
    norm_attention,
    w_query,
    w_key,
    w_value,
    w_out,
    norm_feed,
    w_gate,
    w_up,
    w_down,
    cotangent,
    *,
    n,
):
    sequences, rows, width = hidden.shape
    half = rows // 2
    place, head = lax.axis_index("ctx"), lax.axis_index("head")
    seq, core = head // 2, head % 2
    order = jnp.array(ring_order(n), jnp.int32)
    ring_place = jnp.where(place % 2 == 0, place // 2, n - 1 - place // 2)
    step_sign = 1 - 2 * core
    ring_from = order[(ring_place - step_sign * jnp.arange(n, dtype=jnp.int32)) % n]

    gain_a = norm_attention.astype(F32)[:, None]
    gain_f = norm_feed.astype(F32)[:, None]
    q_width, k_width = w_query.shape[1], w_key.shape[1]
    slice_rows = width // n
    side = {}

    def exchange(cut):
        return lax.all_to_all(cut, "ctx", 0, 0, tiled=True)

    def cut_units(w):
        return w.reshape(w.shape[0], n, -1).swapaxes(0, 1)

    def scaled(w):
        return (w.astype(F32) * gain_f).astype(BF)

    def in_halves(array):
        size = array.shape[0] // 2
        return array[:size], array[size:]

    def in_columns(array):
        size = array.shape[1] // 2
        return array[:, :size], array[:, size:]

    def joined(own, near_own, far, token):
        far = jnp.concatenate([in_turn(far[0], token), far[1]], axis=1)
        return jnp.concatenate([own, far, near_own, other_core(far)], axis=1)

    own_qkv = jnp.concatenate([w_key, w_value, pair_heads(w_query)], axis=1)

    def gate_exchange(token):
        side["gate"] = exchange(cut_units(scaled(in_turn(w_gate, token))))

    def norm_work(token):
        rows_in = in_turn(hidden, token).astype(F32)
        inverse = lax.rsqrt(jnp.mean(rows_in * rows_in, axis=-1, keepdims=True) + EPSILON)
        side["unit_a"] = (rows_in * inverse).astype(BF)
        return side["unit_a"]

    qkv_pieces = ring_gather(
        cut_chains((own_qkv.astype(F32) * gain_a).astype(BF), n),
        n,
        {0: gate_exchange, 2: norm_work},
    )
    unit_a = side["unit_a"]
    gate_got = side["gate"]

    own_hidden = part(hidden, seq, core).astype(F32)
    own_cotangent = part(cotangent, seq, core)
    own_positions = lax.dynamic_slice_in_dim(positions, place * rows, rows, 1)
    cos, sin = rotation_tables(own_positions)
    starts = positions[:, ::RUN] // RUN
    starts_q = own_positions[:, ::RUN] // RUN
    key_runs = jnp.stack([ring_from * 2, ring_from * 2 + 1], axis=1).reshape(-1)
    starts_k = jnp.take(starts, key_runs, axis=1)
    key_value, query, qkv_weight = qkv_call(
        ring_from, unit_a, qkv_pieces, cos, sin, q_width, 2 * k_width
    )
    key_value, gate_got = lax.optimization_barrier((key_value, gate_got))
    gate_own = gate_got.reshape(width, -1)
    gate_near = other_core(gate_own)
    gate_far = [other_x(piece) for piece in in_columns(gate_own)]

    def gate_work(token):
        side["gate_weight"] = joined(gate_own, gate_near, gate_far, token)
        return side["gate_weight"]

    def up_down_work(token):
        side["sent"] = jnp.stack(
            [cut_units(scaled(in_turn(w_up, token))), cut_units(w_down.T)], axis=1
        )
        return side["sent"]

    pieces = ring_gather(
        (
            jnp.concatenate([key_value[j] for j in range(sequences)], axis=1),
            pair_heads(w_out.T),
            own_cotangent,
        ),
        n,
        {n - 5: gate_work, n - 3: up_down_work},
    )
    kv = [piece[0] for piece in pieces]
    out_pieces = [piece[1] for piece in pieces]
    cot_pieces = [piece[2] for piece in pieces]
    kv, out_pieces, sent = lax.optimization_barrier((kv, out_pieces, side["sent"]))
    feed_got = exchange(sent)
    attended_full, attended, lse = attend_call(starts_q, starts_k, query, kv)
    out_pieces[0] = in_turn(out_pieces[0], lse)
    out_weight_t = ctx_order_call(ring_from, [(piece,) for piece in out_pieces])
    out_weight_t = out_weight_t.reshape(width, q_width)

    sent_core = jnp.concatenate(
        [part(attended, seq, 1 - core), part(attended, 1 - seq, 1 - core)], axis=0
    )
    got_core = other_core(mm(sent_core, out_weight_t, NT).astype(BF)).astype(F32)
    sum_far = (mm(part(attended, 1 - seq, core), out_weight_t, NT) + got_core[half:]).astype(BF)
    sum_own = mm(part(attended, seq, core), out_weight_t, NT) + got_core[:half]
    cots = []
    for at in range(2):
        some = cot_pieces[at * n // 2 : (at + 1) * n // 2]
        cots.append(gather_rows_call([in_turn(some[0], sum_far)] + some[1:]))
    got_x, cots = lax.optimization_barrier((other_x(sum_far), cots))
    x1 = own_hidden + sum_own + got_x.astype(F32)
    x1, feed_got = lax.optimization_barrier((x1, feed_got))

    inverse_f = lax.rsqrt(jnp.mean(x1 * x1, axis=-1, keepdims=True) + EPSILON)
    unit_f = x1 * inverse_f
    up_own, down_own = [feed_got[:, j].reshape(width, -1) for j in range(2)]
    units = 4 * up_own.shape[1]
    arrived, inputs, slabs, partial = [], [], [], []
    owns = (up_own, down_own)
    nears = [other_core(own) for own in owns]
    fars = [[other_x(piece) for piece in in_columns(own)] for own in owns]

    def up_work(token):
        side["up_weight"] = joined(owns[0], nears[0], fars[0], token)
        return side["up_weight"]

    def down_work(token):
        side["down_weight_t"] = joined(owns[1], nears[1], fars[1], token)
        return side["down_weight_t"]

    feeds = []

    def feed_work(token):
        at = len(feeds) * n // 2
        some = [part for piece in arrived[at : at + n // 2] for part in piece]
        feeds.append(gather_rows_call([in_turn(some[0], token)] + some[1:]))
        return feeds[-1]

    def feed_in(at):
        gate = mm(feeds[at], side["gate_weight"])
        up = mm(feeds[at], side["up_weight"])
        dact = mm(cots[at], side["down_weight_t"])
        inputs.append((feeds[at], feeds[at], cots[at]))
        return gate, up, dact

    def feed_middle(gate, up, dact):
        sigma = jax.nn.sigmoid(gate)
        silu = gate * sigma
        act = (silu * up).astype(BF)
        dgate = (dact * up * sigma * (1.0 + gate * (1.0 - sigma))).astype(BF)
        dup = (dact * silu).astype(BF)
        return dgate, dup, act

    def feed_out(dgate, dup, act):
        e = (mm(dgate, side["gate_weight"], NT) + mm(dup, side["up_weight"], NT)).astype(BF)
        x = mm(act, side["down_weight_t"], NT).astype(BF)
        return [
            (e[j : j + half], x[j : j + half]) for j in range(0, e.shape[0], half)
        ]

    ring_gather(
        cut_chains(unit_f.astype(BF), n),
        n,
        {n - 5: up_work, n - 4: feed_work},
        arrived,
    )
    down_work(arrived[-1][-1])
    feed_work(None)
    for at in range(2):
        slabs.append(feed_middle(*feed_in(at)))
        partial.extend(feed_out(*slabs[at]))

    grads, near = [], []

    def grad_work(token):
        j = len(grads)
        first = mm(inputs[0][j], in_turn(slabs[0][j], token), TN).astype(BF)
        first, slab = lax.optimization_barrier((first, slabs[1][j]))
        second = mm(inputs[1][j], slab, TN)
        grads.append((second + first.astype(F32)).astype(BF))
        return grads[-1]

    def near_work(token):
        grad = grads[len(near)]
        kept, sent = grad[:, : units // 2], grad[:, units // 2 :]
        total = in_turn(kept, token).astype(F32) + other_core(sent).astype(F32)
        near.append(total.astype(BF))
        quarter = units // 4
        for kept, sent in zip(in_halves(near[-1][:, :quarter]), in_halves(near[-1][:, quarter:])):
            if len(near) < 3:
                to_x.append((kept, other_x(sent)))
        return near[-1]

    def x_work(token):
        kept, far = to_x[len(sums_x)]
        total = in_turn(kept, token).astype(F32) + far.astype(F32)
        sums_x.append(total.astype(BF).reshape(n // 2, slice_rows, -1))
        return sums_x[-1]

    to_x, sums_x = [], []
    e_own, x_own = ring_scatter(
        partial,
        n,
        {
            0: grad_work,
            1: lambda token: (near_work(token), grad_work(token)),
            2: lambda token: (near_work(token), grad_work(token)),
            3: lambda token: (near_work(token), x_work(token)),
            4: x_work,
            5: x_work,
        },
        slabs[1] + partial[-1],
    )
    while len(sums_x) < 4:
        x_work(e_own)
    gate_delivered, up_delivered = [jnp.concatenate(sums_x[j : j + 2], axis=0) for j in (0, 2)]
    feed_delivered = exchange(jnp.stack([gate_delivered, up_delivered], axis=1))
    e_feed = e_own.astype(F32)
    mid_grad = own_cotangent.astype(F32) + inverse_f * (
        e_feed - unit_f * jnp.mean(e_feed * unit_f, axis=-1, keepdims=True)
    )

    mid_parts = head_parts(mid_grad.astype(BF))
    down_kept, down_sent = near[2][:, : units // 4], near[2][:, units // 4 :]
    down_far = other_x(in_turn(down_sent, mid_parts[1]))
    unit_rows = unit_a.reshape(sequences * rows, width)
    attended_grad = placed([mm(p, out_weight_t).astype(BF) for p in mid_parts], seq, core)
    dquery, dkv = attend_back_call(
        starts_q, starts_k, query, attended_grad, attended_full, lse, kv, cos, sin
    )
    dquery = dquery.reshape(sequences * rows, -1)
    attended_parts = jnp.concatenate(
        [part(attended, s, c) for c in (core, 1 - core) for s in (seq, 1 - seq)], axis=0
    )
    out_grad_t = mm(jnp.concatenate(mid_parts, axis=0), attended_parts, TN).astype(BF)
    out_grad_t = ring_order_call(ring_from, out_grad_t.reshape(n, slice_rows, q_width))
    dquery, dkv, out_grad_t, feed_delivered, x_own = lax.optimization_barrier(
        (dquery, dkv, out_grad_t, feed_delivered, x_own)
    )
    dkv = dkv.reshape(n, rows, -1)
    x2 = x1 + x_own.astype(F32)

    def down_total(token):
        total = in_turn(down_kept, token).astype(F32) + down_far.astype(F32)
        side["down"] = total.astype(BF).reshape(n, slice_rows, -1)
        return side["down"]

    def down_exchange(token):
        side["down"] = exchange(in_turn(side["down"], token))

    def output_work(token):
        side["output"] = head_parts(in_turn(x2, token).astype(BF))
        return side["output"]

    def output_place(token):
        own, *rest = side["output"]
        side["output"] = placed((in_turn(own, token), *rest), seq, core)
        return side["output"]

    def gate_finish(token):
        side["gate"] = finish_call(in_turn(feed_delivered[:, 0], token), w_gate, gain_f)
        return side["gate"]

    def up_finish(token):
        side["up"] = finish_call(in_turn(feed_delivered[:, 1], token), w_up, gain_f)
        return side["up"]

    dkv_own, out_sum = ring_scatter(
        [(dkv[s], out_grad_t[s]) for s in range(n)],
        n,
        {
            0: down_total,
            1: lambda token: (down_exchange(token), output_work(token))[1],
            3: output_place,
            4: lambda token: (gate_finish(token), side["down"]),
            5: up_finish,
        },
    )
    (gate_grad, gate_sums), (up_grad, up_sums) = side["gate"], side["up"]
    pair_width = 2 * k_width
    dkv_own = jnp.stack(
        [dkv_own[:, j * pair_width : (j + 1) * pair_width] for j in range(sequences)]
    ).astype(F32)
    dkey_rot = dkv_own[:, :, :k_width]
    swapped = jnp.concatenate(
        [
            dkey_rot[:, :, HD // 2 : HD],
            dkey_rot[:, :, : HD // 2],
            dkey_rot[:, :, HD + HD // 2 :],
            dkey_rot[:, :, HD : HD + HD // 2],
        ],
        axis=-1,
    )
    dkey = dkey_rot * cos - swapped * sin
    dkv_low = jnp.concatenate(
        [dkey.astype(BF), dkv_own[:, :, k_width:].astype(BF)], axis=2
    ).reshape(sequences * rows, -1)
    dqkv = jnp.concatenate([dkv_low, dquery], axis=1)
    qkv_grad = mm(unit_rows, dqkv, TN).astype(BF).reshape(n, slice_rows, -1)
    qkv_ring = ring_order_call(ring_from, qkv_grad)

    dqkv_rows = dqkv.reshape(sequences, rows, -1)
    sent_core = jnp.concatenate(
        [part(dqkv_rows, seq, 1 - core), part(dqkv_rows, 1 - seq, 1 - core)], axis=0
    )
    sent_core = in_turn(sent_core, qkv_ring)
    got_core = other_core(mm(sent_core, qkv_weight, NT).astype(BF))
    inverse_a = lax.rsqrt(jnp.mean(own_hidden * own_hidden, axis=-1, keepdims=True) + EPSILON)
    unit_own = own_hidden * inverse_a

    def sum_work(token):
        got = in_turn(got_core, token).astype(F32)
        sum_far = mm(part(dqkv_rows, 1 - seq, core), qkv_weight, NT) + got[half:]
        side["e_own"] = mm(part(dqkv_rows, seq, core), qkv_weight, NT) + got[:half]
        side["e_far"] = other_x(sum_far.astype(BF))
        return side["e_own"]

    def input_work(token):
        e_in = side["e_own"] + in_turn(side["e_far"], token).astype(F32)
        input_grad = mid_grad + inverse_a * (
            e_in - unit_own * jnp.mean(e_in * unit_own, axis=-1, keepdims=True)
        )
        side["input"] = head_parts(input_grad.astype(BF))

    def input_place(token):
        own, *rest = side["input"]
        side["input"] = placed((in_turn(own, token), *rest), seq, core).astype(F32)

    def down_finish(token):
        side["down"] = finish_down_call(in_turn(side["down"], token))
        return side["down"]

    def out_finish(token):
        side["out"] = unpair_heads(in_turn(out_sum, token).astype(F32)).T
        return side["out"]

    qkv_sum = ring_scatter(
        [cut_chains(qkv_ring[s], n) for s in range(n)],
        n,
        {0: sum_work, 1: out_finish, 2: input_work, 3: down_finish, 5: input_place},
    )
    qkv_sum = jnp.concatenate(qkv_sum, axis=0).astype(F32)
    output, input_grad = side["output"], side["input"]
    out_grad, down_grad = side["out"], side["down"]

    feed_sums = gate_sums + up_sums
    attention_sums = jnp.sum(qkv_sum * own_qkv.astype(F32), axis=1, keepdims=True)
    qkv_sum = qkv_sum * gain_a
    kv_grad, query_grad = qkv_sum[:, : 2 * k_width], unpair_heads(qkv_sum[:, 2 * k_width :])
    sums = jnp.concatenate([attention_sums, feed_sums], axis=1).T
    both = lax.ppermute(sums, "head", [(h, h ^ 3) for h in range(4)])
    sums = sums + other_core(sums) + (other_x(sums) + both)

    return (
        output,
        input_grad,
        sums[0],
        query_grad,
        kv_grad[:, :k_width],
        kv_grad[:, k_width:],
        out_grad,
        sums[1],
        gate_grad,
        up_grad,
        down_grad,
    )


def solution(mesh):
    return jax.shard_map(
        functools.partial(local, n=mesh.shape["ctx"]),
        mesh=mesh,
        in_specs=(
            P(None, "ctx", None),
            P(),
            P("ctx"),
            P("ctx", "head"),
            P("ctx", "head"),
            P("ctx", "head"),
            P("head", "ctx"),
            P("ctx"),
            P("ctx", "head"),
            P("ctx", "head"),
            P("head", "ctx"),
            P(None, "ctx", None),
        ),
        out_specs=(
            P(None, "ctx", None),
            P(None, "ctx", None),
            P("ctx"),
            P("ctx", "head"),
            P("ctx", "head"),
            P("ctx", "head"),
            P("head", "ctx"),
            P("ctx"),
            P("ctx", "head"),
            P("ctx", "head"),
            P("head", "ctx"),
        ),
        check_vma=False,
    )
```

```python
import functools
import math

import jax
import jax.numpy as jnp
from jax import lax
from jax.experimental import pallas as pl
from jax.experimental.pallas import tpu as pltpu
from jax.sharding import PartitionSpec as P

HQ = 32
HK = 8
HD = 64
GROUP = HQ // HK
RUN = 128

EPSILON = 1e-05
ROPE_BASE = 500000.0
NEGATIVE = -1e30
LOG2E = math.log2(math.e)
SCALE = HD ** (-0.5)
BF = jnp.bfloat16
F32 = jnp.float32

NN = (((1,), (0,)), ((), ()))
NT = (((1,), (1,)), ((), ()))
TN = (((0,), (0,)), ((), ()))


def mm(a, b, dims=NN):
    return lax.dot_general(a, b, dims, preferred_element_type=F32)


def ring_order(n):
    return list(range(0, n, 2)) + list(range(1, n, 2))[::-1]


def ring_step(value, n):
    order = ring_order(n)
    pairs = []
    for p in range(n):
        for h in range(4):
            step = 1 if h % 2 == 0 else -1
            pairs.append((order[p] * 4 + h, order[(p + step) % n] * 4 + h))
    return lax.ppermute(value, ("ctx", "head"), pairs)


def in_turn(value, other):
    return value if other is None else lax.optimization_barrier((value, other))[0]


class Side:
    def __init__(self, hooks):
        self.hooks, self.due = hooks or {}, None

    def arrived(self, got, last):
        due, self.due = self.due, None
        return in_turn(got, last if due is None else (last, due))

    def after(self, step, token):
        if step in self.hooks:
            self.due = self.hooks[step](token)


def ring_gather(chains, n, hooks=None, pieces=None):
    chains, side, last = list(chains), Side(hooks), None
    pieces = [] if pieces is None else pieces
    pieces.append(tuple(chains))
    for step in range(n - 1):
        for j in range(len(chains)):
            got = ring_step(chains[j], n)
            final = j == len(chains) - 1
            last = chains[j] = side.arrived(got, last) if final else in_turn(got, last)
        pieces.append(tuple(chains))
        side.after(step, last)
    return pieces


def ring_scatter(pieces, n, hooks=None, due=None):
    totals, side, last = list(pieces[1 % n]), Side(hooks), None
    side.due = due
    for step, s in enumerate(list(range(2, n)) + [0]):
        for j in range(len(totals)):
            got = ring_step(totals[j], n)
            final = j == len(totals) - 1
            got = side.arrived(got, last) if final else in_turn(got, last)
            last = totals[j] = (got.astype(F32) + pieces[s][j].astype(F32)).astype(BF)
        side.after(step, last)
    return totals


def cut_chains(piece, n):
    count = 2 if n <= 8 else 1
    size = piece.shape[0] // count
    return tuple(piece[j * size : (j + 1) * size] for j in range(count))


def other_core(value):
    return lax.ppermute(value, "head", [(h, h ^ 1) for h in range(4)])


def other_x(value):
    return lax.ppermute(value, "head", [(h, h ^ 2) for h in range(4)])


def part(array, seq, core):
    half = array.shape[1] // 2
    return lax.dynamic_slice(array, (seq, core * half, 0), (1, half, array.shape[2]))[0]


def head_parts(own):
    far = other_x(own)
    near = other_core(jnp.concatenate([own, far], axis=0))
    return own, far, near[: own.shape[0]], near[own.shape[0] :]


def placed(parts, seq, core):
    own, far, near, both = parts
    by_core = lambda a, b: (jnp.where(core == 0, a, b), jnp.where(core == 0, b, a))
    mine, other = by_core(own, near), by_core(far, both)
    first = [jnp.where(seq == 0, a, b) for a, b in zip(mine, other)]
    second = [jnp.where(seq == 0, b, a) for a, b in zip(mine, other)]
    return jnp.stack([jnp.concatenate(first, axis=0), jnp.concatenate(second, axis=0)])


def swap_halves(v):
    lane = lax.broadcasted_iota(jnp.int32, v.shape, 1) % HD
    return jnp.where(lane < HD // 2, pltpu.roll(v, 2 * HD - HD // 2, 1), pltpu.roll(v, HD // 2, 1))


def rotated(v, cos, sin):
    return v * cos + swap_halves(v) * sin


def qkv_kernel(count, index_ref, unit_ref, cos_ref, sin_ref, *refs):
    *pieces, kv_ref, q_ref, w_ref = refs
    lines = pieces[0].shape[0]

    @pl.when(pl.program_id(0) == 0)
    def _():
        for at, piece in enumerate(pieces):
            line = (index_ref[at // count] * count + at % count) * lines
            w_ref[pl.ds(pl.multiple_of(line, lines), lines), :] = piece[...]

    y = mm(unit_ref[0], w_ref[...])
    cos, sin = cos_ref[0], sin_ref[0]
    width = kv_ref.shape[2] // 2
    for j in range(0, width, 2 * HD):
        kv_ref[0, :, j : j + 2 * HD] = rotated(y[:, j : j + 2 * HD], cos, sin).astype(BF)
    kv_ref[0, :, width:] = y[:, width : 2 * width].astype(BF)
    for j in range(0, q_ref.shape[2], 2 * HD):
        at = 2 * width + j
        q_ref[0, :, j : j + 2 * HD] = rotated(y[:, at : at + 2 * HD], cos, sin).astype(BF)


def qkv_call(ring_from, unit, pieces, cos, sin, q_width, kv_width):
    sequences, rows, width = unit.shape
    count = len(pieces[0])
    parts = [part for piece in pieces for part in piece]
    spec = lambda w: pl.BlockSpec((1, rows, w), lambda s: (s, 0, 0))
    whole = lambda shape: pl.BlockSpec(shape, lambda s: (0, 0))
    weight = (width, kv_width + q_width)
    return pl.pallas_call(
        functools.partial(qkv_kernel, count),
        grid=(sequences,),
        in_specs=[
            pl.BlockSpec(memory_space=pltpu.SMEM),
            spec(width),
            spec(2 * HD),
            spec(2 * HD),
        ]
        + [whole(part.shape) for part in parts],
        out_specs=[spec(kv_width), spec(q_width), whole(weight)],
        out_shape=[
            jax.ShapeDtypeStruct((sequences, rows, kv_width), BF),
            jax.ShapeDtypeStruct((sequences, rows, q_width), BF),
            jax.ShapeDtypeStruct(weight, BF),
        ],
        compiler_params=pltpu.CompilerParams(vmem_limit_bytes=60 * 1024 * 1024),
        cost_estimate=pl.CostEstimate(
            flops=2 * sequences * rows * width * weight[1],
            bytes_accessed=weight[0] * weight[1] * 4 + unit.size * 4,
            transcendentals=0,
        ),
        name="qkv",
    )(ring_from, unit, cos, sin, *parts)


def half_mask(v, which):
    lane = lax.broadcasted_iota(jnp.int32, v.shape, 1)
    keep = (lane < HD) if which == 0 else (lane >= HD)
    return jnp.where(keep, v, jnp.zeros_like(v))


def stack_heads(block):
    return jnp.concatenate(
        [block[:, g * 2 * HD : (g + 1) * 2 * HD] for g in range(GROUP)], axis=0
    )


def causal_mask(shape):
    key = lax.broadcasted_iota(jnp.int32, shape, 0)
    query = lax.broadcasted_iota(jnp.int32, shape, 1) % RUN
    return key <= query


def load_runs(pieces, kv_ref):
    rows = pieces[0].shape[0]
    for at, piece in enumerate(pieces):
        for r in range(rows // RUN):
            kv_ref[at * rows // RUN + r] = piece[r * RUN : (r + 1) * RUN]


def attend_kernel(n, sq_ref, sk_ref, q_ref, *refs):
    pieces, refs = refs[:n], refs[n:]
    o_ref, low_ref, lse_ref, kv_ref, s_ref, m_ref, l_ref, acc_ref = refs
    seq, run = pl.program_id(0), pl.program_id(1)
    start = sq_ref[seq, run]

    @pl.when(run == 0)
    def _():
        load_runs(pieces, kv_ref)

    runs = kv_ref.shape[0]
    columns = GROUP * RUN
    queries = stack_heads(q_ref[0])
    q_pair = [half_mask(queries, k) for k in range(2)]
    m_ref[...] = jnp.full_like(m_ref, NEGATIVE)
    l_ref[...] = jnp.zeros_like(l_ref)
    acc_ref[...] = jnp.zeros_like(acc_ref)

    def score_step(i, carry):
        key_start = sk_ref[seq, i]

        def scores(masked):
            keys = kv_ref[i, :, : 2 * HD]
            for k in range(2):
                s = mm(keys, q_pair[k], NT) * (SCALE * LOG2E)
                if masked:
                    s = jnp.where(causal_mask(s.shape), s, NEGATIVE)
                s_ref[k, pl.ds(pl.multiple_of(i * RUN, RUN), RUN), :] = s
                m_ref[k] = jnp.maximum(m_ref[k], jnp.max(s.reshape(-1, 8, columns), axis=0))

        @pl.when(key_start < start)
        def _():
            scores(False)

        @pl.when(key_start == start)
        def _():
            scores(True)

        return carry

    lax.fori_loop(0, runs, score_step, 0)
    peaks = [jnp.max(m_ref[k], axis=0, keepdims=True) for k in range(2)]

    def value_step(i, carry):
        @pl.when(sk_ref[seq, i] <= start)
        def _():
            values = kv_ref[i, :, 2 * HD :]
            for k in range(2):
                p = jnp.exp2(s_ref[k, pl.ds(pl.multiple_of(i * RUN, RUN), RUN), :] - peaks[k])
                l_ref[k] += jnp.sum(p.reshape(-1, 8, columns), axis=0)
                acc_ref[k] += mm(values, p.astype(BF), TN)

        return carry

    lax.fori_loop(0, runs, value_step, 0)
    rows = []
    for k in range(2):
        total = jnp.sum(l_ref[k], axis=0, keepdims=True)
        lse_ref[0, 0, k : k + 1, :] = peaks[k] + jnp.log2(total)
        rows.append(acc_ref[k, k * HD : (k + 1) * HD, :] / total)
    both = jnp.concatenate(rows, axis=0)
    for g in range(GROUP):
        out = both[:, g * RUN : (g + 1) * RUN].T
        o_ref[0, :, g * 2 * HD : (g + 1) * 2 * HD] = out
        low_ref[0, :, g * 2 * HD : (g + 1) * 2 * HD] = out.astype(BF)


def attend_call(starts_q, starts_k, query, pieces):
    sequences, rows, width = query.shape
    n, piece_rows, kv_width = len(pieces), pieces[0].shape[0], pieces[0].shape[1] // sequences
    runs = n * piece_rows // RUN
    columns = GROUP * RUN
    smem = pl.BlockSpec(memory_space=pltpu.SMEM)
    row_spec = pl.BlockSpec((1, RUN, width), lambda s, r: (s, r, 0))
    return pl.pallas_call(
        functools.partial(attend_kernel, n),
        grid=(sequences, rows // RUN),
        in_specs=[
            smem,
            smem,
            row_spec,
        ]
        + [pl.BlockSpec((piece_rows, kv_width), lambda s, r: (0, s))] * n,
        out_specs=[row_spec, row_spec, pl.BlockSpec((1, 1, 2, columns), lambda s, r: (s, r, 0, 0))],
        out_shape=[
            jax.ShapeDtypeStruct((sequences, rows, width), F32),
            jax.ShapeDtypeStruct((sequences, rows, width), BF),
            jax.ShapeDtypeStruct((sequences, rows // RUN, 2, columns), F32),
        ],
        scratch_shapes=[
            pltpu.VMEM((runs, RUN, kv_width), BF),
            pltpu.VMEM((2, runs * RUN, columns), F32),
            pltpu.VMEM((2, 8, columns), F32),
            pltpu.VMEM((2, 8, columns), F32),
            pltpu.VMEM((2, 2 * HD, columns), F32),
        ],
        compiler_params=pltpu.CompilerParams(vmem_limit_bytes=56 * 1024 * 1024),
        cost_estimate=pl.CostEstimate(
            flops=50 * sequences * rows * runs * RUN * width,
            bytes_accessed=n * pieces[0].size * 2 + query.size * 6,
            transcendentals=sequences * rows * runs * RUN * 4,
        ),
        name="attend",
    )(starts_q, starts_k, query, *pieces)


def attend_back_kernel(n, sq_ref, sk_ref, q_ref, do_ref, o_ref, lse_ref, cos_ref, sin_ref, *refs):
    pieces, refs = refs[:n], refs[n:]
    dq_ref, dkv_ref, kv_ref, sum_ref, acc_ref = refs
    seq, run = pl.program_id(0), pl.program_id(1)
    start = sq_ref[seq, run]
    runs = kv_ref.shape[0]
    queries = stack_heads(q_ref[0])
    upstream = stack_heads(do_ref[0])
    attended = stack_heads(o_ref[0])
    q_pair = [half_mask(queries, k) for k in range(2)]
    u_pair = [half_mask(upstream, k) for k in range(2)]
    product = upstream.astype(F32) * attended
    deltas = [
        lax.dot_general(
            half_mask(jnp.ones((8, 2 * HD), F32), k),
            product,
            NT,
            precision=lax.Precision.HIGHEST,
            preferred_element_type=F32,
        )[:1]
        for k in range(2)
    ]
    lses = [lse_ref[0, 0, k : k + 1, :] for k in range(2)]
    acc_ref[...] = jnp.zeros_like(acc_ref)

    @pl.when(run == 0)
    def _():
        load_runs(pieces, kv_ref)
        sum_ref[...] = jnp.zeros_like(sum_ref)

    def step(i, carry):
        key_start = sk_ref[seq, i]

        def work(masked):
            keys = kv_ref[i, :, : 2 * HD]
            values = kv_ref[i, :, 2 * HD :]
            for k in range(2):
                s = mm(keys, q_pair[k], NT) * (SCALE * LOG2E)
                if masked:
                    s = jnp.where(causal_mask(s.shape), s, NEGATIVE)
                p = jnp.exp2(s - lses[k])
                dp = mm(values, u_pair[k], NT)
                ds = (p * (dp - deltas[k])).astype(BF)
                sum_ref[i, :, : 2 * HD] += mm(ds, q_pair[k])
                sum_ref[i, :, 2 * HD :] += mm(p.astype(BF), u_pair[k])
                acc_ref[k] += mm(keys, ds, TN)

        @pl.when(key_start < start)
        def _():
            work(False)

        @pl.when(key_start == start)
        def _():
            work(True)

        return carry

    lax.fori_loop(0, runs, step, 0)
    both = jnp.concatenate([acc_ref[k, k * HD : (k + 1) * HD, :] for k in range(2)], axis=0)
    cos, sin = cos_ref[0], sin_ref[0]
    for g in range(GROUP):
        v = both[:, g * RUN : (g + 1) * RUN].T * SCALE
        dq_ref[0, :, g * 2 * HD : (g + 1) * 2 * HD] = (v * cos - swap_halves(v) * sin).astype(BF)

    @pl.when(run == pl.num_programs(1) - 1)
    def _():
        dkv_ref[:, :, : 2 * HD] = (sum_ref[:, :, : 2 * HD] * SCALE).astype(BF)
        dkv_ref[:, :, 2 * HD :] = sum_ref[:, :, 2 * HD :].astype(BF)


def attend_back_call(starts_q, starts_k, query, upstream, attended, lse, pieces, cos, sin):
    sequences, rows, width = query.shape
    n, piece_rows, kv_width = len(pieces), pieces[0].shape[0], pieces[0].shape[1] // sequences
    runs = n * piece_rows // RUN
    columns = GROUP * RUN
    smem = pl.BlockSpec(memory_space=pltpu.SMEM)
    row_spec = pl.BlockSpec((1, RUN, width), lambda s, r: (s, r, 0))
    table_spec = pl.BlockSpec((1, RUN, 2 * HD), lambda s, r: (s, r, 0))
    kv_spec = pl.BlockSpec((runs, RUN, kv_width), lambda s, r: (0, 0, s))
    return pl.pallas_call(
        functools.partial(attend_back_kernel, n),
        grid=(sequences, rows // RUN),
        in_specs=[
            smem,
            smem,
            row_spec,
            row_spec,
            row_spec,
            pl.BlockSpec((1, 1, 2, columns), lambda s, r: (s, r, 0, 0)),
            table_spec,
            table_spec,
        ]
        + [pl.BlockSpec((piece_rows, kv_width), lambda s, r: (0, s))] * n,
        out_specs=[row_spec, kv_spec],
        out_shape=[
            jax.ShapeDtypeStruct((sequences, rows, width), BF),
            jax.ShapeDtypeStruct((runs, RUN, sequences * kv_width), BF),
        ],
        scratch_shapes=[
            pltpu.VMEM((runs, RUN, kv_width), BF),
            pltpu.VMEM((runs, RUN, 4 * HD), F32),
            pltpu.VMEM((2, 2 * HD, columns), F32),
        ],
        compiler_params=pltpu.CompilerParams(vmem_limit_bytes=56 * 1024 * 1024),
        cost_estimate=pl.CostEstimate(
            flops=80 * sequences * rows * runs * RUN * width,
            bytes_accessed=n * pieces[0].size * 4 + query.size * 10,
            transcendentals=sequences * rows * runs * RUN * 4,
        ),
        name="attend_back",
    )(starts_q, starts_k, query, upstream, attended, lse, cos, sin, *pieces)


def ctx_order_kernel(index_ref, *refs):
    *pieces, o_ref = refs
    count = len(pieces) // o_ref.shape[0]
    rows = pieces[0].shape[0]
    for at, piece in enumerate(pieces):
        line = at % count * rows
        o_ref[index_ref[at // count], line : line + rows, :] = piece[...]


def ctx_order_call(ring_from, pieces):
    n, count = len(pieces), len(pieces[0])
    rows, width = pieces[0][0].shape
    return pl.pallas_call(
        ctx_order_kernel,
        grid=(1,),
        in_specs=[pl.BlockSpec(memory_space=pltpu.SMEM)]
        + [pl.BlockSpec((rows, width), lambda i: (0, 0))] * (n * count),
        out_specs=pl.BlockSpec((n, count * rows, width), lambda i: (0, 0, 0)),
        out_shape=jax.ShapeDtypeStruct((n, count * rows, width), BF),
        compiler_params=pltpu.CompilerParams(vmem_limit_bytes=60 * 1024 * 1024),
        name="ctx_order",
    )(ring_from, *[piece for chains in pieces for piece in chains])


def ring_order_kernel(index_ref, x_ref, o_ref):
    for s in range(o_ref.shape[0]):
        o_ref[s] = x_ref[index_ref[s]]


def ring_order_call(ring_from, blocks):
    return pl.pallas_call(
        ring_order_kernel,
        in_specs=[
            pl.BlockSpec(memory_space=pltpu.SMEM),
            pl.BlockSpec(memory_space=pltpu.VMEM),
        ],
        out_specs=pl.BlockSpec(memory_space=pltpu.VMEM),
        out_shape=jax.ShapeDtypeStruct(blocks.shape, blocks.dtype),
        compiler_params=pltpu.CompilerParams(vmem_limit_bytes=12 * 1024 * 1024),
        name="ring_order",
    )(ring_from, blocks)


def gather_rows_kernel(*refs):
    *pieces, o_ref = refs
    rows = pieces[0].shape[0]
    for at, piece in enumerate(pieces):
        o_ref[at * rows : (at + 1) * rows] = piece[...]


def gather_rows_call(pieces):
    rows, width = pieces[0].shape
    shape = (len(pieces) * rows, width)
    return pl.pallas_call(
        gather_rows_kernel,
        grid=(1,),
        in_specs=[pl.BlockSpec((rows, width), lambda i: (0, 0))] * len(pieces),
        out_specs=pl.BlockSpec(shape, lambda i: (0, 0)),
        out_shape=jax.ShapeDtypeStruct(shape, BF),
        compiler_params=pltpu.CompilerParams(vmem_limit_bytes=16 * 1024 * 1024),
        name="gather_rows",
    )(*pieces)


def cut_kernel(chunk, gain_ref, *refs):
    *weights, o_ref = refs
    n = o_ref.shape[-3]
    for j, w_ref in enumerate(weights):
        for t in range(n):
            if w_ref.shape[0] == o_ref.shape[-2]:
                piece = w_ref[:, t * chunk : (t + 1) * chunk].astype(F32) * gain_ref[...]
            else:
                piece = w_ref[t * chunk : (t + 1) * chunk, :].astype(F32).T
            if len(o_ref.shape) == 4:
                o_ref[j, t] = piece.astype(BF)
            else:
                o_ref[t] = piece.astype(BF)


def cut_call(gain, weights, n):
    rows = gain.shape[0]
    chunk = weights[0].shape[1] // n
    shape = (n, rows, chunk) if len(weights) == 1 else (len(weights), n, rows, chunk)
    whole = lambda shape: pl.BlockSpec(shape, lambda i: (0,) * len(shape))
    return pl.pallas_call(
        functools.partial(cut_kernel, chunk),
        grid=(1,),
        in_specs=[whole(gain.shape)] + [whole(w.shape) for w in weights],
        out_specs=whole(shape),
        out_shape=jax.ShapeDtypeStruct(shape, BF),
        compiler_params=pltpu.CompilerParams(vmem_limit_bytes=16 * 1024 * 1024),
        name="cut",
    )(gain, *weights)


def finish_kernel(got_ref, w_ref, gain_ref, grad_ref, sum_ref):
    n, rows, chunk = got_ref.shape
    sums = jnp.zeros((rows, 1), F32)
    for t in range(n):
        grad = got_ref[t].astype(F32)
        grad_ref[:, t * chunk : (t + 1) * chunk] = grad * gain_ref[...]
        weight = w_ref[:, t * chunk : (t + 1) * chunk].astype(F32)
        sums += jnp.sum(grad * weight, axis=1, keepdims=True)
    sum_ref[...] = sums


def finish_call(got, weight, gain):
    n, rows, chunk = got.shape
    vmem = pl.BlockSpec(memory_space=pltpu.VMEM)
    return pl.pallas_call(
        finish_kernel,
        in_specs=[vmem] * 3,
        out_specs=[vmem] * 2,
        out_shape=[
            jax.ShapeDtypeStruct((rows, n * chunk), F32),
            jax.ShapeDtypeStruct((rows, 1), F32),
        ],
        compiler_params=pltpu.CompilerParams(vmem_limit_bytes=16 * 1024 * 1024),
        name="finish",
    )(got, weight, gain)


def finish_down_kernel(got_ref, grad_ref):
    n, rows, chunk = got_ref.shape
    for t in range(n):
        grad_ref[t * chunk : (t + 1) * chunk, :] = got_ref[t].astype(F32).T


def finish_down_call(got):
    n, rows, chunk = got.shape
    vmem = pl.BlockSpec(memory_space=pltpu.VMEM)
    return pl.pallas_call(
        finish_down_kernel,
        in_specs=[vmem],
        out_specs=vmem,
        out_shape=jax.ShapeDtypeStruct((n * chunk, rows), F32),
        compiler_params=pltpu.CompilerParams(vmem_limit_bytes=16 * 1024 * 1024),
        name="finish_down",
    )(got)


def rotation_tables(place_rows):
    half = HD // 2
    frequency = jnp.exp(jnp.arange(half, dtype=F32) * (-2.0 * math.log(ROPE_BASE) / HD))
    angles = place_rows.astype(F32)[..., None] * frequency
    cos, sin = jnp.cos(angles), jnp.sin(angles)
    return (
        jnp.concatenate([cos, cos, cos, cos], axis=-1),
        jnp.concatenate([-sin, sin, -sin, sin], axis=-1),
    )


def pair_heads(w):
    return w.reshape(w.shape[0], 2, GROUP, HD).swapaxes(1, 2).reshape(w.shape[0], -1)


def unpair_heads(w):
    return w.reshape(w.shape[0], GROUP, 2, HD).swapaxes(1, 2).reshape(w.shape[0], -1)


def local(
    hidden,
    positions,
    norm_attention,
    w_query,
    w_key,
    w_value,
    w_out,
    norm_feed,
    w_gate,
    w_up,
    w_down,
    cotangent,
    *,
    n,
):
    sequences, rows, width = hidden.shape
    half = rows // 2
    place, head = lax.axis_index("ctx"), lax.axis_index("head")
    seq, core = head // 2, head % 2
    order = jnp.array(ring_order(n), jnp.int32)
    ring_place = jnp.where(place % 2 == 0, place // 2, n - 1 - place // 2)
    step_sign = 1 - 2 * core
    ring_from = order[(ring_place - step_sign * jnp.arange(n, dtype=jnp.int32)) % n]

    gain_a = norm_attention.astype(F32)[:, None]
    gain_f = norm_feed.astype(F32)[:, None]
    q_width, k_width = w_query.shape[1], w_key.shape[1]
    slice_rows = width // n
    side = {}

    def exchange(cut, axis=0):
        return lax.all_to_all(cut, "ctx", axis, axis, tiled=True)

    def in_halves(array):
        size = array.shape[0] // 2
        return array[:size], array[size:]

    def in_columns(array):
        size = array.shape[1] // 2
        return array[:, :size], array[:, size:]

    def joined(own, near_own, far, token):
        far = jnp.concatenate([in_turn(far[0], token), far[1]], axis=0)
        return jnp.concatenate([own, far, near_own, other_core(far)], axis=1)

    own_qkv = jnp.concatenate([w_key, w_value, pair_heads(w_query)], axis=1)

    def gate_exchange(token):
        side["gate"] = exchange(cut_call(gain_f, [in_turn(w_gate, token)], n))

    def norm_work(token):
        rows_in = in_turn(hidden, token).astype(F32)
        inverse = lax.rsqrt(jnp.mean(rows_in * rows_in, axis=-1, keepdims=True) + EPSILON)
        side["unit_a"] = (rows_in * inverse).astype(BF)
        return side["unit_a"]

    qkv_pieces = ring_gather(
        cut_chains((own_qkv.astype(F32) * gain_a).astype(BF), n),
        n,
        {0: gate_exchange, 2: norm_work},
    )
    unit_a = side["unit_a"]
    gate_got = side["gate"]

    own_hidden = part(hidden, seq, core).astype(F32)
    own_cotangent = part(cotangent, seq, core)
    own_positions = lax.dynamic_slice_in_dim(positions, place * rows, rows, 1)
    cos, sin = rotation_tables(own_positions)
    starts = positions[:, ::RUN] // RUN
    starts_q = own_positions[:, ::RUN] // RUN
    key_runs = jnp.stack([ring_from * 2, ring_from * 2 + 1], axis=1).reshape(-1)
    starts_k = jnp.take(starts, key_runs, axis=1)
    key_value, query, qkv_weight = qkv_call(
        ring_from, unit_a, qkv_pieces, cos, sin, q_width, 2 * k_width
    )
    key_value, gate_got = lax.optimization_barrier((key_value, gate_got))
    gate_own = gate_got.reshape(width, -1)
    gate_near = other_core(gate_own)
    gate_far = [other_x(piece) for piece in in_halves(gate_own)]

    def gate_work(token):
        side["gate_weight"] = joined(gate_own, gate_near, gate_far, token)
        return side["gate_weight"]

    def up_down_work(token):
        side["sent"] = cut_call(gain_f, [in_turn(w_up, token), w_down], n)
        return side["sent"]

    pieces = ring_gather(
        (
            jnp.concatenate([key_value[j] for j in range(sequences)], axis=1),
            pair_heads(w_out.T),
            own_cotangent,
        ),
        n,
        {n - 5: gate_work, n - 3: up_down_work},
    )
    kv = [piece[0] for piece in pieces]
    out_pieces = [piece[1] for piece in pieces]
    cot_pieces = [piece[2] for piece in pieces]
    kv, out_pieces, sent = lax.optimization_barrier((kv, out_pieces, side["sent"]))
    feed_got = exchange(sent, 1)
    attended_full, attended, lse = attend_call(starts_q, starts_k, query, kv)
    out_pieces[0] = in_turn(out_pieces[0], lse)
    out_weight_t = ctx_order_call(ring_from, [(piece,) for piece in out_pieces])
    out_weight_t = out_weight_t.reshape(width, q_width)

    sent_core = jnp.concatenate(
        [part(attended, seq, 1 - core), part(attended, 1 - seq, 1 - core)], axis=0
    )
    got_core = other_core(mm(sent_core, out_weight_t, NT).astype(BF)).astype(F32)
    sum_far = (mm(part(attended, 1 - seq, core), out_weight_t, NT) + got_core[half:]).astype(BF)
    sum_own = mm(part(attended, seq, core), out_weight_t, NT) + got_core[:half]
    cots = []
    for at in range(2):
        some = cot_pieces[at * n // 2 : (at + 1) * n // 2]
        cots.append(gather_rows_call([in_turn(some[0], sum_far)] + some[1:]))
    got_x, cots = lax.optimization_barrier((other_x(sum_far), cots))
    x1 = own_hidden + sum_own + got_x.astype(F32)
    x1, feed_got = lax.optimization_barrier((x1, feed_got))

    inverse_f = lax.rsqrt(jnp.mean(x1 * x1, axis=-1, keepdims=True) + EPSILON)
    unit_f = x1 * inverse_f
    up_own, down_own = [feed_got[j].reshape(width, -1) for j in range(2)]
    units = 4 * up_own.shape[1]
    arrived, inputs, slabs, partial = [], [], [], []
    owns = (up_own, down_own)
    nears = [other_core(own) for own in owns]
    fars = [[other_x(piece) for piece in in_halves(own)] for own in owns]

    def up_work(token):
        side["up_weight"] = joined(owns[0], nears[0], fars[0], token)
        return side["up_weight"]

    def down_work(token):
        side["down_weight_t"] = joined(owns[1], nears[1], fars[1], token)
        return side["down_weight_t"]

    feeds = []

    def feed_work(token):
        at = len(feeds) * n // 2
        some = [part for piece in arrived[at : at + n // 2] for part in piece]
        feeds.append(gather_rows_call([in_turn(some[0], token)] + some[1:]))
        return feeds[-1]

    def feed_in(at):
        gate = mm(feeds[at], side["gate_weight"])
        up = mm(feeds[at], side["up_weight"])
        if "down_weight_t" not in side:
            down_work(up)
        dact = mm(cots[at], side["down_weight_t"])
        inputs.append((feeds[at], feeds[at], cots[at]))
        return gate, up, dact

    def feed_middle(gate, up, dact):
        sigma = jax.nn.sigmoid(gate)
        silu = gate * sigma
        act = (silu * up).astype(BF)
        dgate = (dact * up * sigma * (1.0 + gate * (1.0 - sigma))).astype(BF)
        dup = (dact * silu).astype(BF)
        return dgate, dup, act

    def feed_out(dgate, dup, act):
        e = (mm(dgate, side["gate_weight"], NT) + mm(dup, side["up_weight"], NT)).astype(BF)
        x = mm(act, side["down_weight_t"], NT).astype(BF)
        return [
            (e[j : j + half], x[j : j + half]) for j in range(0, e.shape[0], half)
        ]

    ring_gather(
        cut_chains(unit_f.astype(BF), n),
        n,
        {
            0: lambda token: fars[0][0],
            n - 6: lambda token: fars[0][1],
            n - 5: lambda token: (up_work(token), fars[1][0]),
            n - 4: feed_work,
            n - 3: lambda token: fars[1][1],
        },
        arrived,
    )
    feed_work(None)
    for at in range(2):
        slabs.append(feed_middle(*feed_in(at)))
        partial.extend(feed_out(*slabs[at]))

    grads, near = [], []

    def grad_work(token):
        j = len(grads)
        first = mm(inputs[0][j], in_turn(slabs[0][j], token), TN).astype(BF)
        first, slab = lax.optimization_barrier((first, slabs[1][j]))
        second = mm(inputs[1][j], slab, TN)
        grads.append((second + first.astype(F32)).astype(BF))
        return grads[-1]

    def near_work(token):
        grad = grads[len(near)]
        kept, sent = grad[:, : units // 2], grad[:, units // 2 :]
        total = in_turn(kept, token).astype(F32) + other_core(sent).astype(F32)
        near.append(total.astype(BF))
        quarter = units // 4
        if len(near) < 3:
            to_x.append((near[-1][:, :quarter], other_x(near[-1][:, quarter:])))
        return near[-1]

    def x_work(token):
        kept, far = to_x[len(sums_x)]
        total = in_turn(kept, token).astype(F32) + far.astype(F32)
        sums_x.append(total.astype(BF).reshape(n, slice_rows, -1))
        return sums_x[-1]

    to_x, sums_x = [], []
    e_own, x_own = ring_scatter(
        partial,
        n,
        {
            0: grad_work,
            1: lambda token: (near_work(token), grad_work(token)),
            2: lambda token: (near_work(token), grad_work(token)),
            3: near_work,
            4: lambda token: to_x[0][1],
            5: x_work,
        },
        slabs[1] + partial[-1],
    )
    x_work(e_own)
    feed_delivered = exchange(jnp.stack(sums_x), 1)
    e_feed = e_own.astype(F32)
    mid_grad = own_cotangent.astype(F32) + inverse_f * (
        e_feed - unit_f * jnp.mean(e_feed * unit_f, axis=-1, keepdims=True)
    )

    mid_parts = head_parts(mid_grad.astype(BF))
    down_kept, down_sent = near[2][:, : units // 4], near[2][:, units // 4 :]
    down_far = other_x(in_turn(down_sent, mid_parts[1]))
    unit_rows = unit_a.reshape(sequences * rows, width)
    attended_grad = placed([mm(p, out_weight_t).astype(BF) for p in mid_parts], seq, core)
    dquery, dkv = attend_back_call(
        starts_q, starts_k, query, attended_grad, attended_full, lse, kv, cos, sin
    )
    dquery = dquery.reshape(sequences * rows, -1)
    attended_parts = jnp.concatenate(
        [part(attended, s, c) for c in (core, 1 - core) for s in (seq, 1 - seq)], axis=0
    )
    out_grad_t = mm(jnp.concatenate(mid_parts, axis=0), attended_parts, TN).astype(BF)
    out_grad_t = ring_order_call(ring_from, out_grad_t.reshape(n, slice_rows, q_width))
    dquery, dkv, out_grad_t, feed_delivered, x_own = lax.optimization_barrier(
        (dquery, dkv, out_grad_t, feed_delivered, x_own)
    )
    dkv = dkv.reshape(n, rows, -1)
    x2 = x1 + x_own.astype(F32)

    def down_total(token):
        total = in_turn(down_kept, token).astype(F32) + down_far.astype(F32)
        side["down"] = total.astype(BF).reshape(n, slice_rows, -1)
        return side["down"]

    def down_exchange(token):
        side["down"] = exchange(in_turn(side["down"], token))

    def output_work(token):
        side["output"] = head_parts(in_turn(x2, token).astype(BF))
        return side["output"]

    def output_place(token):
        own, *rest = side["output"]
        side["output"] = placed((in_turn(own, token), *rest), seq, core)
        return side["output"]

    def gate_finish(token):
        side["gate"] = finish_call(in_turn(feed_delivered[0], token), w_gate, gain_f)
        return side["gate"]

    def up_finish(token):
        side["up"] = finish_call(in_turn(feed_delivered[1], token), w_up, gain_f)
        return side["up"]

    dkv_own, out_sum = ring_scatter(
        [(dkv[s], out_grad_t[s]) for s in range(n)],
        n,
        {
            0: down_total,
            1: lambda token: (down_exchange(token), output_work(token))[1],
            3: output_place,
            4: lambda token: (gate_finish(token), side["down"]),
            5: up_finish,
        },
    )
    (gate_grad, gate_sums), (up_grad, up_sums) = side["gate"], side["up"]
    pair_width = 2 * k_width
    dkv_own = jnp.stack(
        [dkv_own[:, j * pair_width : (j + 1) * pair_width] for j in range(sequences)]
    ).astype(F32)
    dkey_rot = dkv_own[:, :, :k_width]
    swapped = jnp.concatenate(
        [
            dkey_rot[:, :, HD // 2 : HD],
            dkey_rot[:, :, : HD // 2],
            dkey_rot[:, :, HD + HD // 2 :],
            dkey_rot[:, :, HD : HD + HD // 2],
        ],
        axis=-1,
    )
    dkey = dkey_rot * cos - swapped * sin
    dkv_low = jnp.concatenate(
        [dkey.astype(BF), dkv_own[:, :, k_width:].astype(BF)], axis=2
    ).reshape(sequences * rows, -1)
    dqkv = jnp.concatenate([dkv_low, dquery], axis=1)
    qkv_grad = mm(unit_rows, dqkv, TN).astype(BF).reshape(n, slice_rows, -1)
    qkv_ring = ring_order_call(ring_from, qkv_grad)

    dqkv_rows = dqkv.reshape(sequences, rows, -1)
    sent_core = jnp.concatenate(
        [part(dqkv_rows, seq, 1 - core), part(dqkv_rows, 1 - seq, 1 - core)], axis=0
    )
    sent_core = in_turn(sent_core, qkv_ring)
    got_core = other_core(mm(sent_core, qkv_weight, NT).astype(BF))
    inverse_a = lax.rsqrt(jnp.mean(own_hidden * own_hidden, axis=-1, keepdims=True) + EPSILON)
    unit_own = own_hidden * inverse_a

    def sum_work(token):
        got = in_turn(got_core, token).astype(F32)
        sum_far = mm(part(dqkv_rows, 1 - seq, core), qkv_weight, NT) + got[half:]
        side["e_own"] = mm(part(dqkv_rows, seq, core), qkv_weight, NT) + got[:half]
        side["e_far"] = other_x(sum_far.astype(BF))
        return side["e_own"]

    def input_work(token):
        e_in = side["e_own"] + in_turn(side["e_far"], token).astype(F32)
        input_grad = mid_grad + inverse_a * (
            e_in - unit_own * jnp.mean(e_in * unit_own, axis=-1, keepdims=True)
        )
        side["input"] = head_parts(input_grad.astype(BF))

    def input_place(token):
        own, *rest = side["input"]
        side["input"] = placed((in_turn(own, token), *rest), seq, core).astype(F32)

    def down_finish(token):
        side["down"] = finish_down_call(in_turn(side["down"], token))
        return side["down"]

    def out_finish(token):
        side["out"] = unpair_heads(in_turn(out_sum, token).astype(F32)).T
        return side["out"]

    qkv_sum = ring_scatter(
        [cut_chains(qkv_ring[s], n) for s in range(n)],
        n,
        {0: sum_work, 1: out_finish, 2: input_work, 3: down_finish, 5: input_place},
    )
    qkv_sum = jnp.concatenate(qkv_sum, axis=0).astype(F32)
    output, input_grad = side["output"], side["input"]
    out_grad, down_grad = side["out"], side["down"]

    feed_sums = gate_sums + up_sums
    attention_sums = jnp.sum(qkv_sum * own_qkv.astype(F32), axis=1, keepdims=True)
    qkv_sum = qkv_sum * gain_a
    kv_grad, query_grad = qkv_sum[:, : 2 * k_width], unpair_heads(qkv_sum[:, 2 * k_width :])
    sums = jnp.concatenate([attention_sums, feed_sums], axis=1).T
    both = lax.ppermute(sums, "head", [(h, h ^ 3) for h in range(4)])
    sums = sums + other_core(sums) + (other_x(sums) + both)

    return (
        output,
        input_grad,
        sums[0],
        query_grad,
        kv_grad[:, :k_width],
        kv_grad[:, k_width:],
        out_grad,
        sums[1],
        gate_grad,
        up_grad,
        down_grad,
    )


def solution(mesh):
    return jax.shard_map(
        functools.partial(local, n=mesh.shape["ctx"]),
        mesh=mesh,
        in_specs=(
            P(None, "ctx", None),
            P(),
            P("ctx"),
            P("ctx", "head"),
            P("ctx", "head"),
            P("ctx", "head"),
            P("head", "ctx"),
            P("ctx"),
            P("ctx", "head"),
            P("ctx", "head"),
            P("head", "ctx"),
            P(None, "ctx", None),
        ),
        out_specs=(
            P(None, "ctx", None),
            P(None, "ctx", None),
            P("ctx"),
            P("ctx", "head"),
            P("ctx", "head"),
            P("ctx", "head"),
            P("head", "ctx"),
            P("ctx"),
            P("ctx", "head"),
            P("ctx", "head"),
            P("head", "ctx"),
        ),
        check_vma=False,
    )
```

```python
import functools
import math

import jax
import jax.numpy as jnp
from jax import lax
from jax.experimental import pallas as pl
from jax.experimental.pallas import tpu as pltpu
from jax.sharding import PartitionSpec as P

HQ = 32
HK = 8
HD = 64
GROUP = HQ // HK
RUN = 128

EPSILON = 1e-05
ROPE_BASE = 500000.0
NEGATIVE = -1e30
LOG2E = math.log2(math.e)
SCALE = HD ** (-0.5)
BF = jnp.bfloat16
F32 = jnp.float32

NN = (((1,), (0,)), ((), ()))
NT = (((1,), (1,)), ((), ()))
TN = (((0,), (0,)), ((), ()))


def mm(a, b, dims=NN):
    return lax.dot_general(a, b, dims, preferred_element_type=F32)


def ring_order(n):
    return list(range(0, n, 2)) + list(range(1, n, 2))[::-1]


def ring_step(value, n):
    order = ring_order(n)
    pairs = []
    for p in range(n):
        for h in range(4):
            step = 1 if h % 2 == 0 else -1
            pairs.append((order[p] * 4 + h, order[(p + step) % n] * 4 + h))
    return lax.ppermute(value, ("ctx", "head"), pairs)


def in_turn(value, other):
    return value if other is None else lax.optimization_barrier((value, other))[0]


class Side:
    def __init__(self, hooks):
        self.hooks, self.due = hooks or {}, None

    def arrived(self, got, last):
        due, self.due = self.due, None
        return in_turn(got, last if due is None else (last, due))

    def after(self, step, token):
        if step in self.hooks:
            self.due = self.hooks[step](token)


def ring_gather(chains, n, hooks=None, pieces=None):
    chains, side, last = list(chains), Side(hooks), None
    pieces = [] if pieces is None else pieces
    pieces.append(tuple(chains))
    for step in range(n - 1):
        for j in range(len(chains)):
            got = ring_step(chains[j], n)
            final = j == len(chains) - 1
            last = chains[j] = side.arrived(got, last) if final else in_turn(got, last)
        pieces.append(tuple(chains))
        side.after(step, last)
    return pieces


def ring_scatter(pieces, n, hooks=None, due=None):
    totals, side, last = list(pieces[1 % n]), Side(hooks), None
    side.due = due
    for step, s in enumerate(list(range(2, n)) + [0]):
        for j in range(len(totals)):
            got = ring_step(totals[j], n)
            final = j == len(totals) - 1
            got = side.arrived(got, last) if final else in_turn(got, last)
            last = totals[j] = (got.astype(F32) + pieces[s][j].astype(F32)).astype(BF)
        side.after(step, last)
    return totals


def cut_chains(piece, n):
    count = 2 if n <= 8 else 1
    size = piece.shape[0] // count
    return tuple(piece[j * size : (j + 1) * size] for j in range(count))


def other_core(value):
    return lax.ppermute(value, "head", [(h, h ^ 1) for h in range(4)])


def other_x(value):
    return lax.ppermute(value, "head", [(h, h ^ 2) for h in range(4)])


def part(array, seq, core):
    half = array.shape[1] // 2
    return lax.dynamic_slice(array, (seq, core * half, 0), (1, half, array.shape[2]))[0]


def head_parts(own):
    far = other_x(own)
    near = other_core(jnp.concatenate([own, far], axis=0))
    return own, far, near[: own.shape[0]], near[own.shape[0] :]


def placed(parts, seq, core):
    own, far, near, both = parts
    by_core = lambda a, b: (jnp.where(core == 0, a, b), jnp.where(core == 0, b, a))
    mine, other = by_core(own, near), by_core(far, both)
    first = [jnp.where(seq == 0, a, b) for a, b in zip(mine, other)]
    second = [jnp.where(seq == 0, b, a) for a, b in zip(mine, other)]
    return jnp.stack([jnp.concatenate(first, axis=0), jnp.concatenate(second, axis=0)])


def swap_halves(v):
    lane = lax.broadcasted_iota(jnp.int32, v.shape, 1) % HD
    return jnp.where(lane < HD // 2, pltpu.roll(v, 2 * HD - HD // 2, 1), pltpu.roll(v, HD // 2, 1))


def rotated(v, cos, sin):
    return v * cos + swap_halves(v) * sin


def qkv_kernel(count, index_ref, unit_ref, cos_ref, sin_ref, *refs):
    *pieces, kv_ref, q_ref, w_ref = refs
    lines = pieces[0].shape[0]

    @pl.when(pl.program_id(0) == 0)
    def _():
        for at, piece in enumerate(pieces):
            line = (index_ref[at // count] * count + at % count) * lines
            w_ref[pl.ds(pl.multiple_of(line, lines), lines), :] = piece[...]

    y = mm(unit_ref[0], w_ref[...])
    cos, sin = cos_ref[0], sin_ref[0]
    width = kv_ref.shape[2] // 2
    for j in range(0, width, 2 * HD):
        kv_ref[0, :, j : j + 2 * HD] = rotated(y[:, j : j + 2 * HD], cos, sin).astype(BF)
    kv_ref[0, :, width:] = y[:, width : 2 * width].astype(BF)
    for j in range(0, q_ref.shape[2], 2 * HD):
        at = 2 * width + j
        q_ref[0, :, j : j + 2 * HD] = rotated(y[:, at : at + 2 * HD], cos, sin).astype(BF)


def qkv_call(ring_from, unit, pieces, cos, sin, q_width, kv_width):
    sequences, rows, width = unit.shape
    count = len(pieces[0])
    parts = [part for piece in pieces for part in piece]
    spec = lambda w: pl.BlockSpec((1, rows, w), lambda s: (s, 0, 0))
    whole = lambda shape: pl.BlockSpec(shape, lambda s: (0, 0))
    weight = (width, kv_width + q_width)
    return pl.pallas_call(
        functools.partial(qkv_kernel, count),
        grid=(sequences,),
        in_specs=[
            pl.BlockSpec(memory_space=pltpu.SMEM),
            spec(width),
            spec(2 * HD),
            spec(2 * HD),
        ]
        + [whole(part.shape) for part in parts],
        out_specs=[spec(kv_width), spec(q_width), whole(weight)],
        out_shape=[
            jax.ShapeDtypeStruct((sequences, rows, kv_width), BF),
            jax.ShapeDtypeStruct((sequences, rows, q_width), BF),
            jax.ShapeDtypeStruct(weight, BF),
        ],
        compiler_params=pltpu.CompilerParams(vmem_limit_bytes=60 * 1024 * 1024),
        cost_estimate=pl.CostEstimate(
            flops=2 * sequences * rows * width * weight[1],
            bytes_accessed=weight[0] * weight[1] * 4 + unit.size * 4,
            transcendentals=0,
        ),
        name="qkv",
    )(ring_from, unit, cos, sin, *parts)


def half_mask(v, which):
    lane = lax.broadcasted_iota(jnp.int32, v.shape, 1)
    keep = (lane < HD) if which == 0 else (lane >= HD)
    return jnp.where(keep, v, jnp.zeros_like(v))


def stack_heads(block):
    return jnp.concatenate(
        [block[:, g * 2 * HD : (g + 1) * 2 * HD] for g in range(GROUP)], axis=0
    )


def causal(scores, gap):
    key = lax.broadcasted_iota(jnp.int32, scores.shape, 0)
    query = lax.broadcasted_iota(jnp.int32, scores.shape, 1) % RUN
    return jnp.where(key <= query + gap, scores, NEGATIVE)


def run_pair(kv_ref, slots, at):
    return jnp.concatenate([kv_ref[j, :, at : at + 2 * HD] for j in slots], axis=0)


def load_runs(pieces, kv_ref):
    rows = pieces[0].shape[0]
    for at, piece in enumerate(pieces):
        for r in range(rows // RUN):
            kv_ref[at * rows // RUN + r] = piece[r * RUN : (r + 1) * RUN]


def attend_kernel(n, sq_ref, sk_ref, q_ref, *refs):
    pieces, refs = refs[:n], refs[n:]
    o_ref, low_ref, lse_ref, kv_ref, s_ref, m_ref, l_ref, acc_ref = refs
    seq, run = pl.program_id(0), pl.program_id(1)
    start = sq_ref[seq, run]

    @pl.when(run == 0)
    def _():
        load_runs(pieces, kv_ref)

    runs = kv_ref.shape[0]
    columns = GROUP * RUN
    queries = stack_heads(q_ref[0])
    q_pair = [half_mask(queries, k) for k in range(2)]
    m_ref[...] = jnp.full_like(m_ref, NEGATIVE)
    l_ref[...] = jnp.zeros_like(l_ref)
    acc_ref[...] = jnp.zeros_like(acc_ref)

    def slots_of(i):
        return [sk_ref[seq, 2 * i], sk_ref[seq, 2 * i + 1]]

    def rows_of(i):
        return pl.ds(pl.multiple_of(i * 2 * RUN, 2 * RUN), 2 * RUN)

    def scores(i, masked):
        keys = run_pair(kv_ref, slots_of(i), 0)
        for k in range(2):
            s = mm(keys, q_pair[k], NT) * (SCALE * LOG2E)
            if masked:
                s = causal(s, (start - 2 * i) * RUN)
            s_ref[k, rows_of(i), :] = s
            m_ref[k] = jnp.maximum(m_ref[k], jnp.max(s.reshape(-1, 8, columns), axis=0))

    def score_step(i, carry):
        scores(i, False)
        return carry

    last = start // 2
    lax.fori_loop(0, last, score_step, 0)
    scores(last, True)
    peaks = [jnp.max(m_ref[k], axis=0, keepdims=True) for k in range(2)]

    def value_step(i, carry):
        values = run_pair(kv_ref, slots_of(i), 2 * HD)
        for k in range(2):
            p = jnp.exp2(s_ref[k, rows_of(i), :] - peaks[k])
            l_ref[k] += jnp.sum(p.reshape(-1, 8, columns), axis=0)
            acc_ref[k] += mm(values, p.astype(BF), TN)
        return carry

    lax.fori_loop(0, last + 1, value_step, 0)
    rows = []
    for k in range(2):
        total = jnp.sum(l_ref[k], axis=0, keepdims=True)
        lse_ref[0, 0, k : k + 1, :] = peaks[k] + jnp.log2(total)
        rows.append(acc_ref[k, k * HD : (k + 1) * HD, :] / total)
    both = jnp.concatenate(rows, axis=0)
    for g in range(GROUP):
        out = both[:, g * RUN : (g + 1) * RUN].T
        o_ref[0, :, g * 2 * HD : (g + 1) * 2 * HD] = out
        low_ref[0, :, g * 2 * HD : (g + 1) * 2 * HD] = out.astype(BF)


def attend_call(starts_q, starts_k, query, pieces):
    sequences, rows, width = query.shape
    n, piece_rows, kv_width = len(pieces), pieces[0].shape[0], pieces[0].shape[1] // sequences
    runs = n * piece_rows // RUN
    columns = GROUP * RUN
    smem = pl.BlockSpec(memory_space=pltpu.SMEM)
    row_spec = pl.BlockSpec((1, RUN, width), lambda s, r: (s, r, 0))
    return pl.pallas_call(
        functools.partial(attend_kernel, n),
        grid=(sequences, rows // RUN),
        in_specs=[
            smem,
            smem,
            row_spec,
        ]
        + [pl.BlockSpec((piece_rows, kv_width), lambda s, r: (0, s))] * n,
        out_specs=[row_spec, row_spec, pl.BlockSpec((1, 1, 2, columns), lambda s, r: (s, r, 0, 0))],
        out_shape=[
            jax.ShapeDtypeStruct((sequences, rows, width), F32),
            jax.ShapeDtypeStruct((sequences, rows, width), BF),
            jax.ShapeDtypeStruct((sequences, rows // RUN, 2, columns), F32),
        ],
        scratch_shapes=[
            pltpu.VMEM((runs, RUN, kv_width), BF),
            pltpu.VMEM((2, runs * RUN, columns), F32),
            pltpu.VMEM((2, 8, columns), F32),
            pltpu.VMEM((2, 8, columns), F32),
            pltpu.VMEM((2, 2 * HD, columns), F32),
        ],
        compiler_params=pltpu.CompilerParams(vmem_limit_bytes=56 * 1024 * 1024),
        cost_estimate=pl.CostEstimate(
            flops=50 * sequences * rows * runs * RUN * width,
            bytes_accessed=n * pieces[0].size * 2 + query.size * 6,
            transcendentals=sequences * rows * runs * RUN * 4,
        ),
        name="attend",
    )(starts_q, starts_k, query, *pieces)


def attend_back_kernel(n, sq_ref, sk_ref, q_ref, do_ref, o_ref, lse_ref, cos_ref, sin_ref, *refs):
    pieces, refs = refs[:n], refs[n:]
    dq_ref, dkv_ref, kv_ref, sum_ref, acc_ref = refs
    seq, run = pl.program_id(0), pl.program_id(1)
    start = sq_ref[seq, run]
    runs = kv_ref.shape[0]
    queries = stack_heads(q_ref[0])
    upstream = stack_heads(do_ref[0])
    attended = stack_heads(o_ref[0])
    q_pair = [half_mask(queries, k) for k in range(2)]
    u_pair = [half_mask(upstream, k) for k in range(2)]
    product = upstream.astype(F32) * attended
    deltas = [
        lax.dot_general(
            half_mask(jnp.ones((8, 2 * HD), F32), k),
            product,
            NT,
            precision=lax.Precision.HIGHEST,
            preferred_element_type=F32,
        )[:1]
        for k in range(2)
    ]
    lses = [lse_ref[0, 0, k : k + 1, :] for k in range(2)]
    acc_ref[...] = jnp.zeros_like(acc_ref)

    @pl.when(run == 0)
    def _():
        load_runs(pieces, kv_ref)
        sum_ref[...] = jnp.zeros_like(sum_ref)

    def work(i, masked):
        slots = [sk_ref[seq, 2 * i], sk_ref[seq, 2 * i + 1]]
        keys, values = run_pair(kv_ref, slots, 0), run_pair(kv_ref, slots, 2 * HD)
        dk, dv = 0.0, 0.0
        for k in range(2):
            s = mm(keys, q_pair[k], NT) * (SCALE * LOG2E)
            if masked:
                s = causal(s, (start - 2 * i) * RUN)
            p = jnp.exp2(s - lses[k])
            dp = mm(values, u_pair[k], NT)
            ds = (p * (dp - deltas[k])).astype(BF)
            dk += mm(ds, q_pair[k])
            dv += mm(p.astype(BF), u_pair[k])
            acc_ref[k] += mm(keys, ds, TN)
        for half, j in enumerate(slots):
            sum_ref[j, :, : 2 * HD] += dk[half * RUN : (half + 1) * RUN]
            sum_ref[j, :, 2 * HD :] += dv[half * RUN : (half + 1) * RUN]

    def step(i, carry):
        work(i, False)
        return carry

    lax.fori_loop(0, start // 2, step, 0)
    work(start // 2, True)
    both = jnp.concatenate([acc_ref[k, k * HD : (k + 1) * HD, :] for k in range(2)], axis=0)
    cos, sin = cos_ref[0], sin_ref[0]
    for g in range(GROUP):
        v = both[:, g * RUN : (g + 1) * RUN].T * SCALE
        dq_ref[0, :, g * 2 * HD : (g + 1) * 2 * HD] = (v * cos - swap_halves(v) * sin).astype(BF)

    @pl.when(run == pl.num_programs(1) - 1)
    def _():
        dkv_ref[:, :, : 2 * HD] = (sum_ref[:, :, : 2 * HD] * SCALE).astype(BF)
        dkv_ref[:, :, 2 * HD :] = sum_ref[:, :, 2 * HD :].astype(BF)


def attend_back_call(starts_q, starts_k, query, upstream, attended, lse, pieces, cos, sin):
    sequences, rows, width = query.shape
    n, piece_rows, kv_width = len(pieces), pieces[0].shape[0], pieces[0].shape[1] // sequences
    runs = n * piece_rows // RUN
    columns = GROUP * RUN
    smem = pl.BlockSpec(memory_space=pltpu.SMEM)
    row_spec = pl.BlockSpec((1, RUN, width), lambda s, r: (s, r, 0))
    table_spec = pl.BlockSpec((1, RUN, 2 * HD), lambda s, r: (s, r, 0))
    kv_spec = pl.BlockSpec((runs, RUN, kv_width), lambda s, r: (0, 0, s))
    return pl.pallas_call(
        functools.partial(attend_back_kernel, n),
        grid=(sequences, rows // RUN),
        in_specs=[
            smem,
            smem,
            row_spec,
            row_spec,
            row_spec,
            pl.BlockSpec((1, 1, 2, columns), lambda s, r: (s, r, 0, 0)),
            table_spec,
            table_spec,
        ]
        + [pl.BlockSpec((piece_rows, kv_width), lambda s, r: (0, s))] * n,
        out_specs=[row_spec, kv_spec],
        out_shape=[
            jax.ShapeDtypeStruct((sequences, rows, width), BF),
            jax.ShapeDtypeStruct((runs, RUN, sequences * kv_width), BF),
        ],
        scratch_shapes=[
            pltpu.VMEM((runs, RUN, kv_width), BF),
            pltpu.VMEM((runs, RUN, 4 * HD), F32),
            pltpu.VMEM((2, 2 * HD, columns), F32),
        ],
        compiler_params=pltpu.CompilerParams(vmem_limit_bytes=56 * 1024 * 1024),
        cost_estimate=pl.CostEstimate(
            flops=80 * sequences * rows * runs * RUN * width,
            bytes_accessed=n * pieces[0].size * 4 + query.size * 10,
            transcendentals=sequences * rows * runs * RUN * 4,
        ),
        name="attend_back",
    )(starts_q, starts_k, query, upstream, attended, lse, cos, sin, *pieces)


def ctx_order_kernel(index_ref, *refs):
    *pieces, o_ref = refs
    count = len(pieces) // o_ref.shape[0]
    rows = pieces[0].shape[0]
    for at, piece in enumerate(pieces):
        line = at % count * rows
        o_ref[index_ref[at // count], line : line + rows, :] = piece[...]


def ctx_order_call(ring_from, pieces):
    n, count = len(pieces), len(pieces[0])
    rows, width = pieces[0][0].shape
    return pl.pallas_call(
        ctx_order_kernel,
        grid=(1,),
        in_specs=[pl.BlockSpec(memory_space=pltpu.SMEM)]
        + [pl.BlockSpec((rows, width), lambda i: (0, 0))] * (n * count),
        out_specs=pl.BlockSpec((n, count * rows, width), lambda i: (0, 0, 0)),
        out_shape=jax.ShapeDtypeStruct((n, count * rows, width), BF),
        compiler_params=pltpu.CompilerParams(vmem_limit_bytes=60 * 1024 * 1024),
        name="ctx_order",
    )(ring_from, *[piece for chains in pieces for piece in chains])


def ring_order_kernel(index_ref, x_ref, o_ref):
    for s in range(o_ref.shape[0]):
        o_ref[s] = x_ref[index_ref[s]]


def ring_order_call(ring_from, blocks):
    return pl.pallas_call(
        ring_order_kernel,
        in_specs=[
            pl.BlockSpec(memory_space=pltpu.SMEM),
            pl.BlockSpec(memory_space=pltpu.VMEM),
        ],
        out_specs=pl.BlockSpec(memory_space=pltpu.VMEM),
        out_shape=jax.ShapeDtypeStruct(blocks.shape, blocks.dtype),
        compiler_params=pltpu.CompilerParams(vmem_limit_bytes=12 * 1024 * 1024),
        name="ring_order",
    )(ring_from, blocks)


def gather_rows_kernel(*refs):
    *pieces, o_ref = refs
    rows = pieces[0].shape[0]
    for at, piece in enumerate(pieces):
        o_ref[at * rows : (at + 1) * rows] = piece[...]


def gather_rows_call(pieces):
    rows, width = pieces[0].shape
    shape = (len(pieces) * rows, width)
    return pl.pallas_call(
        gather_rows_kernel,
        grid=(1,),
        in_specs=[pl.BlockSpec((rows, width), lambda i: (0, 0))] * len(pieces),
        out_specs=pl.BlockSpec(shape, lambda i: (0, 0)),
        out_shape=jax.ShapeDtypeStruct(shape, BF),
        compiler_params=pltpu.CompilerParams(vmem_limit_bytes=16 * 1024 * 1024),
        name="gather_rows",
    )(*pieces)


def cut_kernel(chunk, gain_ref, *refs):
    *weights, o_ref = refs
    n = o_ref.shape[-3]
    for j, w_ref in enumerate(weights):
        for t in range(n):
            if w_ref.shape[0] == o_ref.shape[-2]:
                piece = w_ref[:, t * chunk : (t + 1) * chunk].astype(F32) * gain_ref[...]
            else:
                piece = w_ref[t * chunk : (t + 1) * chunk, :].astype(F32).T
            if len(o_ref.shape) == 4:
                o_ref[j, t] = piece.astype(BF)
            else:
                o_ref[t] = piece.astype(BF)


def cut_call(gain, weights, n):
    rows = gain.shape[0]
    chunk = weights[0].shape[1] // n
    shape = (n, rows, chunk) if len(weights) == 1 else (len(weights), n, rows, chunk)
    whole = lambda shape: pl.BlockSpec(shape, lambda i: (0,) * len(shape))
    return pl.pallas_call(
        functools.partial(cut_kernel, chunk),
        grid=(1,),
        in_specs=[whole(gain.shape)] + [whole(w.shape) for w in weights],
        out_specs=whole(shape),
        out_shape=jax.ShapeDtypeStruct(shape, BF),
        compiler_params=pltpu.CompilerParams(vmem_limit_bytes=16 * 1024 * 1024),
        name="cut",
    )(gain, *weights)


def finish_kernel(got_ref, w_ref, gain_ref, grad_ref, sum_ref):
    n, rows, chunk = got_ref.shape
    sums = jnp.zeros((rows, 1), F32)
    for t in range(n):
        grad = got_ref[t].astype(F32)
        grad_ref[:, t * chunk : (t + 1) * chunk] = grad * gain_ref[...]
        weight = w_ref[:, t * chunk : (t + 1) * chunk].astype(F32)
        sums += jnp.sum(grad * weight, axis=1, keepdims=True)
    sum_ref[...] = sums


def finish_call(got, weight, gain):
    n, rows, chunk = got.shape
    vmem = pl.BlockSpec(memory_space=pltpu.VMEM)
    return pl.pallas_call(
        finish_kernel,
        in_specs=[vmem] * 3,
        out_specs=[vmem] * 2,
        out_shape=[
            jax.ShapeDtypeStruct((rows, n * chunk), F32),
            jax.ShapeDtypeStruct((rows, 1), F32),
        ],
        compiler_params=pltpu.CompilerParams(vmem_limit_bytes=16 * 1024 * 1024),
        name="finish",
    )(got, weight, gain)


def finish_down_kernel(got_ref, grad_ref):
    n, rows, chunk = got_ref.shape
    for t in range(n):
        grad_ref[t * chunk : (t + 1) * chunk, :] = got_ref[t].astype(F32).T


def finish_down_call(got):
    n, rows, chunk = got.shape
    vmem = pl.BlockSpec(memory_space=pltpu.VMEM)
    return pl.pallas_call(
        finish_down_kernel,
        in_specs=[vmem],
        out_specs=vmem,
        out_shape=jax.ShapeDtypeStruct((n * chunk, rows), F32),
        compiler_params=pltpu.CompilerParams(vmem_limit_bytes=16 * 1024 * 1024),
        name="finish_down",
    )(got)


def rotation_tables(place_rows):
    half = HD // 2
    frequency = jnp.exp(jnp.arange(half, dtype=F32) * (-2.0 * math.log(ROPE_BASE) / HD))
    angles = place_rows.astype(F32)[..., None] * frequency
    cos, sin = jnp.cos(angles), jnp.sin(angles)
    return (
        jnp.concatenate([cos, cos, cos, cos], axis=-1),
        jnp.concatenate([-sin, sin, -sin, sin], axis=-1),
    )


def pair_heads(w):
    return w.reshape(w.shape[0], 2, GROUP, HD).swapaxes(1, 2).reshape(w.shape[0], -1)


def unpair_heads(w):
    return w.reshape(w.shape[0], GROUP, 2, HD).swapaxes(1, 2).reshape(w.shape[0], -1)


def local(
    hidden,
    positions,
    norm_attention,
    w_query,
    w_key,
    w_value,
    w_out,
    norm_feed,
    w_gate,
    w_up,
    w_down,
    cotangent,
    *,
    n,
):
    sequences, rows, width = hidden.shape
    half = rows // 2
    place, head = lax.axis_index("ctx"), lax.axis_index("head")
    seq, core = head // 2, head % 2
    order = jnp.array(ring_order(n), jnp.int32)
    ring_place = jnp.where(place % 2 == 0, place // 2, n - 1 - place // 2)
    step_sign = 1 - 2 * core
    ring_from = order[(ring_place - step_sign * jnp.arange(n, dtype=jnp.int32)) % n]

    gain_a = norm_attention.astype(F32)[:, None]
    gain_f = norm_feed.astype(F32)[:, None]
    q_width, k_width = w_query.shape[1], w_key.shape[1]
    slice_rows = width // n
    side = {}

    def exchange(cut, axis=0):
        return lax.all_to_all(cut, "ctx", axis, axis, tiled=True)

    def in_halves(array):
        size = array.shape[0] // 2
        return array[:size], array[size:]

    def in_columns(array):
        size = array.shape[1] // 2
        return array[:, :size], array[:, size:]

    def joined(own, near_own, far, token):
        far = jnp.concatenate([in_turn(far[0], token), far[1]], axis=0)
        return jnp.concatenate([own, far, near_own, other_core(far)], axis=1)

    own_qkv = jnp.concatenate([w_key, w_value, pair_heads(w_query)], axis=1)

    def gate_exchange(token):
        side["gate"] = exchange(cut_call(gain_f, [in_turn(w_gate, token)], n))

    def norm_work(token):
        rows_in = in_turn(hidden, token).astype(F32)
        inverse = lax.rsqrt(jnp.mean(rows_in * rows_in, axis=-1, keepdims=True) + EPSILON)
        side["unit_a"] = (rows_in * inverse).astype(BF)
        return side["unit_a"]

    qkv_pieces = ring_gather(
        cut_chains((own_qkv.astype(F32) * gain_a).astype(BF), n),
        n,
        {0: gate_exchange, 2: norm_work},
    )
    unit_a = side["unit_a"]
    gate_got = side["gate"]

    own_hidden = part(hidden, seq, core).astype(F32)
    own_cotangent = part(cotangent, seq, core)
    own_positions = lax.dynamic_slice_in_dim(positions, place * rows, rows, 1)
    cos, sin = rotation_tables(own_positions)
    starts = positions[:, ::RUN] // RUN
    starts_q = own_positions[:, ::RUN] // RUN
    key_runs = jnp.stack([ring_from * 2, ring_from * 2 + 1], axis=1).reshape(-1)
    starts_k = jnp.take(starts, key_runs, axis=1)
    every = jnp.arange(2 * n, dtype=jnp.int32)
    slots = jnp.sum(
        jnp.where(starts_k[:, None, :] == every[None, :, None], every, 0), axis=2, dtype=jnp.int32
    )
    key_value, query, qkv_weight = qkv_call(
        ring_from, unit_a, qkv_pieces, cos, sin, q_width, 2 * k_width
    )
    key_value, gate_got = lax.optimization_barrier((key_value, gate_got))
    gate_own = gate_got.reshape(width, -1)
    gate_near = other_core(gate_own)
    gate_far = [other_x(piece) for piece in in_halves(gate_own)]

    def gate_work(token):
        side["gate_weight"] = joined(gate_own, gate_near, gate_far, token)
        return side["gate_weight"]

    def up_down_work(token):
        side["sent"] = cut_call(gain_f, [in_turn(w_up, token), w_down], n)
        return side["sent"]

    pieces = ring_gather(
        (
            jnp.concatenate([key_value[j] for j in range(sequences)], axis=1),
            pair_heads(w_out.T),
            own_cotangent,
        ),
        n,
        {n - 5: gate_work, n - 3: up_down_work},
    )
    kv = [piece[0] for piece in pieces]
    out_pieces = [piece[1] for piece in pieces]
    cot_pieces = [piece[2] for piece in pieces]
    kv, out_pieces, sent = lax.optimization_barrier((kv, out_pieces, side["sent"]))
    feed_got = exchange(sent, 1)
    attended_full, attended, lse = attend_call(starts_q, slots, query, kv)
    out_pieces[0] = in_turn(out_pieces[0], lse)
    out_weight_t = ctx_order_call(ring_from, [(piece,) for piece in out_pieces])
    out_weight_t = out_weight_t.reshape(width, q_width)

    sent_core = jnp.concatenate(
        [part(attended, seq, 1 - core), part(attended, 1 - seq, 1 - core)], axis=0
    )
    got_core = other_core(mm(sent_core, out_weight_t, NT).astype(BF)).astype(F32)
    sum_far = (mm(part(attended, 1 - seq, core), out_weight_t, NT) + got_core[half:]).astype(BF)
    sum_own = mm(part(attended, seq, core), out_weight_t, NT) + got_core[:half]
    cots = []
    for at in range(2):
        some = cot_pieces[at * n // 2 : (at + 1) * n // 2]
        cots.append(gather_rows_call([in_turn(some[0], sum_far)] + some[1:]))
    got_x, cots = lax.optimization_barrier((other_x(sum_far), cots))
    x1 = own_hidden + sum_own + got_x.astype(F32)
    x1, feed_got = lax.optimization_barrier((x1, feed_got))

    inverse_f = lax.rsqrt(jnp.mean(x1 * x1, axis=-1, keepdims=True) + EPSILON)
    unit_f = x1 * inverse_f
    up_own, down_own = [feed_got[j].reshape(width, -1) for j in range(2)]
    units = 4 * up_own.shape[1]
    arrived, inputs, slabs, partial = [], [], [], []
    owns = (up_own, down_own)
    nears = [other_core(own) for own in owns]
    fars = [[other_x(piece) for piece in in_halves(own)] for own in owns]

    def up_work(token):
        side["up_weight"] = joined(owns[0], nears[0], fars[0], token)
        return side["up_weight"]

    def down_work(token):
        side["down_weight_t"] = joined(owns[1], nears[1], fars[1], token)
        return side["down_weight_t"]

    feeds = []

    def feed_work(token):
        at = len(feeds) * n // 2
        some = [part for piece in arrived[at : at + n // 2] for part in piece]
        feeds.append(gather_rows_call([in_turn(some[0], token)] + some[1:]))
        return feeds[-1]

    def feed_in(at):
        gate = mm(feeds[at], side["gate_weight"])
        up = mm(feeds[at], side["up_weight"])
        if "down_weight_t" not in side:
            down_work(up)
        dact = mm(cots[at], side["down_weight_t"])
        inputs.append((feeds[at], feeds[at], cots[at]))
        return gate, up, dact

    def feed_middle(gate, up, dact):
        sigma = jax.nn.sigmoid(gate)
        silu = gate * sigma
        act = (silu * up).astype(BF)
        dgate = (dact * up * sigma * (1.0 + gate * (1.0 - sigma))).astype(BF)
        dup = (dact * silu).astype(BF)
        return dgate, dup, act

    def feed_out(dgate, dup, act):
        e = (mm(dgate, side["gate_weight"], NT) + mm(dup, side["up_weight"], NT)).astype(BF)
        x = mm(act, side["down_weight_t"], NT).astype(BF)
        return [
            (e[j : j + half], x[j : j + half]) for j in range(0, e.shape[0], half)
        ]

    ring_gather(
        cut_chains(unit_f.astype(BF), n),
        n,
        {
            0: lambda token: fars[0][0],
            n - 6: lambda token: fars[0][1],
            n - 5: lambda token: (up_work(token), fars[1][0]),
            n - 4: feed_work,
            n - 3: lambda token: fars[1][1],
        },
        arrived,
    )
    feed_work(None)
    for at in range(2):
        slabs.append(feed_middle(*feed_in(at)))
        partial.extend(feed_out(*slabs[at]))

    grads, near = [], []

    def grad_work(token):
        j = len(grads)
        first = mm(inputs[0][j], in_turn(slabs[0][j], token), TN).astype(BF)
        first, slab = lax.optimization_barrier((first, slabs[1][j]))
        second = mm(inputs[1][j], slab, TN)
        grads.append((second + first.astype(F32)).astype(BF))
        return grads[-1]

    def near_work(token):
        grad = grads[len(near)]
        kept, sent = grad[:, : units // 2], grad[:, units // 2 :]
        total = in_turn(kept, token).astype(F32) + other_core(sent).astype(F32)
        near.append(total.astype(BF))
        quarter = units // 4
        if len(near) < 3:
            to_x.append((near[-1][:, :quarter], other_x(near[-1][:, quarter:])))
        return near[-1]

    def x_work(token):
        kept, far = to_x[len(sums_x)]
        total = in_turn(kept, token).astype(F32) + far.astype(F32)
        sums_x.append(total.astype(BF).reshape(n, slice_rows, -1))
        return sums_x[-1]

    to_x, sums_x = [], []
    e_own, x_own = ring_scatter(
        partial,
        n,
        {
            0: lambda token: (grad_work(token), near_work(token)),
            1: lambda token: (grad_work(token), near_work(token)),
            2: lambda token: (grad_work(token), to_x[0][1]),
            3: lambda token: (near_work(token), x_work(token)),
            4: lambda token: to_x[1][1],
            5: x_work,
        },
        slabs[1] + partial[-1],
    )
    while len(sums_x) < 2:
        x_work(e_own)
    feed_delivered = exchange(jnp.stack(sums_x), 1)
    e_feed = e_own.astype(F32)
    mid_grad = own_cotangent.astype(F32) + inverse_f * (
        e_feed - unit_f * jnp.mean(e_feed * unit_f, axis=-1, keepdims=True)
    )

    mid_parts = head_parts(mid_grad.astype(BF))
    down_kept, down_sent = near[2][:, : units // 4], near[2][:, units // 4 :]
    down_far = other_x(in_turn(down_sent, mid_parts[1]))
    unit_rows = unit_a.reshape(sequences * rows, width)
    attended_grad = placed([mm(p, out_weight_t).astype(BF) for p in mid_parts], seq, core)
    dquery, dkv = attend_back_call(
        starts_q, slots, query, attended_grad, attended_full, lse, kv, cos, sin
    )
    dquery = dquery.reshape(sequences * rows, -1)
    attended_parts = jnp.concatenate(
        [part(attended, s, c) for c in (core, 1 - core) for s in (seq, 1 - seq)], axis=0
    )
    out_grad_t = mm(jnp.concatenate(mid_parts, axis=0), attended_parts, TN).astype(BF)
    out_grad_t = ring_order_call(ring_from, out_grad_t.reshape(n, slice_rows, q_width))
    dquery, dkv, out_grad_t, feed_delivered, x_own = lax.optimization_barrier(
        (dquery, dkv, out_grad_t, feed_delivered, x_own)
    )
    dkv = dkv.reshape(n, rows, -1)
    x2 = x1 + x_own.astype(F32)

    def down_total(token):
        total = in_turn(down_kept, token).astype(F32) + down_far.astype(F32)
        side["down"] = total.astype(BF).reshape(n, slice_rows, -1)
        return side["down"]

    def down_exchange(token):
        side["down"] = exchange(in_turn(side["down"], token))

    def query_grad_work(token):
        grad = mm(unit_rows, in_turn(dquery, token), TN).astype(BF)
        side["q_ring"] = ring_order_call(ring_from, grad.reshape(n, slice_rows, -1))
        return side["q_ring"]

    def output_work(token):
        side["output"] = head_parts(in_turn(x2, token).astype(BF))
        return side["output"]

    def output_place(token):
        own, *rest = side["output"]
        side["output"] = placed((in_turn(own, token), *rest), seq, core)
        return side["output"]

    def gate_finish(token):
        side["gate"] = finish_call(in_turn(feed_delivered[0], token), w_gate, gain_f)
        return side["gate"]

    def up_finish(token):
        side["up"] = finish_call(in_turn(feed_delivered[1], token), w_up, gain_f)
        return side["up"]

    dkv_own, out_sum = ring_scatter(
        [(dkv[s], out_grad_t[s]) for s in range(n)],
        n,
        {
            0: down_total,
            1: lambda token: (down_exchange(token), output_work(token))[1],
            3: output_place,
            4: lambda token: (gate_finish(token), side["down"]),
            5: lambda token: (up_finish(token), query_grad_work(token)),
        },
    )
    (gate_grad, gate_sums), (up_grad, up_sums) = side["gate"], side["up"]
    pair_width = 2 * k_width
    dkv_own = jnp.stack(
        [dkv_own[:, j * pair_width : (j + 1) * pair_width] for j in range(sequences)]
    ).astype(F32)
    dkey_rot = dkv_own[:, :, :k_width]
    swapped = jnp.concatenate(
        [
            dkey_rot[:, :, HD // 2 : HD],
            dkey_rot[:, :, : HD // 2],
            dkey_rot[:, :, HD + HD // 2 :],
            dkey_rot[:, :, HD : HD + HD // 2],
        ],
        axis=-1,
    )
    dkey = dkey_rot * cos - swapped * sin
    dkv_low = jnp.concatenate(
        [dkey.astype(BF), dkv_own[:, :, k_width:].astype(BF)], axis=2
    ).reshape(sequences * rows, -1)
    dqkv = jnp.concatenate([dkv_low, dquery], axis=1)
    kv_grad = mm(unit_rows, dkv_low, TN).astype(BF).reshape(n, slice_rows, -1)
    q_ring, kv_ring = side["q_ring"], ring_order_call(ring_from, kv_grad)

    dqkv_rows = dqkv.reshape(sequences, rows, -1)
    sent_core = jnp.concatenate(
        [part(dqkv_rows, seq, 1 - core), part(dqkv_rows, 1 - seq, 1 - core)], axis=0
    )
    sent_core = in_turn(sent_core, kv_ring)
    got_core = other_core(mm(sent_core, qkv_weight, NT).astype(BF))
    inverse_a = lax.rsqrt(jnp.mean(own_hidden * own_hidden, axis=-1, keepdims=True) + EPSILON)
    unit_own = own_hidden * inverse_a

    def sum_work(token):
        got = in_turn(got_core, token).astype(F32)
        sum_far = mm(part(dqkv_rows, 1 - seq, core), qkv_weight, NT) + got[half:]
        side["e_own"] = mm(part(dqkv_rows, seq, core), qkv_weight, NT) + got[:half]
        side["e_far"] = other_x(sum_far.astype(BF))
        return side["e_own"]

    def input_work(token):
        e_in = side["e_own"] + in_turn(side["e_far"], token).astype(F32)
        input_grad = mid_grad + inverse_a * (
            e_in - unit_own * jnp.mean(e_in * unit_own, axis=-1, keepdims=True)
        )
        side["input"] = head_parts(input_grad.astype(BF))

    def input_place(token):
        own, *rest = side["input"]
        side["input"] = placed((in_turn(own, token), *rest), seq, core).astype(F32)

    def down_finish(token):
        side["down"] = finish_down_call(in_turn(side["down"], token))
        return side["down"]

    def out_finish(token):
        side["out"] = unpair_heads(in_turn(out_sum, token).astype(F32)).T
        return side["out"]

    qkv_sum = ring_scatter(
        [(q_ring[s], kv_ring[s]) for s in range(n)],
        n,
        {0: sum_work, 1: out_finish, 2: input_work, 3: down_finish, 5: input_place},
    )
    qkv_sum = jnp.concatenate(qkv_sum[::-1], axis=1).astype(F32)
    output, input_grad = side["output"], side["input"]
    out_grad, down_grad = side["out"], side["down"]

    feed_sums = gate_sums + up_sums
    attention_sums = jnp.sum(qkv_sum * own_qkv.astype(F32), axis=1, keepdims=True)
    qkv_sum = qkv_sum * gain_a
    kv_grad, query_grad = qkv_sum[:, : 2 * k_width], unpair_heads(qkv_sum[:, 2 * k_width :])
    sums = jnp.concatenate([attention_sums, feed_sums], axis=1).T
    both = lax.ppermute(sums, "head", [(h, h ^ 3) for h in range(4)])
    sums = sums + other_core(sums) + (other_x(sums) + both)

    return (
        output,
        input_grad,
        sums[0],
        query_grad,
        kv_grad[:, :k_width],
        kv_grad[:, k_width:],
        out_grad,
        sums[1],
        gate_grad,
        up_grad,
        down_grad,
    )


def solution(mesh):
    return jax.shard_map(
        functools.partial(local, n=mesh.shape["ctx"]),
        mesh=mesh,
        in_specs=(
            P(None, "ctx", None),
            P(),
            P("ctx"),
            P("ctx", "head"),
            P("ctx", "head"),
            P("ctx", "head"),
            P("head", "ctx"),
            P("ctx"),
            P("ctx", "head"),
            P("ctx", "head"),
            P("head", "ctx"),
            P(None, "ctx", None),
        ),
        out_specs=(
            P(None, "ctx", None),
            P(None, "ctx", None),
            P("ctx"),
            P("ctx", "head"),
            P("ctx", "head"),
            P("ctx", "head"),
            P("head", "ctx"),
            P("ctx"),
            P("ctx", "head"),
            P("ctx", "head"),
            P("head", "ctx"),
        ),
        check_vma=False,
    )
```

```python
import functools
import math

import jax
import jax.numpy as jnp
from jax import lax
from jax.experimental import pallas as pl
from jax.experimental.pallas import tpu as pltpu
from jax.sharding import PartitionSpec as P

HQ = 32
HK = 8
HD = 64
GROUP = HQ // HK
RUN = 128

EPSILON = 1e-05
ROPE_BASE = 500000.0
NEGATIVE = -1e30
LOG2E = math.log2(math.e)
SCALE = HD ** (-0.5)
BF = jnp.bfloat16
F32 = jnp.float32

NN = (((1,), (0,)), ((), ()))
NT = (((1,), (1,)), ((), ()))
TN = (((0,), (0,)), ((), ()))


def mm(a, b, dims=NN):
    return lax.dot_general(a, b, dims, preferred_element_type=F32)


def ring_order(n):
    return list(range(0, n, 2)) + list(range(1, n, 2))[::-1]


def ring_step(value, n):
    order = ring_order(n)
    pairs = []
    for p in range(n):
        for h in range(4):
            step = 1 if h % 2 == 0 else -1
            pairs.append((order[p] * 4 + h, order[(p + step) % n] * 4 + h))
    return lax.ppermute(value, ("ctx", "head"), pairs)


def in_turn(value, other):
    return value if other is None else lax.optimization_barrier((value, other))[0]


class Side:
    def __init__(self, hooks):
        self.hooks, self.due = hooks or {}, None

    def arrived(self, got, last):
        due, self.due = self.due, None
        return in_turn(got, last if due is None else (last, due))

    def after(self, step, token):
        if step in self.hooks:
            self.due = self.hooks[step](token)


def ring_gather(chains, n, hooks=None, pieces=None, due=None):
    chains, side, last = list(chains), Side(hooks), None
    side.due = due
    pieces = [] if pieces is None else pieces
    pieces.append(tuple(chains))
    for step in range(n - 1):
        for j in range(len(chains)):
            got = ring_step(chains[j], n)
            final = j == len(chains) - 1
            last = chains[j] = side.arrived(got, last) if final else in_turn(got, last)
        pieces.append(tuple(chains))
        side.after(step, last)
    return pieces


def ring_scatter(pieces, n, hooks=None, due=None):
    totals, side, last = list(pieces[1 % n]), Side(hooks), None
    side.due = due
    for step, s in enumerate(list(range(2, n)) + [0]):
        for j in range(len(totals)):
            got = ring_step(totals[j], n)
            final = j == len(totals) - 1
            got = side.arrived(got, last) if final else in_turn(got, last)
            last = totals[j] = (got.astype(F32) + pieces[s][j].astype(F32)).astype(BF)
        side.after(step, last)
    return totals


def cut_chains(piece, n):
    count = 2 if n <= 8 else 1
    size = piece.shape[0] // count
    return tuple(piece[j * size : (j + 1) * size] for j in range(count))


def other_core(value):
    return lax.ppermute(value, "head", [(h, h ^ 1) for h in range(4)])


def other_x(value):
    return lax.ppermute(value, "head", [(h, h ^ 2) for h in range(4)])


def part(array, seq, core):
    half = array.shape[1] // 2
    return lax.dynamic_slice(array, (seq, core * half, 0), (1, half, array.shape[2]))[0]


def head_parts(own):
    far = other_x(own)
    near = other_core(jnp.concatenate([own, far], axis=0))
    return own, far, near[: own.shape[0]], near[own.shape[0] :]


def placed(parts, seq, core):
    own, far, near, both = parts
    by_core = lambda a, b: (jnp.where(core == 0, a, b), jnp.where(core == 0, b, a))
    mine, other = by_core(own, near), by_core(far, both)
    first = [jnp.where(seq == 0, a, b) for a, b in zip(mine, other)]
    second = [jnp.where(seq == 0, b, a) for a, b in zip(mine, other)]
    return jnp.stack([jnp.concatenate(first, axis=0), jnp.concatenate(second, axis=0)])


def swap_halves(v):
    lane = lax.broadcasted_iota(jnp.int32, v.shape, 1) % HD
    return jnp.where(lane < HD // 2, pltpu.roll(v, 2 * HD - HD // 2, 1), pltpu.roll(v, HD // 2, 1))


def rotated(v, cos, sin):
    return v * cos + swap_halves(v) * sin


def qkv_kernel(count, index_ref, unit_ref, cos_ref, sin_ref, *refs):
    *pieces, kv_ref, q_ref, w_ref = refs
    lines = pieces[0].shape[0]

    @pl.when(pl.program_id(0) == 0)
    def _():
        for at, piece in enumerate(pieces):
            line = (index_ref[at // count] * count + at % count) * lines
            w_ref[pl.ds(pl.multiple_of(line, lines), lines), :] = piece[...]

    y = mm(unit_ref[0], w_ref[...])
    cos, sin = cos_ref[0], sin_ref[0]
    width = kv_ref.shape[2] // 2
    for j in range(0, width, 2 * HD):
        kv_ref[0, :, j : j + 2 * HD] = rotated(y[:, j : j + 2 * HD], cos, sin).astype(BF)
    kv_ref[0, :, width:] = y[:, width : 2 * width].astype(BF)
    for j in range(0, q_ref.shape[2], 2 * HD):
        at = 2 * width + j
        q_ref[0, :, j : j + 2 * HD] = rotated(y[:, at : at + 2 * HD], cos, sin).astype(BF)


def qkv_call(ring_from, unit, pieces, cos, sin, q_width, kv_width):
    sequences, rows, width = unit.shape
    count = len(pieces[0])
    parts = [part for piece in pieces for part in piece]
    spec = lambda w: pl.BlockSpec((1, rows, w), lambda s: (s, 0, 0))
    whole = lambda shape: pl.BlockSpec(shape, lambda s: (0, 0))
    weight = (width, kv_width + q_width)
    return pl.pallas_call(
        functools.partial(qkv_kernel, count),
        grid=(sequences,),
        in_specs=[
            pl.BlockSpec(memory_space=pltpu.SMEM),
            spec(width),
            spec(2 * HD),
            spec(2 * HD),
        ]
        + [whole(part.shape) for part in parts],
        out_specs=[spec(kv_width), spec(q_width), whole(weight)],
        out_shape=[
            jax.ShapeDtypeStruct((sequences, rows, kv_width), BF),
            jax.ShapeDtypeStruct((sequences, rows, q_width), BF),
            jax.ShapeDtypeStruct(weight, BF),
        ],
        compiler_params=pltpu.CompilerParams(vmem_limit_bytes=60 * 1024 * 1024),
        cost_estimate=pl.CostEstimate(
            flops=2 * sequences * rows * width * weight[1],
            bytes_accessed=weight[0] * weight[1] * 4 + unit.size * 4,
            transcendentals=0,
        ),
        name="qkv",
    )(ring_from, unit, cos, sin, *parts)


def half_mask(v, which):
    lane = lax.broadcasted_iota(jnp.int32, v.shape, 1)
    keep = (lane < HD) if which == 0 else (lane >= HD)
    return jnp.where(keep, v, jnp.zeros_like(v))


def stack_heads(block):
    return jnp.concatenate(
        [block[:, g * 2 * HD : (g + 1) * 2 * HD] for g in range(GROUP)], axis=0
    )


def causal(scores, gap):
    key = lax.broadcasted_iota(jnp.int32, scores.shape, 0)
    query = lax.broadcasted_iota(jnp.int32, scores.shape, 1) % RUN
    return jnp.where(key <= query + gap, scores, NEGATIVE)


def run_pair(kv_ref, slots, at):
    return jnp.concatenate([kv_ref[j, :, at : at + 2 * HD] for j in slots], axis=0)


def load_runs(pieces, kv_ref):
    rows = pieces[0].shape[0]
    for at, piece in enumerate(pieces):
        for r in range(rows // RUN):
            kv_ref[at * rows // RUN + r] = piece[r * RUN : (r + 1) * RUN]


def attend_kernel(n, sq_ref, sk_ref, q_ref, *refs):
    pieces, refs = refs[:n], refs[n:]
    o_ref, low_ref, lse_ref, kv_ref, s_ref, m_ref, l_ref, acc_ref = refs
    seq, run = pl.program_id(0), pl.program_id(1)
    start = sq_ref[seq, run]

    @pl.when(run == 0)
    def _():
        load_runs(pieces, kv_ref)

    runs = kv_ref.shape[0]
    columns = GROUP * RUN
    queries = stack_heads(q_ref[0])
    q_pair = [half_mask(queries, k) for k in range(2)]
    m_ref[...] = jnp.full_like(m_ref, NEGATIVE)
    l_ref[...] = jnp.zeros_like(l_ref)
    acc_ref[...] = jnp.zeros_like(acc_ref)

    def slots_of(i):
        return [sk_ref[seq, 2 * i], sk_ref[seq, 2 * i + 1]]

    def rows_of(i):
        return pl.ds(pl.multiple_of(i * 2 * RUN, 2 * RUN), 2 * RUN)

    def scores(i, masked):
        keys = run_pair(kv_ref, slots_of(i), 0)
        for k in range(2):
            s = mm(keys, q_pair[k], NT) * (SCALE * LOG2E)
            if masked:
                s = causal(s, (start - 2 * i) * RUN)
            s_ref[k, rows_of(i), :] = s
            m_ref[k] = jnp.maximum(m_ref[k], jnp.max(s.reshape(-1, 8, columns), axis=0))

    def score_step(i, carry):
        scores(i, False)
        return carry

    last = start // 2
    lax.fori_loop(0, last, score_step, 0)
    scores(last, True)
    peaks = [jnp.max(m_ref[k], axis=0, keepdims=True) for k in range(2)]

    def value_step(i, carry):
        values = run_pair(kv_ref, slots_of(i), 2 * HD)
        for k in range(2):
            p = jnp.exp2(s_ref[k, rows_of(i), :] - peaks[k])
            l_ref[k] += jnp.sum(p.reshape(-1, 8, columns), axis=0)
            acc_ref[k] += mm(values, p.astype(BF), TN)
        return carry

    lax.fori_loop(0, last + 1, value_step, 0)
    rows = []
    for k in range(2):
        total = jnp.sum(l_ref[k], axis=0, keepdims=True)
        lse_ref[0, 0, k : k + 1, :] = peaks[k] + jnp.log2(total)
        rows.append(acc_ref[k, k * HD : (k + 1) * HD, :] / total)
    both = jnp.concatenate(rows, axis=0)
    for g in range(GROUP):
        out = both[:, g * RUN : (g + 1) * RUN].T
        o_ref[0, :, g * 2 * HD : (g + 1) * 2 * HD] = out
        low_ref[0, :, g * 2 * HD : (g + 1) * 2 * HD] = out.astype(BF)


def attend_call(starts_q, starts_k, query, pieces):
    sequences, rows, width = query.shape
    n, piece_rows, kv_width = len(pieces), pieces[0].shape[0], pieces[0].shape[1] // sequences
    runs = n * piece_rows // RUN
    columns = GROUP * RUN
    smem = pl.BlockSpec(memory_space=pltpu.SMEM)
    row_spec = pl.BlockSpec((1, RUN, width), lambda s, r: (s, r, 0))
    return pl.pallas_call(
        functools.partial(attend_kernel, n),
        grid=(sequences, rows // RUN),
        in_specs=[
            smem,
            smem,
            row_spec,
        ]
        + [pl.BlockSpec((piece_rows, kv_width), lambda s, r: (0, s))] * n,
        out_specs=[row_spec, row_spec, pl.BlockSpec((1, 1, 2, columns), lambda s, r: (s, r, 0, 0))],
        out_shape=[
            jax.ShapeDtypeStruct((sequences, rows, width), F32),
            jax.ShapeDtypeStruct((sequences, rows, width), BF),
            jax.ShapeDtypeStruct((sequences, rows // RUN, 2, columns), F32),
        ],
        scratch_shapes=[
            pltpu.VMEM((runs, RUN, kv_width), BF),
            pltpu.VMEM((2, runs * RUN, columns), F32),
            pltpu.VMEM((2, 8, columns), F32),
            pltpu.VMEM((2, 8, columns), F32),
            pltpu.VMEM((2, 2 * HD, columns), F32),
        ],
        compiler_params=pltpu.CompilerParams(vmem_limit_bytes=56 * 1024 * 1024),
        cost_estimate=pl.CostEstimate(
            flops=50 * sequences * rows * runs * RUN * width,
            bytes_accessed=n * pieces[0].size * 2 + query.size * 6,
            transcendentals=sequences * rows * runs * RUN * 4,
        ),
        name="attend",
    )(starts_q, starts_k, query, *pieces)


def attend_back_kernel(n, sq_ref, sk_ref, q_ref, do_ref, o_ref, lse_ref, cos_ref, sin_ref, *refs):
    pieces, refs = refs[:n], refs[n:]
    dq_ref, dkv_ref, kv_ref, sum_ref, acc_ref = refs
    seq, run = pl.program_id(0), pl.program_id(1)
    start = sq_ref[seq, run]
    runs = kv_ref.shape[0]
    queries = stack_heads(q_ref[0])
    upstream = stack_heads(do_ref[0])
    attended = stack_heads(o_ref[0])
    q_pair = [half_mask(queries, k) for k in range(2)]
    u_pair = [half_mask(upstream, k) for k in range(2)]
    product = upstream.astype(F32) * attended
    deltas = [
        lax.dot_general(
            half_mask(jnp.ones((8, 2 * HD), F32), k),
            product,
            NT,
            precision=lax.Precision.HIGHEST,
            preferred_element_type=F32,
        )[:1]
        for k in range(2)
    ]
    lses = [lse_ref[0, 0, k : k + 1, :] for k in range(2)]
    acc_ref[...] = jnp.zeros_like(acc_ref)

    @pl.when(run == 0)
    def _():
        load_runs(pieces, kv_ref)
        sum_ref[...] = jnp.zeros_like(sum_ref)

    def work(i, masked):
        slots = [sk_ref[seq, 2 * i], sk_ref[seq, 2 * i + 1]]
        keys, values = run_pair(kv_ref, slots, 0), run_pair(kv_ref, slots, 2 * HD)
        dk, dv = 0.0, 0.0
        for k in range(2):
            s = mm(keys, q_pair[k], NT) * (SCALE * LOG2E)
            if masked:
                s = causal(s, (start - 2 * i) * RUN)
            p = jnp.exp2(s - lses[k])
            dp = mm(values, u_pair[k], NT)
            ds = (p * (dp - deltas[k])).astype(BF)
            dk += mm(ds, q_pair[k])
            dv += mm(p.astype(BF), u_pair[k])
            acc_ref[k] += mm(keys, ds, TN)
        for half, j in enumerate(slots):
            sum_ref[j, :, : 2 * HD] += dk[half * RUN : (half + 1) * RUN]
            sum_ref[j, :, 2 * HD :] += dv[half * RUN : (half + 1) * RUN]

    def step(i, carry):
        work(i, False)
        return carry

    lax.fori_loop(0, start // 2, step, 0)
    work(start // 2, True)
    both = jnp.concatenate([acc_ref[k, k * HD : (k + 1) * HD, :] for k in range(2)], axis=0)
    cos, sin = cos_ref[0], sin_ref[0]
    for g in range(GROUP):
        v = both[:, g * RUN : (g + 1) * RUN].T * SCALE
        dq_ref[0, :, g * 2 * HD : (g + 1) * 2 * HD] = (v * cos - swap_halves(v) * sin).astype(BF)

    @pl.when(run == pl.num_programs(1) - 1)
    def _():
        dkv_ref[:, :, : 2 * HD] = (sum_ref[:, :, : 2 * HD] * SCALE).astype(BF)
        dkv_ref[:, :, 2 * HD :] = sum_ref[:, :, 2 * HD :].astype(BF)


def attend_back_call(starts_q, starts_k, query, upstream, attended, lse, pieces, cos, sin):
    sequences, rows, width = query.shape
    n, piece_rows, kv_width = len(pieces), pieces[0].shape[0], pieces[0].shape[1] // sequences
    runs = n * piece_rows // RUN
    columns = GROUP * RUN
    smem = pl.BlockSpec(memory_space=pltpu.SMEM)
    row_spec = pl.BlockSpec((1, RUN, width), lambda s, r: (s, r, 0))
    table_spec = pl.BlockSpec((1, RUN, 2 * HD), lambda s, r: (s, r, 0))
    kv_spec = pl.BlockSpec((runs, RUN, kv_width), lambda s, r: (0, 0, s))
    return pl.pallas_call(
        functools.partial(attend_back_kernel, n),
        grid=(sequences, rows // RUN),
        in_specs=[
            smem,
            smem,
            row_spec,
            row_spec,
            row_spec,
            pl.BlockSpec((1, 1, 2, columns), lambda s, r: (s, r, 0, 0)),
            table_spec,
            table_spec,
        ]
        + [pl.BlockSpec((piece_rows, kv_width), lambda s, r: (0, s))] * n,
        out_specs=[row_spec, kv_spec],
        out_shape=[
            jax.ShapeDtypeStruct((sequences, rows, width), BF),
            jax.ShapeDtypeStruct((runs, RUN, sequences * kv_width), BF),
        ],
        scratch_shapes=[
            pltpu.VMEM((runs, RUN, kv_width), BF),
            pltpu.VMEM((runs, RUN, 4 * HD), F32),
            pltpu.VMEM((2, 2 * HD, columns), F32),
        ],
        compiler_params=pltpu.CompilerParams(vmem_limit_bytes=56 * 1024 * 1024),
        cost_estimate=pl.CostEstimate(
            flops=80 * sequences * rows * runs * RUN * width,
            bytes_accessed=n * pieces[0].size * 4 + query.size * 10,
            transcendentals=sequences * rows * runs * RUN * 4,
        ),
        name="attend_back",
    )(starts_q, starts_k, query, upstream, attended, lse, cos, sin, *pieces)


def ctx_order_kernel(index_ref, *refs):
    *pieces, o_ref = refs
    count = len(pieces) // o_ref.shape[0]
    rows = pieces[0].shape[0]
    for at, piece in enumerate(pieces):
        line = at % count * rows
        o_ref[index_ref[at // count], line : line + rows, :] = piece[...]


def ctx_order_call(ring_from, pieces):
    n, count = len(pieces), len(pieces[0])
    rows, width = pieces[0][0].shape
    return pl.pallas_call(
        ctx_order_kernel,
        grid=(1,),
        in_specs=[pl.BlockSpec(memory_space=pltpu.SMEM)]
        + [pl.BlockSpec((rows, width), lambda i: (0, 0))] * (n * count),
        out_specs=pl.BlockSpec((n, count * rows, width), lambda i: (0, 0, 0)),
        out_shape=jax.ShapeDtypeStruct((n, count * rows, width), BF),
        compiler_params=pltpu.CompilerParams(vmem_limit_bytes=60 * 1024 * 1024),
        name="ctx_order",
    )(ring_from, *[piece for chains in pieces for piece in chains])


def ring_order_kernel(index_ref, x_ref, o_ref):
    for s in range(o_ref.shape[0]):
        o_ref[s] = x_ref[index_ref[s]]


def ring_order_call(ring_from, blocks):
    return pl.pallas_call(
        ring_order_kernel,
        in_specs=[
            pl.BlockSpec(memory_space=pltpu.SMEM),
            pl.BlockSpec(memory_space=pltpu.VMEM),
        ],
        out_specs=pl.BlockSpec(memory_space=pltpu.VMEM),
        out_shape=jax.ShapeDtypeStruct(blocks.shape, blocks.dtype),
        compiler_params=pltpu.CompilerParams(vmem_limit_bytes=12 * 1024 * 1024),
        name="ring_order",
    )(ring_from, blocks)


def gather_rows_kernel(*refs):
    *pieces, o_ref = refs
    rows = pieces[0].shape[0]
    for at, piece in enumerate(pieces):
        o_ref[at * rows : (at + 1) * rows] = piece[...]


def gather_rows_call(pieces):
    rows, width = pieces[0].shape
    shape = (len(pieces) * rows, width)
    return pl.pallas_call(
        gather_rows_kernel,
        grid=(1,),
        in_specs=[pl.BlockSpec((rows, width), lambda i: (0, 0))] * len(pieces),
        out_specs=pl.BlockSpec(shape, lambda i: (0, 0)),
        out_shape=jax.ShapeDtypeStruct(shape, BF),
        compiler_params=pltpu.CompilerParams(vmem_limit_bytes=16 * 1024 * 1024),
        name="gather_rows",
    )(*pieces)


def cut_kernel(chunk, gain_ref, *refs):
    *weights, o_ref = refs
    n = o_ref.shape[-3]
    for j, w_ref in enumerate(weights):
        for t in range(n):
            if w_ref.shape[0] == o_ref.shape[-2]:
                piece = w_ref[:, t * chunk : (t + 1) * chunk].astype(F32) * gain_ref[...]
            else:
                piece = w_ref[t * chunk : (t + 1) * chunk, :].astype(F32).T
            if len(o_ref.shape) == 4:
                o_ref[j, t] = piece.astype(BF)
            else:
                o_ref[t] = piece.astype(BF)


def cut_call(gain, weights, n):
    rows = gain.shape[0]
    chunk = weights[0].shape[1] // n
    shape = (n, rows, chunk) if len(weights) == 1 else (len(weights), n, rows, chunk)
    whole = lambda shape: pl.BlockSpec(shape, lambda i: (0,) * len(shape))
    return pl.pallas_call(
        functools.partial(cut_kernel, chunk),
        grid=(1,),
        in_specs=[whole(gain.shape)] + [whole(w.shape) for w in weights],
        out_specs=whole(shape),
        out_shape=jax.ShapeDtypeStruct(shape, BF),
        compiler_params=pltpu.CompilerParams(vmem_limit_bytes=16 * 1024 * 1024),
        name="cut",
    )(gain, *weights)


def finish_kernel(got_ref, w_ref, gain_ref, grad_ref, sum_ref):
    n, rows, chunk = got_ref.shape
    sums = jnp.zeros((rows, 1), F32)
    for t in range(n):
        grad = got_ref[t].astype(F32)
        grad_ref[:, t * chunk : (t + 1) * chunk] = grad * gain_ref[...]
        weight = w_ref[:, t * chunk : (t + 1) * chunk].astype(F32)
        sums += jnp.sum(grad * weight, axis=1, keepdims=True)
    sum_ref[...] = sums


def finish_call(got, weight, gain):
    n, rows, chunk = got.shape
    vmem = pl.BlockSpec(memory_space=pltpu.VMEM)
    return pl.pallas_call(
        finish_kernel,
        in_specs=[vmem] * 3,
        out_specs=[vmem] * 2,
        out_shape=[
            jax.ShapeDtypeStruct((rows, n * chunk), F32),
            jax.ShapeDtypeStruct((rows, 1), F32),
        ],
        compiler_params=pltpu.CompilerParams(vmem_limit_bytes=16 * 1024 * 1024),
        name="finish",
    )(got, weight, gain)


def finish_down_kernel(got_ref, grad_ref):
    n, rows, chunk = got_ref.shape
    for t in range(n):
        grad_ref[t * chunk : (t + 1) * chunk, :] = got_ref[t].astype(F32).T


def finish_down_call(got):
    n, rows, chunk = got.shape
    vmem = pl.BlockSpec(memory_space=pltpu.VMEM)
    return pl.pallas_call(
        finish_down_kernel,
        in_specs=[vmem],
        out_specs=vmem,
        out_shape=jax.ShapeDtypeStruct((n * chunk, rows), F32),
        compiler_params=pltpu.CompilerParams(vmem_limit_bytes=16 * 1024 * 1024),
        name="finish_down",
    )(got)


def rotation_tables(place_rows):
    half = HD // 2
    frequency = jnp.exp(jnp.arange(half, dtype=F32) * (-2.0 * math.log(ROPE_BASE) / HD))
    angles = place_rows.astype(F32)[..., None] * frequency
    cos, sin = jnp.cos(angles), jnp.sin(angles)
    return (
        jnp.concatenate([cos, cos, cos, cos], axis=-1),
        jnp.concatenate([-sin, sin, -sin, sin], axis=-1),
    )


def pair_heads(w):
    return w.reshape(w.shape[0], 2, GROUP, HD).swapaxes(1, 2).reshape(w.shape[0], -1)


def unpair_heads(w):
    return w.reshape(w.shape[0], GROUP, 2, HD).swapaxes(1, 2).reshape(w.shape[0], -1)


def local(
    hidden,
    positions,
    norm_attention,
    w_query,
    w_key,
    w_value,
    w_out,
    norm_feed,
    w_gate,
    w_up,
    w_down,
    cotangent,
    *,
    n,
):
    sequences, rows, width = hidden.shape
    half = rows // 2
    place, head = lax.axis_index("ctx"), lax.axis_index("head")
    seq, core = head // 2, head % 2
    order = jnp.array(ring_order(n), jnp.int32)
    ring_place = jnp.where(place % 2 == 0, place // 2, n - 1 - place // 2)
    step_sign = 1 - 2 * core
    ring_from = order[(ring_place - step_sign * jnp.arange(n, dtype=jnp.int32)) % n]

    gain_a = norm_attention.astype(F32)[:, None]
    gain_f = norm_feed.astype(F32)[:, None]
    q_width, k_width = w_query.shape[1], w_key.shape[1]
    slice_rows = width // n
    side = {}

    def exchange(cut, axis=0):
        return lax.all_to_all(cut, "ctx", axis, axis, tiled=True)

    def in_halves(array):
        size = array.shape[0] // 2
        return array[:size], array[size:]

    def in_columns(array):
        size = array.shape[1] // 2
        return array[:, :size], array[:, size:]

    def joined(own, near_own, far, token):
        far = jnp.concatenate([in_turn(far[0], token), far[1]], axis=0)
        return jnp.concatenate([own, far, near_own, other_core(far)], axis=1)

    own_qkv = jnp.concatenate([w_key, w_value, pair_heads(w_query)], axis=1)

    def cut_work(token):
        side["gate_cut"] = cut_call(gain_f, [in_turn(w_gate, token)], n)
        return side["gate_cut"]

    def norm_work(token):
        rows_in = in_turn(hidden, token).astype(F32)
        inverse = lax.rsqrt(jnp.mean(rows_in * rows_in, axis=-1, keepdims=True) + EPSILON)
        side["unit_a"] = (rows_in * inverse).astype(BF)
        return side["unit_a"]

    qkv_pieces = ring_gather(
        cut_chains((own_qkv.astype(F32) * gain_a).astype(BF), n),
        n,
        {2: norm_work, 4: cut_work},
    )
    unit_a = side["unit_a"]
    gate_got = exchange(in_turn(side["gate_cut"], qkv_pieces[-1][-1]))

    own_hidden = part(hidden, seq, core).astype(F32)
    own_cotangent = part(cotangent, seq, core)
    own_positions = lax.dynamic_slice_in_dim(positions, place * rows, rows, 1)
    cos, sin = rotation_tables(own_positions)
    starts = positions[:, ::RUN] // RUN
    starts_q = own_positions[:, ::RUN] // RUN
    key_runs = jnp.stack([ring_from * 2, ring_from * 2 + 1], axis=1).reshape(-1)
    starts_k = jnp.take(starts, key_runs, axis=1)
    every = jnp.arange(2 * n, dtype=jnp.int32)
    slots = jnp.sum(
        jnp.where(starts_k[:, None, :] == every[None, :, None], every, 0), axis=2, dtype=jnp.int32
    )
    key_value, query, qkv_weight = qkv_call(
        ring_from, unit_a, qkv_pieces, cos, sin, q_width, 2 * k_width
    )
    gate_own = gate_got.reshape(width, -1)
    gate_near = other_core(gate_own)
    gate_far = [other_x(piece) for piece in in_halves(gate_own)]

    def gate_work(token):
        side["gate_weight"] = joined(gate_own, gate_near, gate_far, token)
        return side["gate_weight"]

    def up_down_work(token):
        side["sent"] = cut_call(gain_f, [in_turn(w_up, token), w_down], n)
        return side["sent"]

    pieces = ring_gather(
        (
            jnp.concatenate([key_value[j] for j in range(sequences)], axis=1),
            pair_heads(w_out.T),
            own_cotangent,
        ),
        n,
        {
            1: lambda token: gate_far[0],
            n - 5: lambda token: gate_far[1],
            n - 4: gate_work,
            n - 3: up_down_work,
        },
        due=gate_got,
    )
    kv = [piece[0] for piece in pieces]
    out_pieces = [piece[1] for piece in pieces]
    cot_pieces = [piece[2] for piece in pieces]
    kv, out_pieces, sent = lax.optimization_barrier((kv, out_pieces, side["sent"]))
    feed_got = exchange(sent, 1)
    attended_full, attended, lse = attend_call(starts_q, slots, query, kv)
    out_pieces[0] = in_turn(out_pieces[0], lse)
    out_weight_t = ctx_order_call(ring_from, [(piece,) for piece in out_pieces])
    out_weight_t = out_weight_t.reshape(width, q_width)

    sent_core = jnp.concatenate(
        [part(attended, seq, 1 - core), part(attended, 1 - seq, 1 - core)], axis=0
    )
    got_core = other_core(mm(sent_core, out_weight_t, NT).astype(BF)).astype(F32)
    sum_far = (mm(part(attended, 1 - seq, core), out_weight_t, NT) + got_core[half:]).astype(BF)
    sum_own = mm(part(attended, seq, core), out_weight_t, NT) + got_core[:half]
    cots = []
    for at in range(2):
        some = cot_pieces[at * n // 2 : (at + 1) * n // 2]
        cots.append(gather_rows_call([in_turn(some[0], sum_far)] + some[1:]))
    got_x, cots = lax.optimization_barrier((other_x(sum_far), cots))
    x1 = own_hidden + sum_own + got_x.astype(F32)
    x1, feed_got = lax.optimization_barrier((x1, feed_got))

    inverse_f = lax.rsqrt(jnp.mean(x1 * x1, axis=-1, keepdims=True) + EPSILON)
    unit_f = x1 * inverse_f
    up_own, down_own = [feed_got[j].reshape(width, -1) for j in range(2)]
    units = 4 * up_own.shape[1]
    arrived, inputs, slabs, partial = [], [], [], []
    owns = (up_own, down_own)
    nears = [other_core(own) for own in owns]
    fars = [[other_x(piece) for piece in in_halves(own)] for own in owns]

    def up_work(token):
        side["up_weight"] = joined(owns[0], nears[0], fars[0], token)
        return side["up_weight"]

    def down_work(token):
        side["down_weight_t"] = joined(owns[1], nears[1], fars[1], token)
        return side["down_weight_t"]

    feeds = []

    def feed_work(token):
        at = len(feeds) * n // 2
        some = [part for piece in arrived[at : at + n // 2] for part in piece]
        feeds.append(gather_rows_call([in_turn(some[0], token)] + some[1:]))
        return feeds[-1]

    def feed_in(at):
        gate = mm(feeds[at], side["gate_weight"])
        up = mm(feeds[at], side["up_weight"])
        if "down_weight_t" not in side:
            down_work(up)
        dact = mm(cots[at], side["down_weight_t"])
        inputs.append((feeds[at], feeds[at], cots[at]))
        return gate, up, dact

    def feed_middle(gate, up, dact):
        sigma = jax.nn.sigmoid(gate)
        silu = gate * sigma
        act = (silu * up).astype(BF)
        dgate = (dact * up * sigma * (1.0 + gate * (1.0 - sigma))).astype(BF)
        dup = (dact * silu).astype(BF)
        return dgate, dup, act

    def feed_out(dgate, dup, act):
        e = (mm(dgate, side["gate_weight"], NT) + mm(dup, side["up_weight"], NT)).astype(BF)
        x = mm(act, side["down_weight_t"], NT).astype(BF)
        return [
            (e[j : j + half], x[j : j + half]) for j in range(0, e.shape[0], half)
        ]

    ring_gather(
        cut_chains(unit_f.astype(BF), n),
        n,
        {
            0: lambda token: fars[0][0],
            n - 6: lambda token: fars[0][1],
            n - 5: lambda token: (up_work(token), fars[1][0]),
            n - 4: feed_work,
            n - 3: lambda token: fars[1][1],
        },
        arrived,
    )
    feed_work(None)
    for at in range(2):
        slabs.append(feed_middle(*feed_in(at)))
        partial.extend(feed_out(*slabs[at]))

    grads, near = [], []

    def grad_work(token):
        j = len(grads)
        first = mm(inputs[0][j], in_turn(slabs[0][j], token), TN).astype(BF)
        first, slab = lax.optimization_barrier((first, slabs[1][j]))
        second = mm(inputs[1][j], slab, TN)
        grads.append((second + first.astype(F32)).astype(BF))
        return grads[-1]

    def near_work(token):
        grad = grads[len(near)]
        kept, sent = grad[:, : units // 2], grad[:, units // 2 :]
        total = in_turn(kept, token).astype(F32) + other_core(sent).astype(F32)
        near.append(total.astype(BF))
        quarter = units // 4
        if len(near) < 3:
            to_x.append((near[-1][:, :quarter], other_x(near[-1][:, quarter:])))
        return near[-1]

    def x_work(token):
        kept, far = to_x[len(sums_x)]
        total = in_turn(kept, token).astype(F32) + far.astype(F32)
        sums_x.append(total.astype(BF).reshape(n, slice_rows, -1))
        return sums_x[-1]

    to_x, sums_x = [], []
    e_own, x_own = ring_scatter(
        partial,
        n,
        {
            0: lambda token: (grad_work(token), near_work(token)),
            1: lambda token: (grad_work(token), near_work(token)),
            2: lambda token: (grad_work(token), to_x[0][1]),
            3: lambda token: (near_work(token), x_work(token)),
            4: lambda token: to_x[1][1],
            5: x_work,
        },
        slabs[1] + partial[-1],
    )
    while len(sums_x) < 2:
        x_work(e_own)
    feed_delivered = exchange(jnp.stack(sums_x), 1)
    e_feed = e_own.astype(F32)
    mid_grad = own_cotangent.astype(F32) + inverse_f * (
        e_feed - unit_f * jnp.mean(e_feed * unit_f, axis=-1, keepdims=True)
    )

    mid_parts = head_parts(mid_grad.astype(BF))
    down_kept, down_sent = near[2][:, : units // 4], near[2][:, units // 4 :]
    down_far = other_x(in_turn(down_sent, mid_parts[1]))
    unit_rows = unit_a.reshape(sequences * rows, width)
    attended_grad = placed([mm(p, out_weight_t).astype(BF) for p in mid_parts], seq, core)
    dquery, dkv = attend_back_call(
        starts_q, slots, query, attended_grad, attended_full, lse, kv, cos, sin
    )
    dquery = dquery.reshape(sequences * rows, -1)
    attended_parts = jnp.concatenate(
        [part(attended, s, c) for c in (core, 1 - core) for s in (seq, 1 - seq)], axis=0
    )
    out_grad_t = mm(jnp.concatenate(mid_parts, axis=0), attended_parts, TN).astype(BF)
    out_grad_t = ring_order_call(ring_from, out_grad_t.reshape(n, slice_rows, q_width))
    dquery, dkv, out_grad_t, feed_delivered, x_own = lax.optimization_barrier(
        (dquery, dkv, out_grad_t, feed_delivered, x_own)
    )
    dkv = dkv.reshape(n, rows, -1)
    x2 = x1 + x_own.astype(F32)

    def down_total(token):
        total = in_turn(down_kept, token).astype(F32) + down_far.astype(F32)
        side["down"] = total.astype(BF).reshape(n, slice_rows, -1)
        return side["down"]

    def down_exchange(token):
        side["down"] = exchange(in_turn(side["down"], token))

    def query_grad_work(token):
        grad = mm(unit_rows, in_turn(dquery, token), TN).astype(BF)
        side["q_ring"] = ring_order_call(ring_from, grad.reshape(n, slice_rows, -1))
        return side["q_ring"]

    def output_work(token):
        side["output"] = head_parts(in_turn(x2, token).astype(BF))
        return side["output"]

    def output_place(token):
        own, *rest = side["output"]
        side["output"] = placed((in_turn(own, token), *rest), seq, core)
        return side["output"]

    def gate_finish(token):
        side["gate"] = finish_call(in_turn(feed_delivered[0], token), w_gate, gain_f)
        return side["gate"]

    def up_finish(token):
        side["up"] = finish_call(in_turn(feed_delivered[1], token), w_up, gain_f)
        return side["up"]

    dkv_own, out_sum = ring_scatter(
        [(dkv[s], out_grad_t[s]) for s in range(n)],
        n,
        {
            0: down_total,
            1: lambda token: (down_exchange(token), output_work(token))[1],
            3: output_place,
            4: lambda token: (gate_finish(token), side["down"]),
            5: lambda token: (up_finish(token), query_grad_work(token)),
        },
    )
    (gate_grad, gate_sums), (up_grad, up_sums) = side["gate"], side["up"]
    pair_width = 2 * k_width
    dkv_own = jnp.stack(
        [dkv_own[:, j * pair_width : (j + 1) * pair_width] for j in range(sequences)]
    ).astype(F32)
    dkey_rot = dkv_own[:, :, :k_width]
    swapped = jnp.concatenate(
        [
            dkey_rot[:, :, HD // 2 : HD],
            dkey_rot[:, :, : HD // 2],
            dkey_rot[:, :, HD + HD // 2 :],
            dkey_rot[:, :, HD : HD + HD // 2],
        ],
        axis=-1,
    )
    dkey = dkey_rot * cos - swapped * sin
    dkv_low = jnp.concatenate(
        [dkey.astype(BF), dkv_own[:, :, k_width:].astype(BF)], axis=2
    ).reshape(sequences * rows, -1)
    dqkv = jnp.concatenate([dkv_low, dquery], axis=1)
    kv_grad = mm(unit_rows, dkv_low, TN).astype(BF).reshape(n, slice_rows, -1)
    q_ring, kv_ring = side["q_ring"], ring_order_call(ring_from, kv_grad)

    dqkv_rows = dqkv.reshape(sequences, rows, -1)
    sent_core = jnp.concatenate(
        [part(dqkv_rows, seq, 1 - core), part(dqkv_rows, 1 - seq, 1 - core)], axis=0
    )
    sent_core = in_turn(sent_core, kv_ring)
    got_core = other_core(mm(sent_core, qkv_weight, NT).astype(BF))
    inverse_a = lax.rsqrt(jnp.mean(own_hidden * own_hidden, axis=-1, keepdims=True) + EPSILON)
    unit_own = own_hidden * inverse_a

    def sum_work(token):
        got = in_turn(got_core, token).astype(F32)
        sum_far = mm(part(dqkv_rows, 1 - seq, core), qkv_weight, NT) + got[half:]
        side["e_own"] = mm(part(dqkv_rows, seq, core), qkv_weight, NT) + got[:half]
        side["e_far"] = other_x(sum_far.astype(BF))
        return side["e_own"]

    def input_work(token):
        e_in = side["e_own"] + in_turn(side["e_far"], token).astype(F32)
        input_grad = mid_grad + inverse_a * (
            e_in - unit_own * jnp.mean(e_in * unit_own, axis=-1, keepdims=True)
        )
        side["input"] = head_parts(input_grad.astype(BF))

    def input_place(token):
        own, *rest = side["input"]
        side["input"] = placed((in_turn(own, token), *rest), seq, core).astype(F32)

    def down_finish(token):
        side["down"] = finish_down_call(in_turn(side["down"], token))
        return side["down"]

    def out_finish(token):
        side["out"] = unpair_heads(in_turn(out_sum, token).astype(F32)).T
        return side["out"]

    qkv_sum = ring_scatter(
        [(q_ring[s], kv_ring[s]) for s in range(n)],
        n,
        {0: sum_work, 1: out_finish, 2: input_work, 3: down_finish, 5: input_place},
    )
    qkv_sum = jnp.concatenate(qkv_sum[::-1], axis=1).astype(F32)
    output, input_grad = side["output"], side["input"]
    out_grad, down_grad = side["out"], side["down"]

    feed_sums = gate_sums + up_sums
    attention_sums = jnp.sum(qkv_sum * own_qkv.astype(F32), axis=1, keepdims=True)
    qkv_sum = qkv_sum * gain_a
    kv_grad, query_grad = qkv_sum[:, : 2 * k_width], unpair_heads(qkv_sum[:, 2 * k_width :])
    sums = jnp.concatenate([attention_sums, feed_sums], axis=1).T
    both = lax.ppermute(sums, "head", [(h, h ^ 3) for h in range(4)])
    sums = sums + other_core(sums) + (other_x(sums) + both)

    return (
        output,
        input_grad,
        sums[0],
        query_grad,
        kv_grad[:, :k_width],
        kv_grad[:, k_width:],
        out_grad,
        sums[1],
        gate_grad,
        up_grad,
        down_grad,
    )


def solution(mesh):
    return jax.shard_map(
        functools.partial(local, n=mesh.shape["ctx"]),
        mesh=mesh,
        in_specs=(
            P(None, "ctx", None),
            P(),
            P("ctx"),
            P("ctx", "head"),
            P("ctx", "head"),
            P("ctx", "head"),
            P("head", "ctx"),
            P("ctx"),
            P("ctx", "head"),
            P("ctx", "head"),
            P("head", "ctx"),
            P(None, "ctx", None),
        ),
        out_specs=(
            P(None, "ctx", None),
            P(None, "ctx", None),
            P("ctx"),
            P("ctx", "head"),
            P("ctx", "head"),
            P("ctx", "head"),
            P("head", "ctx"),
            P("ctx"),
            P("ctx", "head"),
            P("ctx", "head"),
            P("head", "ctx"),
        ),
        check_vma=False,
    )
```

```python
import functools
import math

import jax
import jax.numpy as jnp
from jax import lax
from jax.experimental import pallas as pl
from jax.experimental.pallas import tpu as pltpu
from jax.sharding import PartitionSpec as P

HQ = 32
HK = 8
HD = 64
GROUP = HQ // HK
RUN = 128

EPSILON = 1e-05
ROPE_BASE = 500000.0
NEGATIVE = -1e30
LOG2E = math.log2(math.e)
SCALE = HD ** (-0.5)
BF = jnp.bfloat16
F32 = jnp.float32

NN = (((1,), (0,)), ((), ()))
NT = (((1,), (1,)), ((), ()))
TN = (((0,), (0,)), ((), ()))


def mm(a, b, dims=NN):
    return lax.dot_general(a, b, dims, preferred_element_type=F32)


def ring_order(n):
    return list(range(0, n, 2)) + list(range(1, n, 2))[::-1]


def ring_step(value, n):
    order = ring_order(n)
    pairs = []
    for p in range(n):
        for h in range(4):
            step = 1 if h % 2 == 0 else -1
            pairs.append((order[p] * 4 + h, order[(p + step) % n] * 4 + h))
    return lax.ppermute(value, ("ctx", "head"), pairs)


def in_turn(value, other):
    return value if other is None else lax.optimization_barrier((value, other))[0]


class Side:
    def __init__(self, hooks):
        self.hooks, self.due = hooks or {}, None

    def arrived(self, got, last):
        due, self.due = self.due, None
        return in_turn(got, last if due is None else (last, due))

    def after(self, step, token):
        if step in self.hooks:
            self.due = self.hooks[step](token)


def ring_gather(chains, n, hooks=None, pieces=None, due=None):
    chains, side, last = list(chains), Side(hooks), None
    side.due = due
    pieces = [] if pieces is None else pieces
    pieces.append(tuple(chains))
    for step in range(n - 1):
        for j in range(len(chains)):
            got = ring_step(chains[j], n)
            final = j == len(chains) - 1
            last = chains[j] = side.arrived(got, last) if final else in_turn(got, last)
        pieces.append(tuple(chains))
        side.after(step, last)
    return pieces


def ring_scatter(pieces, n, hooks=None, due=None):
    totals, side, last = list(pieces[1 % n]), Side(hooks), None
    side.due = due
    for step, s in enumerate(list(range(2, n)) + [0]):
        for j in range(len(totals)):
            got = ring_step(totals[j], n)
            final = j == len(totals) - 1
            got = side.arrived(got, last) if final else in_turn(got, last)
            last = totals[j] = (got.astype(F32) + pieces[s][j].astype(F32)).astype(BF)
        side.after(step, last)
    return totals


def cut_chains(piece, n):
    count = 2 if n <= 8 else 1
    size = piece.shape[0] // count
    return tuple(piece[j * size : (j + 1) * size] for j in range(count))


def other_core(value):
    return lax.ppermute(value, "head", [(h, h ^ 1) for h in range(4)])


def other_x(value):
    return lax.ppermute(value, "head", [(h, h ^ 2) for h in range(4)])


def part(array, seq, core):
    half = array.shape[1] // 2
    return lax.dynamic_slice(array, (seq, core * half, 0), (1, half, array.shape[2]))[0]


def head_parts(own):
    far = other_x(own)
    near = other_core(jnp.concatenate([own, far], axis=0))
    return own, far, near[: own.shape[0]], near[own.shape[0] :]


def placed(parts, seq, core):
    own, far, near, both = parts
    by_core = lambda a, b: (jnp.where(core == 0, a, b), jnp.where(core == 0, b, a))
    mine, other = by_core(own, near), by_core(far, both)
    first = [jnp.where(seq == 0, a, b) for a, b in zip(mine, other)]
    second = [jnp.where(seq == 0, b, a) for a, b in zip(mine, other)]
    return jnp.stack([jnp.concatenate(first, axis=0), jnp.concatenate(second, axis=0)])


def swap_halves(v):
    lane = lax.broadcasted_iota(jnp.int32, v.shape, 1) % HD
    return jnp.where(lane < HD // 2, pltpu.roll(v, 2 * HD - HD // 2, 1), pltpu.roll(v, HD // 2, 1))


def rotated(v, cos, sin):
    return v * cos + swap_halves(v) * sin


def qkv_kernel(count, index_ref, unit_ref, cos_ref, sin_ref, *refs):
    *pieces, kv_ref, q_ref, w_ref = refs
    lines = pieces[0].shape[0]

    @pl.when(pl.program_id(0) == 0)
    def _():
        for at, piece in enumerate(pieces):
            line = (index_ref[at // count] * count + at % count) * lines
            w_ref[pl.ds(pl.multiple_of(line, lines), lines), :] = piece[...]

    y = mm(unit_ref[0], w_ref[...])
    cos, sin = cos_ref[0], sin_ref[0]
    width = kv_ref.shape[2] // 2
    for j in range(0, width, 2 * HD):
        kv_ref[0, :, j : j + 2 * HD] = rotated(y[:, j : j + 2 * HD], cos, sin).astype(BF)
    kv_ref[0, :, width:] = y[:, width : 2 * width].astype(BF)
    for j in range(0, q_ref.shape[2], 2 * HD):
        at = 2 * width + j
        q_ref[0, :, j : j + 2 * HD] = rotated(y[:, at : at + 2 * HD], cos, sin).astype(BF)


def qkv_call(ring_from, unit, pieces, cos, sin, q_width, kv_width):
    sequences, rows, width = unit.shape
    count = len(pieces[0])
    parts = [part for piece in pieces for part in piece]
    spec = lambda w: pl.BlockSpec((1, rows, w), lambda s: (s, 0, 0))
    whole = lambda shape: pl.BlockSpec(shape, lambda s: (0, 0))
    weight = (width, kv_width + q_width)
    return pl.pallas_call(
        functools.partial(qkv_kernel, count),
        grid=(sequences,),
        in_specs=[
            pl.BlockSpec(memory_space=pltpu.SMEM),
            spec(width),
            spec(2 * HD),
            spec(2 * HD),
        ]
        + [whole(part.shape) for part in parts],
        out_specs=[spec(kv_width), spec(q_width), whole(weight)],
        out_shape=[
            jax.ShapeDtypeStruct((sequences, rows, kv_width), BF),
            jax.ShapeDtypeStruct((sequences, rows, q_width), BF),
            jax.ShapeDtypeStruct(weight, BF),
        ],
        compiler_params=pltpu.CompilerParams(vmem_limit_bytes=60 * 1024 * 1024),
        cost_estimate=pl.CostEstimate(
            flops=2 * sequences * rows * width * weight[1],
            bytes_accessed=weight[0] * weight[1] * 4 + unit.size * 4,
            transcendentals=0,
        ),
        name="qkv",
    )(ring_from, unit, cos, sin, *parts)


def half_mask(v, which):
    lane = lax.broadcasted_iota(jnp.int32, v.shape, 1)
    keep = (lane < HD) if which == 0 else (lane >= HD)
    return jnp.where(keep, v, jnp.zeros_like(v))


def stack_heads(block):
    return jnp.concatenate(
        [block[:, g * 2 * HD : (g + 1) * 2 * HD] for g in range(GROUP)], axis=0
    )


def causal(scores, gap):
    key = lax.broadcasted_iota(jnp.int32, scores.shape, 0)
    query = lax.broadcasted_iota(jnp.int32, scores.shape, 1) % RUN
    return jnp.where(key <= query + gap, scores, NEGATIVE)


def run_pair(kv_ref, slots, at):
    return jnp.concatenate([kv_ref[j, :, at : at + 2 * HD] for j in slots], axis=0)


def load_runs(pieces, kv_ref):
    rows = pieces[0].shape[0]
    for at, piece in enumerate(pieces):
        for r in range(rows // RUN):
            kv_ref[at * rows // RUN + r] = piece[r * RUN : (r + 1) * RUN]


def attend_kernel(n, sq_ref, sk_ref, q_ref, *refs):
    pieces, refs = refs[:n], refs[n:]
    o_ref, low_ref, lse_ref, kv_ref, s_ref, m_ref, l_ref, acc_ref = refs
    seq, run = pl.program_id(0), pl.program_id(1)
    start = sq_ref[seq, run]

    @pl.when(run == 0)
    def _():
        load_runs(pieces, kv_ref)

    runs = kv_ref.shape[0]
    columns = GROUP * RUN
    queries = stack_heads(q_ref[0])
    q_pair = [half_mask(queries, k) for k in range(2)]
    m_ref[...] = jnp.full_like(m_ref, NEGATIVE)
    l_ref[...] = jnp.zeros_like(l_ref)
    acc_ref[...] = jnp.zeros_like(acc_ref)

    def slots_of(i):
        return [sk_ref[seq, 2 * i], sk_ref[seq, 2 * i + 1]]

    def rows_of(i):
        return pl.ds(pl.multiple_of(i * 2 * RUN, 2 * RUN), 2 * RUN)

    def scores(i, masked):
        keys = run_pair(kv_ref, slots_of(i), 0)
        for k in range(2):
            s = mm(keys, q_pair[k], NT) * (SCALE * LOG2E)
            if masked:
                s = causal(s, (start - 2 * i) * RUN)
            s_ref[k, rows_of(i), :] = s
            m_ref[k] = jnp.maximum(m_ref[k], jnp.max(s.reshape(-1, 8, columns), axis=0))

    def score_step(i, carry):
        scores(i, False)
        return carry

    last = start // 2
    lax.fori_loop(0, last, score_step, 0)
    scores(last, True)
    peaks = [jnp.max(m_ref[k], axis=0, keepdims=True) for k in range(2)]

    def value_step(i, carry):
        values = run_pair(kv_ref, slots_of(i), 2 * HD)
        for k in range(2):
            p = jnp.exp2(s_ref[k, rows_of(i), :] - peaks[k])
            l_ref[k] += jnp.sum(p.reshape(-1, 8, columns), axis=0)
            acc_ref[k] += mm(values, p.astype(BF), TN)
        return carry

    lax.fori_loop(0, last + 1, value_step, 0)
    rows = []
    for k in range(2):
        total = jnp.sum(l_ref[k], axis=0, keepdims=True)
        lse_ref[0, 0, k : k + 1, :] = peaks[k] + jnp.log2(total)
        rows.append(acc_ref[k, k * HD : (k + 1) * HD, :] / total)
    both = jnp.concatenate(rows, axis=0)
    for g in range(GROUP):
        out = both[:, g * RUN : (g + 1) * RUN].T
        o_ref[0, :, g * 2 * HD : (g + 1) * 2 * HD] = out
        low_ref[0, :, g * 2 * HD : (g + 1) * 2 * HD] = out.astype(BF)


def attend_call(starts_q, starts_k, query, pieces):
    sequences, rows, width = query.shape
    n, piece_rows, kv_width = len(pieces), pieces[0].shape[0], pieces[0].shape[1] // sequences
    runs = n * piece_rows // RUN
    columns = GROUP * RUN
    smem = pl.BlockSpec(memory_space=pltpu.SMEM)
    row_spec = pl.BlockSpec((1, RUN, width), lambda s, r: (s, r, 0))
    return pl.pallas_call(
        functools.partial(attend_kernel, n),
        grid=(sequences, rows // RUN),
        in_specs=[
            smem,
            smem,
            row_spec,
        ]
        + [pl.BlockSpec((piece_rows, kv_width), lambda s, r: (0, s))] * n,
        out_specs=[row_spec, row_spec, pl.BlockSpec((1, 1, 2, columns), lambda s, r: (s, r, 0, 0))],
        out_shape=[
            jax.ShapeDtypeStruct((sequences, rows, width), F32),
            jax.ShapeDtypeStruct((sequences, rows, width), BF),
            jax.ShapeDtypeStruct((sequences, rows // RUN, 2, columns), F32),
        ],
        scratch_shapes=[
            pltpu.VMEM((runs, RUN, kv_width), BF),
            pltpu.VMEM((2, runs * RUN, columns), F32),
            pltpu.VMEM((2, 8, columns), F32),
            pltpu.VMEM((2, 8, columns), F32),
            pltpu.VMEM((2, 2 * HD, columns), F32),
        ],
        compiler_params=pltpu.CompilerParams(vmem_limit_bytes=56 * 1024 * 1024),
        cost_estimate=pl.CostEstimate(
            flops=50 * sequences * rows * runs * RUN * width,
            bytes_accessed=n * pieces[0].size * 2 + query.size * 6,
            transcendentals=sequences * rows * runs * RUN * 4,
        ),
        name="attend",
    )(starts_q, starts_k, query, *pieces)


def attend_back_kernel(n, sq_ref, sk_ref, q_ref, do_ref, o_ref, lse_ref, cos_ref, sin_ref, *refs):
    pieces, refs = refs[:n], refs[n:]
    dq_ref, dkv_ref, kv_ref, sum_ref, acc_ref = refs
    seq, run = pl.program_id(0), pl.program_id(1)
    start = sq_ref[seq, run]
    runs = kv_ref.shape[0]
    queries = stack_heads(q_ref[0])
    upstream = stack_heads(do_ref[0])
    attended = stack_heads(o_ref[0])
    q_pair = [half_mask(queries, k) for k in range(2)]
    u_pair = [half_mask(upstream, k) for k in range(2)]
    product = upstream.astype(F32) * attended
    deltas = [
        lax.dot_general(
            half_mask(jnp.ones((8, 2 * HD), F32), k),
            product,
            NT,
            precision=lax.Precision.HIGHEST,
            preferred_element_type=F32,
        )[:1]
        for k in range(2)
    ]
    lses = [lse_ref[0, 0, k : k + 1, :] for k in range(2)]
    acc_ref[...] = jnp.zeros_like(acc_ref)

    @pl.when(run == 0)
    def _():
        load_runs(pieces, kv_ref)
        sum_ref[...] = jnp.zeros_like(sum_ref)

    def work(i, masked):
        slots = [sk_ref[seq, 2 * i], sk_ref[seq, 2 * i + 1]]
        keys, values = run_pair(kv_ref, slots, 0), run_pair(kv_ref, slots, 2 * HD)
        dk, dv = 0.0, 0.0
        for k in range(2):
            s = mm(keys, q_pair[k], NT) * (SCALE * LOG2E)
            if masked:
                s = causal(s, (start - 2 * i) * RUN)
            p = jnp.exp2(s - lses[k])
            dp = mm(values, u_pair[k], NT)
            ds = (p * (dp - deltas[k])).astype(BF)
            dk += mm(ds, q_pair[k])
            dv += mm(p.astype(BF), u_pair[k])
            acc_ref[k] += mm(keys, ds, TN)
        for half, j in enumerate(slots):
            sum_ref[j, :, : 2 * HD] += dk[half * RUN : (half + 1) * RUN]
            sum_ref[j, :, 2 * HD :] += dv[half * RUN : (half + 1) * RUN]

    def step(i, carry):
        work(i, False)
        return carry

    lax.fori_loop(0, start // 2, step, 0)
    work(start // 2, True)
    both = jnp.concatenate([acc_ref[k, k * HD : (k + 1) * HD, :] for k in range(2)], axis=0)
    cos, sin = cos_ref[0], sin_ref[0]
    for g in range(GROUP):
        v = both[:, g * RUN : (g + 1) * RUN].T * SCALE
        dq_ref[0, :, g * 2 * HD : (g + 1) * 2 * HD] = (v * cos - swap_halves(v) * sin).astype(BF)

    @pl.when(run == pl.num_programs(1) - 1)
    def _():
        dkv_ref[:, :, : 2 * HD] = (sum_ref[:, :, : 2 * HD] * SCALE).astype(BF)
        dkv_ref[:, :, 2 * HD :] = sum_ref[:, :, 2 * HD :].astype(BF)


def attend_back_call(starts_q, starts_k, query, upstream, attended, lse, pieces, cos, sin):
    sequences, rows, width = query.shape
    n, piece_rows, kv_width = len(pieces), pieces[0].shape[0], pieces[0].shape[1] // sequences
    runs = n * piece_rows // RUN
    columns = GROUP * RUN
    smem = pl.BlockSpec(memory_space=pltpu.SMEM)
    row_spec = pl.BlockSpec((1, RUN, width), lambda s, r: (s, r, 0))
    table_spec = pl.BlockSpec((1, RUN, 2 * HD), lambda s, r: (s, r, 0))
    kv_spec = pl.BlockSpec((runs, RUN, kv_width), lambda s, r: (0, 0, s))
    return pl.pallas_call(
        functools.partial(attend_back_kernel, n),
        grid=(sequences, rows // RUN),
        in_specs=[
            smem,
            smem,
            row_spec,
            row_spec,
            row_spec,
            pl.BlockSpec((1, 1, 2, columns), lambda s, r: (s, r, 0, 0)),
            table_spec,
            table_spec,
        ]
        + [pl.BlockSpec((piece_rows, kv_width), lambda s, r: (0, s))] * n,
        out_specs=[row_spec, kv_spec],
        out_shape=[
            jax.ShapeDtypeStruct((sequences, rows, width), BF),
            jax.ShapeDtypeStruct((runs, RUN, sequences * kv_width), BF),
        ],
        scratch_shapes=[
            pltpu.VMEM((runs, RUN, kv_width), BF),
            pltpu.VMEM((runs, RUN, 4 * HD), F32),
            pltpu.VMEM((2, 2 * HD, columns), F32),
        ],
        compiler_params=pltpu.CompilerParams(vmem_limit_bytes=56 * 1024 * 1024),
        cost_estimate=pl.CostEstimate(
            flops=80 * sequences * rows * runs * RUN * width,
            bytes_accessed=n * pieces[0].size * 4 + query.size * 10,
            transcendentals=sequences * rows * runs * RUN * 4,
        ),
        name="attend_back",
    )(starts_q, starts_k, query, upstream, attended, lse, cos, sin, *pieces)


def ctx_order_kernel(index_ref, *refs):
    *pieces, o_ref = refs
    count = len(pieces) // o_ref.shape[0]
    rows = pieces[0].shape[0]
    for at, piece in enumerate(pieces):
        line = at % count * rows
        o_ref[index_ref[at // count], line : line + rows, :] = piece[...]


def ctx_order_call(ring_from, pieces):
    n, count = len(pieces), len(pieces[0])
    rows, width = pieces[0][0].shape
    return pl.pallas_call(
        ctx_order_kernel,
        grid=(1,),
        in_specs=[pl.BlockSpec(memory_space=pltpu.SMEM)]
        + [pl.BlockSpec((rows, width), lambda i: (0, 0))] * (n * count),
        out_specs=pl.BlockSpec((n, count * rows, width), lambda i: (0, 0, 0)),
        out_shape=jax.ShapeDtypeStruct((n, count * rows, width), BF),
        compiler_params=pltpu.CompilerParams(vmem_limit_bytes=60 * 1024 * 1024),
        name="ctx_order",
    )(ring_from, *[piece for chains in pieces for piece in chains])


def ring_order_kernel(index_ref, x_ref, o_ref):
    for s in range(o_ref.shape[0]):
        o_ref[s] = x_ref[index_ref[s]]


def ring_order_call(ring_from, blocks):
    return pl.pallas_call(
        ring_order_kernel,
        in_specs=[
            pl.BlockSpec(memory_space=pltpu.SMEM),
            pl.BlockSpec(memory_space=pltpu.VMEM),
        ],
        out_specs=pl.BlockSpec(memory_space=pltpu.VMEM),
        out_shape=jax.ShapeDtypeStruct(blocks.shape, blocks.dtype),
        compiler_params=pltpu.CompilerParams(vmem_limit_bytes=12 * 1024 * 1024),
        name="ring_order",
    )(ring_from, blocks)


def gather_rows_kernel(*refs):
    *pieces, o_ref = refs
    rows = pieces[0].shape[0]
    for at, piece in enumerate(pieces):
        o_ref[at * rows : (at + 1) * rows] = piece[...]


def gather_rows_call(pieces):
    rows, width = pieces[0].shape
    shape = (len(pieces) * rows, width)
    return pl.pallas_call(
        gather_rows_kernel,
        grid=(1,),
        in_specs=[pl.BlockSpec((rows, width), lambda i: (0, 0))] * len(pieces),
        out_specs=pl.BlockSpec(shape, lambda i: (0, 0)),
        out_shape=jax.ShapeDtypeStruct(shape, BF),
        compiler_params=pltpu.CompilerParams(vmem_limit_bytes=16 * 1024 * 1024),
        name="gather_rows",
    )(*pieces)


def cut_kernel(chunk, gain_ref, *refs):
    *weights, o_ref = refs
    n = o_ref.shape[-3]
    for j, w_ref in enumerate(weights):
        for t in range(n):
            if w_ref.shape[0] == o_ref.shape[-2]:
                piece = w_ref[:, t * chunk : (t + 1) * chunk].astype(F32) * gain_ref[...]
            else:
                piece = w_ref[t * chunk : (t + 1) * chunk, :].astype(F32).T
            if len(o_ref.shape) == 4:
                o_ref[j, t] = piece.astype(BF)
            else:
                o_ref[t] = piece.astype(BF)


def cut_call(gain, weights, n):
    rows = gain.shape[0]
    chunk = weights[0].shape[1] // n
    shape = (n, rows, chunk) if len(weights) == 1 else (len(weights), n, rows, chunk)
    whole = lambda shape: pl.BlockSpec(shape, lambda i: (0,) * len(shape))
    return pl.pallas_call(
        functools.partial(cut_kernel, chunk),
        grid=(1,),
        in_specs=[whole(gain.shape)] + [whole(w.shape) for w in weights],
        out_specs=whole(shape),
        out_shape=jax.ShapeDtypeStruct(shape, BF),
        compiler_params=pltpu.CompilerParams(vmem_limit_bytes=16 * 1024 * 1024),
        name="cut",
    )(gain, *weights)


def finish_kernel(got_ref, w_ref, gain_ref, grad_ref, sum_ref):
    n, rows, chunk = got_ref.shape
    sums = jnp.zeros((rows, 1), F32)
    for t in range(n):
        grad = got_ref[t].astype(F32)
        grad_ref[:, t * chunk : (t + 1) * chunk] = grad * gain_ref[...]
        weight = w_ref[:, t * chunk : (t + 1) * chunk].astype(F32)
        sums += jnp.sum(grad * weight, axis=1, keepdims=True)
    sum_ref[...] = sums


def finish_call(got, weight, gain):
    n, rows, chunk = got.shape
    vmem = pl.BlockSpec(memory_space=pltpu.VMEM)
    return pl.pallas_call(
        finish_kernel,
        in_specs=[vmem] * 3,
        out_specs=[vmem] * 2,
        out_shape=[
            jax.ShapeDtypeStruct((rows, n * chunk), F32),
            jax.ShapeDtypeStruct((rows, 1), F32),
        ],
        compiler_params=pltpu.CompilerParams(vmem_limit_bytes=16 * 1024 * 1024),
        name="finish",
    )(got, weight, gain)


def finish_down_kernel(got_ref, grad_ref):
    n, rows, chunk = got_ref.shape
    for t in range(n):
        grad_ref[t * chunk : (t + 1) * chunk, :] = got_ref[t].astype(F32).T


def finish_down_call(got):
    n, rows, chunk = got.shape
    vmem = pl.BlockSpec(memory_space=pltpu.VMEM)
    return pl.pallas_call(
        finish_down_kernel,
        in_specs=[vmem],
        out_specs=vmem,
        out_shape=jax.ShapeDtypeStruct((n * chunk, rows), F32),
        compiler_params=pltpu.CompilerParams(vmem_limit_bytes=16 * 1024 * 1024),
        name="finish_down",
    )(got)


def rotation_tables(place_rows):
    half = HD // 2
    frequency = jnp.exp(jnp.arange(half, dtype=F32) * (-2.0 * math.log(ROPE_BASE) / HD))
    angles = place_rows.astype(F32)[..., None] * frequency
    cos, sin = jnp.cos(angles), jnp.sin(angles)
    return (
        jnp.concatenate([cos, cos, cos, cos], axis=-1),
        jnp.concatenate([-sin, sin, -sin, sin], axis=-1),
    )


def pair_heads(w):
    return w.reshape(w.shape[0], 2, GROUP, HD).swapaxes(1, 2).reshape(w.shape[0], -1)


def unpair_heads(w):
    return w.reshape(w.shape[0], GROUP, 2, HD).swapaxes(1, 2).reshape(w.shape[0], -1)


def local(
    hidden,
    positions,
    norm_attention,
    w_query,
    w_key,
    w_value,
    w_out,
    norm_feed,
    w_gate,
    w_up,
    w_down,
    cotangent,
    *,
    n,
):
    sequences, rows, width = hidden.shape
    half = rows // 2
    place, head = lax.axis_index("ctx"), lax.axis_index("head")
    seq, core = head // 2, head % 2
    order = jnp.array(ring_order(n), jnp.int32)
    ring_place = jnp.where(place % 2 == 0, place // 2, n - 1 - place // 2)
    step_sign = 1 - 2 * core
    ring_from = order[(ring_place - step_sign * jnp.arange(n, dtype=jnp.int32)) % n]

    gain_a = norm_attention.astype(F32)[:, None]
    gain_f = norm_feed.astype(F32)[:, None]
    q_width, k_width = w_query.shape[1], w_key.shape[1]
    slice_rows = width // n
    side = {}

    def exchange(cut, axis=0):
        return lax.all_to_all(cut, "ctx", axis, axis, tiled=True)

    def in_halves(array):
        size = array.shape[0] // 2
        return array[:size], array[size:]

    def in_columns(array):
        size = array.shape[1] // 2
        return array[:, :size], array[:, size:]

    def joined(own, near_own, far, token):
        far = jnp.concatenate([in_turn(far[0], token), far[1]], axis=0)
        return jnp.concatenate([own, far, near_own, other_core(far)], axis=1)

    own_qkv = jnp.concatenate([w_key, w_value, pair_heads(w_query)], axis=1)

    def cut_work(token):
        side["gate_cut"] = cut_call(gain_f, [in_turn(w_gate, token)], n)
        return side["gate_cut"]

    def norm_work(token):
        rows_in = in_turn(hidden, token).astype(F32)
        inverse = lax.rsqrt(jnp.mean(rows_in * rows_in, axis=-1, keepdims=True) + EPSILON)
        side["unit_a"] = (rows_in * inverse).astype(BF)
        return side["unit_a"]

    qkv_pieces = ring_gather(
        cut_chains((own_qkv.astype(F32) * gain_a).astype(BF), n),
        n,
        {2: norm_work, 4: cut_work},
    )
    unit_a = side["unit_a"]
    gate_got = exchange(in_turn(side["gate_cut"], qkv_pieces[-1][-1]))

    own_hidden = part(hidden, seq, core).astype(F32)
    own_cotangent = part(cotangent, seq, core)
    own_positions = lax.dynamic_slice_in_dim(positions, place * rows, rows, 1)
    cos, sin = rotation_tables(own_positions)
    starts = positions[:, ::RUN] // RUN
    starts_q = own_positions[:, ::RUN] // RUN
    key_runs = jnp.stack([ring_from * 2, ring_from * 2 + 1], axis=1).reshape(-1)
    starts_k = jnp.take(starts, key_runs, axis=1)
    every = jnp.arange(2 * n, dtype=jnp.int32)
    slots = jnp.sum(
        jnp.where(starts_k[:, None, :] == every[None, :, None], every, 0), axis=2, dtype=jnp.int32
    )
    key_value, query, qkv_weight = qkv_call(
        ring_from, unit_a, qkv_pieces, cos, sin, q_width, 2 * k_width
    )
    gate_own = gate_got.reshape(width, -1)
    gate_near = other_core(gate_own)
    gate_far = [other_x(piece) for piece in in_halves(gate_own)]

    def gate_work(token):
        side["gate_weight"] = joined(gate_own, gate_near, gate_far, token)
        return side["gate_weight"]

    def up_down_work(token):
        side["sent"] = cut_call(gain_f, [in_turn(w_up, token), w_down], n)
        return side["sent"]

    pieces = ring_gather(
        (
            jnp.concatenate([key_value[j] for j in range(sequences)], axis=1),
            pair_heads(w_out.T),
            own_cotangent,
        ),
        n,
        {
            1: lambda token: gate_far[0],
            n - 5: lambda token: gate_far[1],
            n - 4: gate_work,
            n - 3: up_down_work,
        },
        due=gate_got,
    )
    kv = [piece[0] for piece in pieces]
    out_pieces = [piece[1] for piece in pieces]
    cot_pieces = [piece[2] for piece in pieces]
    kv, out_pieces, sent = lax.optimization_barrier((kv, out_pieces, side["sent"]))
    feed_got = exchange(sent, 1)
    attended_full, attended, lse = attend_call(starts_q, slots, query, kv)
    out_pieces[0] = in_turn(out_pieces[0], lse)
    out_weight_t = ctx_order_call(ring_from, [(piece,) for piece in out_pieces])
    out_weight_t = out_weight_t.reshape(width, q_width)

    sent_core = jnp.concatenate(
        [part(attended, seq, 1 - core), part(attended, 1 - seq, 1 - core)], axis=0
    )
    got_core = other_core(mm(sent_core, out_weight_t, NT).astype(BF)).astype(F32)
    sum_far = (mm(part(attended, 1 - seq, core), out_weight_t, NT) + got_core[half:]).astype(BF)
    sum_own = mm(part(attended, seq, core), out_weight_t, NT) + got_core[:half]
    cots = []
    for at in range(2):
        some = cot_pieces[at * n // 2 : (at + 1) * n // 2]
        cots.append(gather_rows_call([in_turn(some[0], sum_far)] + some[1:]))
    got_x, cots = lax.optimization_barrier((other_x(sum_far), cots))
    x1 = own_hidden + sum_own + got_x.astype(F32)
    x1, feed_got = lax.optimization_barrier((x1, feed_got))

    inverse_f = lax.rsqrt(jnp.mean(x1 * x1, axis=-1, keepdims=True) + EPSILON)
    unit_f = x1 * inverse_f
    up_own, down_own = [feed_got[j].reshape(width, -1) for j in range(2)]
    units = 4 * up_own.shape[1]
    arrived, inputs, slabs, partial = [], [], [], []
    owns = (up_own, down_own)
    nears = [other_core(own) for own in owns]
    fars = [[other_x(piece) for piece in in_halves(own)] for own in owns]

    def up_work(token):
        side["up_weight"] = joined(owns[0], nears[0], fars[0], token)
        return side["up_weight"]

    def down_work(token):
        side["down_weight_t"] = joined(owns[1], nears[1], fars[1], token)
        return side["down_weight_t"]

    feeds = []

    def feed_work(token):
        at = len(feeds) * n // 2
        some = [part for piece in arrived[at : at + n // 2] for part in piece]
        feeds.append(gather_rows_call([in_turn(some[0], token)] + some[1:]))
        return feeds[-1]

    def feed_in(at):
        gate = mm(feeds[at], side["gate_weight"])
        up = mm(feeds[at], side["up_weight"])
        if "down_weight_t" not in side:
            down_work(up)
        dact = mm(cots[at], side["down_weight_t"])
        inputs.append((feeds[at], feeds[at], cots[at]))
        return lax.optimization_barrier([value.astype(BF) for value in (gate, up, dact)])

    def feed_middle(gate, up, dact):
        gate, up, dact = [value.astype(F32) for value in (gate, up, dact)]
        sigma = jax.nn.sigmoid(gate)
        silu = gate * sigma
        act = (silu * up).astype(BF)
        dgate = (dact * up * sigma * (1.0 + gate * (1.0 - sigma))).astype(BF)
        dup = (dact * silu).astype(BF)
        return dgate, dup, act

    def feed_out(dgate, dup, act):
        e = (mm(dgate, side["gate_weight"], NT) + mm(dup, side["up_weight"], NT)).astype(BF)
        x = mm(act, side["down_weight_t"], NT).astype(BF)
        return [
            (e[j : j + half], x[j : j + half]) for j in range(0, e.shape[0], half)
        ]

    ring_gather(
        cut_chains(unit_f.astype(BF), n),
        n,
        {
            0: lambda token: fars[0][0],
            n - 6: lambda token: fars[0][1],
            n - 5: lambda token: (up_work(token), fars[1][0]),
            n - 4: feed_work,
            n - 3: lambda token: fars[1][1],
        },
        arrived,
    )
    feed_work(None)
    for at in range(2):
        slabs.append(feed_middle(*feed_in(at)))
        partial.extend(feed_out(*slabs[at]))

    grads, near = [], []

    def grad_work(token):
        j = len(grads)
        first = mm(inputs[0][j], in_turn(slabs[0][j], token), TN).astype(BF)
        first, slab = lax.optimization_barrier((first, slabs[1][j]))
        second = mm(inputs[1][j], slab, TN)
        grads.append((second + first.astype(F32)).astype(BF))
        return grads[-1]

    def near_work(token):
        grad = grads[len(near)]
        kept, sent = grad[:, : units // 2], grad[:, units // 2 :]
        total = in_turn(kept, token).astype(F32) + other_core(sent).astype(F32)
        near.append(total.astype(BF))
        quarter = units // 4
        if len(near) < 3:
            to_x.append((near[-1][:, :quarter], other_x(near[-1][:, quarter:])))
        return near[-1]

    def x_work(token):
        kept, far = to_x[len(sums_x)]
        total = in_turn(kept, token).astype(F32) + far.astype(F32)
        sums_x.append(total.astype(BF).reshape(n, slice_rows, -1))
        return sums_x[-1]

    to_x, sums_x = [], []
    e_own, x_own = ring_scatter(
        partial,
        n,
        {
            0: lambda token: (grad_work(token), near_work(token)),
            1: lambda token: (grad_work(token), near_work(token)),
            2: lambda token: (grad_work(token), to_x[0][1]),
            3: lambda token: (near_work(token), x_work(token)),
            4: lambda token: to_x[1][1],
            5: x_work,
        },
        slabs[1] + partial[-1],
    )
    while len(sums_x) < 2:
        x_work(e_own)
    feed_delivered = exchange(jnp.stack(sums_x), 1)
    e_feed = e_own.astype(F32)
    mid_grad = own_cotangent.astype(F32) + inverse_f * (
        e_feed - unit_f * jnp.mean(e_feed * unit_f, axis=-1, keepdims=True)
    )

    mid_parts = head_parts(mid_grad.astype(BF))
    down_kept, down_sent = near[2][:, : units // 4], near[2][:, units // 4 :]
    down_far = other_x(in_turn(down_sent, mid_parts[1]))
    unit_rows = unit_a.reshape(sequences * rows, width)
    attended_grad = placed([mm(p, out_weight_t).astype(BF) for p in mid_parts], seq, core)
    dquery, dkv = attend_back_call(
        starts_q, slots, query, attended_grad, attended_full, lse, kv, cos, sin
    )
    dquery = dquery.reshape(sequences * rows, -1)
    attended_parts = jnp.concatenate(
        [part(attended, s, c) for c in (core, 1 - core) for s in (seq, 1 - seq)], axis=0
    )
    out_grad_t = mm(jnp.concatenate(mid_parts, axis=0), attended_parts, TN).astype(BF)
    out_grad_t = ring_order_call(ring_from, out_grad_t.reshape(n, slice_rows, q_width))
    dquery, dkv, out_grad_t, feed_delivered, x_own = lax.optimization_barrier(
        (dquery, dkv, out_grad_t, feed_delivered, x_own)
    )
    dkv = dkv.reshape(n, rows, -1)
    x2 = x1 + x_own.astype(F32)

    def down_total(token):
        total = in_turn(down_kept, token).astype(F32) + down_far.astype(F32)
        side["down"] = total.astype(BF).reshape(n, slice_rows, -1)
        return side["down"]

    def down_exchange(token):
        side["down"] = exchange(in_turn(side["down"], token))

    def query_grad_work(token):
        grad = mm(unit_rows, in_turn(dquery, token), TN).astype(BF)
        side["q_ring"] = ring_order_call(ring_from, grad.reshape(n, slice_rows, -1))
        return side["q_ring"]

    def output_work(token):
        side["output"] = head_parts(in_turn(x2, token).astype(BF))
        return side["output"]

    def output_place(token):
        own, *rest = side["output"]
        side["output"] = placed((in_turn(own, token), *rest), seq, core)
        return side["output"]

    def gate_finish(token):
        side["gate"] = finish_call(in_turn(feed_delivered[0], token), w_gate, gain_f)
        return side["gate"]

    def up_finish(token):
        side["up"] = finish_call(in_turn(feed_delivered[1], token), w_up, gain_f)
        return side["up"]

    dkv_own, out_sum = ring_scatter(
        [(dkv[s], out_grad_t[s]) for s in range(n)],
        n,
        {
            0: down_total,
            1: lambda token: (down_exchange(token), output_work(token))[1],
            3: output_place,
            4: lambda token: (gate_finish(token), side["down"]),
            5: lambda token: (up_finish(token), query_grad_work(token)),
        },
    )
    (gate_grad, gate_sums), (up_grad, up_sums) = side["gate"], side["up"]
    pair_width = 2 * k_width
    dkv_own = jnp.stack(
        [dkv_own[:, j * pair_width : (j + 1) * pair_width] for j in range(sequences)]
    ).astype(F32)
    dkey_rot = dkv_own[:, :, :k_width]
    swapped = jnp.concatenate(
        [
            dkey_rot[:, :, HD // 2 : HD],
            dkey_rot[:, :, : HD // 2],
            dkey_rot[:, :, HD + HD // 2 :],
            dkey_rot[:, :, HD : HD + HD // 2],
        ],
        axis=-1,
    )
    dkey = dkey_rot * cos - swapped * sin
    dkv_low = jnp.concatenate(
        [dkey.astype(BF), dkv_own[:, :, k_width:].astype(BF)], axis=2
    ).reshape(sequences * rows, -1)
    dqkv = jnp.concatenate([dkv_low, dquery], axis=1)
    kv_grad = mm(unit_rows, dkv_low, TN).astype(BF).reshape(n, slice_rows, -1)
    q_ring, kv_ring = side["q_ring"], ring_order_call(ring_from, kv_grad)

    dqkv_rows = dqkv.reshape(sequences, rows, -1)
    sent_core = jnp.concatenate(
        [part(dqkv_rows, seq, 1 - core), part(dqkv_rows, 1 - seq, 1 - core)], axis=0
    )
    sent_core = in_turn(sent_core, kv_ring)
    got_core = other_core(mm(sent_core, qkv_weight, NT).astype(BF))
    inverse_a = lax.rsqrt(jnp.mean(own_hidden * own_hidden, axis=-1, keepdims=True) + EPSILON)
    unit_own = own_hidden * inverse_a

    def sum_work(token):
        got = in_turn(got_core, token).astype(F32)
        sum_far = mm(part(dqkv_rows, 1 - seq, core), qkv_weight, NT) + got[half:]
        side["e_own"] = mm(part(dqkv_rows, seq, core), qkv_weight, NT) + got[:half]
        side["e_far"] = other_x(sum_far.astype(BF))
        return side["e_own"]

    def input_work(token):
        e_in = side["e_own"] + in_turn(side["e_far"], token).astype(F32)
        input_grad = mid_grad + inverse_a * (
            e_in - unit_own * jnp.mean(e_in * unit_own, axis=-1, keepdims=True)
        )
        side["input"] = head_parts(input_grad.astype(BF))

    def input_place(token):
        own, *rest = side["input"]
        side["input"] = placed((in_turn(own, token), *rest), seq, core).astype(F32)

    def down_finish(token):
        side["down"] = finish_down_call(in_turn(side["down"], token))
        return side["down"]

    def out_finish(token):
        side["out"] = unpair_heads(in_turn(out_sum, token).astype(F32)).T
        return side["out"]

    qkv_sum = ring_scatter(
        [(q_ring[s], kv_ring[s]) for s in range(n)],
        n,
        {0: sum_work, 1: out_finish, 2: input_work, 3: down_finish, 5: input_place},
    )
    qkv_sum = jnp.concatenate(qkv_sum[::-1], axis=1).astype(F32)
    output, input_grad = side["output"], side["input"]
    out_grad, down_grad = side["out"], side["down"]

    feed_sums = gate_sums + up_sums
    attention_sums = jnp.sum(qkv_sum * own_qkv.astype(F32), axis=1, keepdims=True)
    qkv_sum = qkv_sum * gain_a
    kv_grad, query_grad = qkv_sum[:, : 2 * k_width], unpair_heads(qkv_sum[:, 2 * k_width :])
    sums = jnp.concatenate([attention_sums, feed_sums], axis=1).T
    both = lax.ppermute(sums, "head", [(h, h ^ 3) for h in range(4)])
    sums = sums + other_core(sums) + (other_x(sums) + both)

    return (
        output,
        input_grad,
        sums[0],
        query_grad,
        kv_grad[:, :k_width],
        kv_grad[:, k_width:],
        out_grad,
        sums[1],
        gate_grad,
        up_grad,
        down_grad,
    )


def solution(mesh):
    return jax.shard_map(
        functools.partial(local, n=mesh.shape["ctx"]),
        mesh=mesh,
        in_specs=(
            P(None, "ctx", None),
            P(),
            P("ctx"),
            P("ctx", "head"),
            P("ctx", "head"),
            P("ctx", "head"),
            P("head", "ctx"),
            P("ctx"),
            P("ctx", "head"),
            P("ctx", "head"),
            P("head", "ctx"),
            P(None, "ctx", None),
        ),
        out_specs=(
            P(None, "ctx", None),
            P(None, "ctx", None),
            P("ctx"),
            P("ctx", "head"),
            P("ctx", "head"),
            P("ctx", "head"),
            P("head", "ctx"),
            P("ctx"),
            P("ctx", "head"),
            P("ctx", "head"),
            P("head", "ctx"),
        ),
        check_vma=False,
    )
```
